32 devices in a mesh: seq: 4 (over z), heads: 4 (over y, core), hid: 2 (over x).
Axes of the slice: x: 2, y: 2, z: 4, core: 2. Of those that a mesh axis runs over, the one named last changes fastest.
Arguments:
- tokens_in: bfloat16 [8, 2048, 1024], P(('seq', 'hid'), 'heads'), may hold values from -6 to 6
- first_value: bfloat16 [8, 2048, 1024], P(('seq', 'hid'), None, 'heads')
- cotangent: bfloat16 [8, 2048, 1024], P(('seq', 'hid'), 'heads')
- counts: int32 [8, 4], P(('seq', 'hid')), may hold values from 256 to 512, as said below
- segments: int32 [8, 2048], P(('seq', 'hid')), may hold values from 0 to 2, as said below
- positions: int32 [8, 2048], P(('seq', 'hid')), may hold values from 0 to 2047, as said below
- norm_gains: float32 [2, 1024], replicated
- gain_mean: float32 [2, 1024], replicated
- gain_var: float32 [2, 1024], replicated
- heads_in: float32 [3, 1024, 1024], P(None, ('seq', 'hid'), 'heads')
- heads_in_mean: float32 [3, 1024, 1024], P(None, ('seq', 'hid'), 'heads')
- heads_in_var: float32 [3, 1024, 1024], P(None, ('seq', 'hid'), 'heads')
- heads_out: float32 [1024, 1024], P('heads', ('seq', 'hid'))
- heads_out_mean: float32 [1024, 1024], P('heads', ('seq', 'hid'))
- heads_out_var: float32 [1024, 1024], P('heads', ('seq', 'hid'))
- gate_up: float32 [2, 1024, 2816], P(None, ('seq', 'heads'), 'hid')
- gate_up_mean: float32 [2, 1024, 2816], P(None, ('seq', 'heads'), 'hid')
- gate_up_var: float32 [2, 1024, 2816], P(None, ('seq', 'heads'), 'hid')
- down_proj: float32 [2816, 1024], P('hid', ('seq', 'heads'))
- down_mean: float32 [2816, 1024], P('hid', ('seq', 'heads'))
- down_var: float32 [2816, 1024], P('hid', ('seq', 'heads'))
Outputs:
- block_out: bfloat16 [8, 2048, 1024], P(('seq', 'hid'), 'heads')
- input_grad: float32 [8, 2048, 1024], P(('seq', 'hid'), 'heads')
- first_grad: float32 [8, 2048, 1024], P(('seq', 'hid'), None, 'heads')
- gains_new: float32 [2, 1024], replicated
- gain_mean_new: float32 [2, 1024], replicated
- gain_var_new: float32 [2, 1024], replicated
- heads_in_new: float32 [3, 1024, 1024], P(None, ('seq', 'hid'), 'heads')
- heads_in_mean_new: float32 [3, 1024, 1024], P(None, ('seq', 'hid'), 'heads')
- heads_in_var_new: float32 [3, 1024, 1024], P(None, ('seq', 'hid'), 'heads')
- heads_out_new: float32 [1024, 1024], P('heads', ('seq', 'hid'))
- heads_out_mean_new: float32 [1024, 1024], P('heads', ('seq', 'hid'))
- heads_out_var_new: float32 [1024, 1024], P('heads', ('seq', 'hid'))
- gate_up_new: float32 [2, 1024, 2816], P(None, ('seq', 'heads'), 'hid')
- gate_up_mean_new: float32 [2, 1024, 2816], P(None, ('seq', 'heads'), 'hid')
- gate_up_var_new: float32 [2, 1024, 2816], P(None, ('seq', 'heads'), 'hid')
- down_new: float32 [2816, 1024], P('hid', ('seq', 'heads'))
- down_mean_new: float32 [2816, 1024], P('hid', ('seq', 'heads'))
- down_var_new: float32 [2816, 1024], P('hid', ('seq', 'heads'))
- norms: float32 [14], replicated
- value_norms: float32 [2], replicated
The draws below stay inside these ranges and needn't reach their ends.
Inputs may be any that keep to these rules, and one draw needn't show every extreme that they name: `counts`: in each group one shard holds exactly 512 used positions and another exactly 256. `segments`: never falling within a group. Sequence 1 starts within the used positions of the group's first shard and ends within those of its last; sequences 0 and 2 lie in the first and the last shard. `positions`: within a sequence, rising by one from position to position. In each group sequence 0 starts at 0 and sequence 1 ends at 2047.
All inputs are finite; a program needn't handle non-finite values.
Results may differ from the reference program's by a relative error of at most 0.034.
The reference program's roundings to bfloat16 on the way count: a program that leaves them out, or rounds other values in their place, can miss the bound.
Values may be sent and summed in bfloat16 or wider, within the bound.
No kernel may reach another device: no remote copies, remote signals or barrier semaphores. Data moves between devices by JAX's collectives and lax.ppermute only.
A program may use at most 320 MiB of HBM per device.

```python
import math
import jax
import jax.numpy as jnp
from jax import lax

D = 1024
HEADS = 16
HDIM = 64
FF = 2816
GROUP_LEN = 2048
STEP = 10
SLICES = 4
SHARDS = 4
PACKS = 2
GROUPS = 8
TOK_DEV = 512
TOKENS = 16384


def axis_ramp(ordinal, extent, ramp_span):
    return ramp_span ** (ordinal.astype(jnp.float32) / max(extent - 1, 1) - 0.5)


def spread_profile(slice_ordinal, shard_ordinal, pack_ordinal, ramp_span):
    return axis_ramp(slice_ordinal, SLICES, ramp_span) * axis_ramp(shard_ordinal, SHARDS, ramp_span) * axis_ramp(pack_ordinal, PACKS, ramp_span)


def layout_dims(which):
    if which == 0:
        return (3, D, D)
    if which == 1:
        return (D, D)
    if which == 2:
        return (2, D, FF)
    if which == 3:
        return (FF, D)
    return (2, D)


def layout_profile(which, ramp_span):
    array_dims = layout_dims(which)
    if which == 4:
        return jnp.ones(array_dims, jnp.float32)
    last_axis = len(array_dims) - 1
    row_ids = lax.broadcasted_iota(jnp.int32, array_dims, last_axis - 1)
    col_ids = lax.broadcasted_iota(jnp.int32, array_dims, last_axis)
    if which == 0:
        row_block = row_ids // (D // GROUPS)
        return spread_profile(row_block // PACKS, col_ids // (D // SHARDS), row_block % PACKS, ramp_span)
    if which == 1:
        col_block = col_ids // (D // GROUPS)
        return spread_profile(col_block // PACKS, row_ids // (D // SHARDS), col_block % PACKS, ramp_span)
    if which == 2:
        row_block = row_ids // (D // (SLICES * SHARDS))
        return spread_profile(row_block // SHARDS, row_block % SHARDS, col_ids // (FF // PACKS), ramp_span)
    col_block = col_ids // (D // (SLICES * SHARDS))
    return spread_profile(col_block // SHARDS, col_block % SHARDS, row_ids // (FF // PACKS), ramp_span)


def fan_scale(which):
    return [D ** (-0.5), 4.0 * D ** (-0.5), D ** (-0.5), FF ** (-0.5)][which]


def grad_size(which):
    root_tokens = math.sqrt(TOKENS)
    if which == 0:
        return jnp.array([1.0, 1.0, 3.0], jnp.float32)[:, None, None] * root_tokens
    if which == 4:
        return jnp.array([3.0, 1.3], jnp.float32)[:, None] * root_tokens
    return [0.0, 0.4, 0.5, 0.6][which] * root_tokens


def second_moment(key, which):
    factors = jnp.exp(jax.random.uniform(key, layout_dims(which), jnp.float32, math.log(0.5), math.log(8.0)))
    return factors * 0.001001 * grad_size(which) ** 2


def group_bounds(key):
    first_key, second_key, third_key = jax.random.split(key, 3)
    edge = max(2, TOK_DEV // 2)
    low_cut = jax.random.randint(first_key, (GROUPS, 1), 1, edge)
    high_cut = GROUP_LEN - TOK_DEV + jax.random.randint(second_key, (GROUPS, 1), 1, edge)
    last_offset = jax.random.randint(third_key, (GROUPS, 1), 0, GROUP_LEN - TOK_DEV)
    middle_offset = GROUP_LEN - 1 - (high_cut - 1 - low_cut)
    row_ids = lax.broadcasted_iota(jnp.int32, (GROUPS, GROUP_LEN), 1)
    segment_ids = (row_ids >= low_cut).astype(jnp.int32) + (row_ids >= high_cut).astype(jnp.int32)
    starts = jnp.where(segment_ids == 0, 0, jnp.where(segment_ids == 1, low_cut, high_cut))
    chosen = jnp.where(segment_ids == 0, 0, jnp.where(segment_ids == 1, middle_offset, last_offset))
    return (segment_ids, (chosen + row_ids - starts).astype(jnp.int32))


def draw_segments(key, part):
    shared = group_bounds(key)
    return shared[0]


def draw_positions(key, part):
    shared = group_bounds(key)
    return shared[1]


def draw_counts(key, part):
    key = jax.random.fold_in(key, 3)
    base_key, high_key, low_key = jax.random.split(key, 3)
    base = jax.random.randint(base_key, (GROUPS, SHARDS), TOK_DEV // 2, TOK_DEV + 1)
    high_pick = jax.random.randint(high_key, (GROUPS, 1), 0, SHARDS)
    low_pick = (high_pick + 1 + jax.random.randint(low_key, (GROUPS, 1), 0, SHARDS - 1)) % SHARDS
    col_ids = lax.broadcasted_iota(jnp.int32, (GROUPS, SHARDS), 1)
    filled = jnp.where(col_ids == high_pick, TOK_DEV, base)
    return jnp.where(col_ids == low_pick, TOK_DEV // 2, filled).astype(jnp.int32)


def draw_first_value(key, part):
    key = jax.random.fold_in(key, 5)
    array_dims = (GROUPS, GROUP_LEN, D)
    noise_field = jax.random.normal(key, array_dims, jnp.float32)
    ramp_span = 1.7320508
    group_ids = lax.broadcasted_iota(jnp.int32, array_dims, 0)
    col_ids = lax.broadcasted_iota(jnp.int32, array_dims, 2)
    return (noise_field * spread_profile(group_ids // PACKS, col_ids // (D // SHARDS), group_ids % PACKS, ramp_span)).astype(jnp.bfloat16)


def draw_cotangent(key, part):
    key = jax.random.fold_in(key, 7)
    array_dims = (GROUPS, GROUP_LEN, D)
    noise_field = jax.random.normal(key, array_dims, jnp.float32)
    ramp_span = 1.7320508
    group_ids = lax.broadcasted_iota(jnp.int32, array_dims, 0)
    row_ids = lax.broadcasted_iota(jnp.int32, array_dims, 1)
    return (noise_field * spread_profile(group_ids // PACKS, row_ids // TOK_DEV, group_ids % PACKS, ramp_span)).astype(jnp.bfloat16)


def draw_norm_gains(key, part):
    key = jax.random.fold_in(key, 9)
    array_dims = (2, D)
    noise_field = jax.random.normal(key, array_dims, jnp.float32)
    col_ids = lax.broadcasted_iota(jnp.int32, array_dims, 1).astype(jnp.float32)
    return (0.6 + 0.8 * col_ids / (D - 1)) * (1.0 + 0.1 * noise_field)


def draw_gain_mean(key, part):
    key = jax.random.fold_in(key, 11)
    noise_field = jax.random.normal(key, (2, D), jnp.float32)
    return noise_field * 0.111 * grad_size(4)


def draw_gain_var(key, part):
    key = jax.random.fold_in(key, 13)
    return second_moment(key, 4)


def draw_heads_in(key, part):
    key = jax.random.fold_in(key, 21)
    noise_field = jax.random.normal(key, layout_dims(0), jnp.float32)
    ramp_span = 1.7320508
    return noise_field * layout_profile(0, ramp_span) * fan_scale(0)


def draw_heads_in_mean(key, part):
    key = jax.random.fold_in(key, 22)
    noise_field = jax.random.normal(key, layout_dims(0), jnp.float32)
    ramp_span = 1.7320508
    return noise_field * layout_profile(0, ramp_span) * 0.111 * grad_size(0)


def draw_heads_in_var(key, part):
    key = jax.random.fold_in(key, 23)
    return second_moment(key, 0)


def draw_heads_out(key, part):
    key = jax.random.fold_in(key, 31)
    noise_field = jax.random.normal(key, layout_dims(1), jnp.float32)
    ramp_span = 1.7320508
    return noise_field * layout_profile(1, ramp_span) * fan_scale(1)


def draw_heads_out_mean(key, part):
    key = jax.random.fold_in(key, 32)
    noise_field = jax.random.normal(key, layout_dims(1), jnp.float32)
    ramp_span = 1.7320508
    return noise_field * layout_profile(1, ramp_span) * 0.111 * grad_size(1)


def draw_heads_out_var(key, part):
    key = jax.random.fold_in(key, 33)
    return second_moment(key, 1)


def draw_gate_up(key, part):
    key = jax.random.fold_in(key, 41)
    noise_field = jax.random.normal(key, layout_dims(2), jnp.float32)
    ramp_span = 1.7320508
    return noise_field * layout_profile(2, ramp_span) * fan_scale(2)


def draw_gate_up_mean(key, part):
    key = jax.random.fold_in(key, 42)
    noise_field = jax.random.normal(key, layout_dims(2), jnp.float32)
    ramp_span = 1.7320508
    return noise_field * layout_profile(2, ramp_span) * 0.111 * grad_size(2)


def draw_gate_up_var(key, part):
    key = jax.random.fold_in(key, 43)
    return second_moment(key, 2)


def draw_down_proj(key, part):
    key = jax.random.fold_in(key, 51)
    noise_field = jax.random.normal(key, layout_dims(3), jnp.float32)
    ramp_span = 1.7320508
    return noise_field * layout_profile(3, ramp_span) * fan_scale(3)


def draw_down_mean(key, part):
    key = jax.random.fold_in(key, 52)
    noise_field = jax.random.normal(key, layout_dims(3), jnp.float32)
    ramp_span = 1.7320508
    return noise_field * layout_profile(3, ramp_span) * 0.111 * grad_size(3)


def draw_down_var(key, part):
    key = jax.random.fold_in(key, 53)
    return second_moment(key, 3)


def block_scale(stream_key, shape, cuts, smallest, largest):
    factor_of = 1.0
    for axis_at, blocks in cuts:
        steps = jax.random.uniform(jax.random.fold_in(jax.random.fold_in(stream_key, 6), axis_at), (blocks,), jnp.float32, smallest / len(cuts), largest / len(cuts))
        factor_of = factor_of * jnp.repeat(jnp.exp(steps), shape[axis_at] // blocks).reshape((-1,) + (1,) * (len(shape) - 1 - axis_at))
    return factor_of


def centred(rng, shape, scale, limit, shards=(), kind=jnp.bfloat16):
    drawn = scale * jax.random.normal(rng, shape, jnp.float32)
    if shards:
        drawn = drawn * block_scale(rng, shape, shards, -0.22, 0.18)
    return jnp.clip(drawn, -limit, limit).astype(kind)


def setup_inputs(seed: int = 0) -> dict:
    key_of = jax.random.split(jax.random.key(seed), 22)
    return {
        "tokens_in": centred(key_of[0], (GROUPS, GROUP_LEN, D), 1.0, 6.0, ((0, 8), (1, 4))),
        "first_value": draw_first_value(jax.random.fold_in(key_of[21], 71), 0),
        "cotangent": draw_cotangent(jax.random.fold_in(key_of[21], 71), 0),
        "counts": draw_counts(jax.random.fold_in(key_of[21], 71), 0),
        "segments": draw_segments(jax.random.fold_in(key_of[21], 71), 0),
        "positions": draw_positions(jax.random.fold_in(key_of[21], 71), 0),
        "norm_gains": draw_norm_gains(jax.random.fold_in(key_of[21], 71), 0),
        "gain_mean": draw_gain_mean(jax.random.fold_in(key_of[21], 71), 0),
        "gain_var": draw_gain_var(jax.random.fold_in(key_of[21], 71), 0),
        "heads_in": draw_heads_in(jax.random.fold_in(key_of[21], 71), 0),
        "heads_in_mean": draw_heads_in_mean(jax.random.fold_in(key_of[21], 71), 0),
        "heads_in_var": draw_heads_in_var(jax.random.fold_in(key_of[21], 71), 0),
        "heads_out": draw_heads_out(jax.random.fold_in(key_of[21], 71), 0),
        "heads_out_mean": draw_heads_out_mean(jax.random.fold_in(key_of[21], 71), 0),
        "heads_out_var": draw_heads_out_var(jax.random.fold_in(key_of[21], 71), 0),
        "gate_up": draw_gate_up(jax.random.fold_in(key_of[21], 71), 0),
        "gate_up_mean": draw_gate_up_mean(jax.random.fold_in(key_of[21], 71), 0),
        "gate_up_var": draw_gate_up_var(jax.random.fold_in(key_of[21], 71), 0),
        "down_proj": draw_down_proj(jax.random.fold_in(key_of[21], 71), 0),
        "down_mean": draw_down_mean(jax.random.fold_in(key_of[21], 71), 0),
        "down_var": draw_down_var(jax.random.fold_in(key_of[21], 71), 0),
    }


@jax.custom_vjp
def low(v):
    return lax.optimization_barrier(v.astype(jnp.bfloat16)).astype(jnp.float32)

@jax.custom_vjp
def low_back(v):
    return v

def low_keep(v):
    return (low(v), None)

def low_pass(kept, grad):
    return (grad,)

def back_keep(v):
    return (v, None)

def back_low(kept, grad):
    return (low(grad),)
low.defvjp(low_keep, low_pass)
low_back.defvjp(back_keep, back_low)
HIGHEST = lax.Precision.HIGHEST
NORM_EPS = 1e-05
ROPE_BASE = 10000.0
BLEND = 0.5
BETA_ONE = 0.9
BETA_TWO = 0.999
ADAM_EPS = 1e-06
DECAY = 0.01
MATRIX_RATE = 0.25
GAIN_RATE = 0.7
NEG_LARGE = -1e+30

def rope_tables(position_ids):
    half_dim = HDIM // 2
    freqs = ROPE_BASE ** (-(jnp.arange(half_dim, dtype=jnp.float32) * 2.0 / HDIM))
    angles = position_ids.astype(jnp.float32)[:, None] * freqs[None, :]
    return (jnp.cos(angles), jnp.sin(angles))

def rotate(vectors, cosine, sine_table):
    half_dim = HDIM // 2
    first_half = vectors[..., :half_dim]
    second_half = vectors[..., half_dim:]
    cos_wide = cosine[:, None, :]
    sin_wide = sine_table[:, None, :]
    return jnp.concatenate([first_half * cos_wide - second_half * sin_wide, second_half * cos_wide + first_half * sin_wide], axis=-1)

def attend(queries, keys_rot, values, segment_ids, is_valid):
    block_rows = min(512, GROUP_LEN)
    key_ids = jnp.arange(GROUP_LEN, dtype=jnp.int32)

    def one_block(row_begin):
        query_ids = row_begin + jnp.arange(block_rows, dtype=jnp.int32)
        query_block = lax.dynamic_slice_in_dim(queries, row_begin, block_rows, 0)
        query_segs = lax.dynamic_slice_in_dim(segment_ids, row_begin, block_rows, 0)
        scores = low_back(jnp.einsum('qhd,khd->hqk', query_block, keys_rot, precision=HIGHEST))
        allowed = (query_segs[:, None] == segment_ids[None, :]) & (key_ids[None, :] <= query_ids[:, None]) & is_valid[None, :] | (key_ids[None, :] == query_ids[:, None])
        scores = jnp.where(allowed[None], scores, NEG_LARGE)
        row_max = lax.optimization_barrier(jnp.max(scores, axis=-1, keepdims=True))
        exp_scores = jnp.exp(scores - row_max)
        attn_probs = exp_scores / lax.optimization_barrier(jnp.sum(exp_scores, axis=-1, keepdims=True))
        mixed = jnp.einsum('hqk,khd->qhd', low(attn_probs), values, precision=HIGHEST)
        return low(low_back(mixed))
    starts = jnp.arange(GROUP_LEN // block_rows, dtype=jnp.int32) * block_rows
    outputs = lax.map(jax.checkpoint(one_block), starts)
    return outputs.reshape(GROUP_LEN, HEADS * HDIM)

def group_forward(weights, group_inputs):
    gains_all, in_low, out_low, gu_low, down_low = weights
    rows_in, first_rows, segment_ids, position_ids, shard_counts = group_inputs
    row_ids = jnp.arange(GROUP_LEN, dtype=jnp.int32)
    is_valid = row_ids % TOK_DEV < jnp.repeat(shard_counts, TOK_DEV, total_repeat_length=GROUP_LEN)
    inv_one = lax.rsqrt(lax.optimization_barrier(jnp.mean(rows_in * rows_in, axis=-1, keepdims=True)) + NORM_EPS)
    normed_one = low(rows_in * inv_one * gains_all[0])
    projected = low_back(jnp.einsum('ld,kdc->klc', normed_one, in_low, precision=HIGHEST))
    cosine, sine_table = rope_tables(position_ids)
    shaped = projected.reshape(3, GROUP_LEN, HEADS, HDIM)
    queries = low(rotate(shaped[0], cosine, sine_table) * HDIM ** (-0.5))
    keys_rot = low(rotate(shaped[1], cosine, sine_table))
    blended = low(BLEND * projected[2] + (1.0 - BLEND) * first_rows)
    mixed = attend(queries, keys_rot, blended.reshape(GROUP_LEN, HEADS, HDIM), segment_ids, is_valid)
    hidden = rows_in + low_back(jnp.dot(mixed, out_low, precision=HIGHEST))
    inv_two = lax.rsqrt(lax.optimization_barrier(jnp.mean(hidden * hidden, axis=-1, keepdims=True)) + NORM_EPS)
    normed_two = low(hidden * inv_two * gains_all[1])
    gate_vals = low_back(jnp.einsum('ld,kdf->klf', normed_two, gu_low, precision=HIGHEST))
    activation = low(jax.nn.silu(gate_vals[0]) * gate_vals[1])
    return (hidden + low_back(jnp.dot(activation, down_low, precision=HIGHEST)), blended)

def adam_moments(mean_old, var_old, grad):
    mean_new = BETA_ONE * mean_old + (1.0 - BETA_ONE) * grad
    var_new = BETA_TWO * var_old + (1.0 - BETA_TWO) * grad * grad
    direction = mean_new / (1.0 - BETA_ONE ** STEP) / (jnp.sqrt(var_new / (1.0 - BETA_TWO ** STEP)) + ADAM_EPS)
    return (mean_new, var_new, direction)

def lamb_matrix(weight, mean_old, var_old, grad, axes):
    mean_new, var_new, direction = adam_moments(mean_old, var_old, grad)
    update = direction + DECAY * weight
    weight_sq = lax.optimization_barrier(jnp.sum(weight * weight, axis=axes, keepdims=True))
    update_sq = lax.optimization_barrier(jnp.sum(update * update, axis=axes, keepdims=True))
    ratio = jnp.sqrt(weight_sq) / jnp.sqrt(update_sq + 1e-12)
    return (weight - MATRIX_RATE * ratio * update, mean_new, var_new, weight_sq.reshape(-1), update_sq.reshape(-1))

def reference(tokens_in, first_value, cotangent, counts, segments, positions, norm_gains, gain_mean, gain_var, heads_in, heads_in_mean, heads_in_var, heads_out, heads_out_mean, heads_out_var, gate_up, gate_up_mean, gate_up_var, down_proj, down_mean, down_var):
    tokens_wide = tokens_in.astype(jnp.float32)
    first_wide = first_value.astype(jnp.float32)
    grad_seed = cotangent.astype(jnp.float32)

    def forward(tokens_all, first_all, gains_all, in_w, out_w, gu_w, down_w):
        weights = (gains_all, low(in_w), low(out_w), low(gu_w), low(down_w))

        def scan_step(carry_in, group_inputs):
            return (carry_in, group_forward(weights, group_inputs))
        carry_out, results = lax.scan(jax.checkpoint(scan_step), jnp.zeros((), jnp.float32), (tokens_all, first_all, segments, positions, counts))
        return (results[0], results[1])
    block_wide, pullback, blended_all = jax.vjp(forward, tokens_wide, first_wide, norm_gains, heads_in, heads_out, gate_up, down_proj, has_aux=True)
    grad_tokens, grad_first, grad_gains, grad_in, grad_out, grad_gu, grad_down = pullback(grad_seed)
    in_new, in_mean, in_var, in_wsq, in_usq = lamb_matrix(heads_in, heads_in_mean, heads_in_var, grad_in, (1, 2))
    out_new, out_mean, out_var, out_wsq, out_usq = lamb_matrix(heads_out, heads_out_mean, heads_out_var, grad_out, (0, 1))
    gu_new, gu_mean, gu_var, gu_wsq, gu_usq = lamb_matrix(gate_up, gate_up_mean, gate_up_var, grad_gu, (1, 2))
    down_new, dn_mean, dn_var, down_wsq, down_usq = lamb_matrix(down_proj, down_mean, down_var, grad_down, (0, 1))
    gmean_new, gvar_new, gain_dir = adam_moments(gain_mean, gain_var, grad_gains)
    gains_new = norm_gains - GAIN_RATE * gain_dir
    weight_norms = jnp.sqrt(jnp.concatenate([in_wsq, out_wsq, gu_wsq, down_wsq]))
    update_norms = jnp.sqrt(jnp.concatenate([in_usq, out_usq, gu_usq, down_usq]))
    value_norms = jnp.stack([jnp.sqrt(jnp.mean(first_wide * first_wide)), jnp.sqrt(jnp.mean(blended_all * blended_all))])
    norms = jnp.concatenate([weight_norms, update_norms])
    return (block_wide.astype(jnp.bfloat16), grad_tokens, grad_first, gains_new, gmean_new, gvar_new, in_new, in_mean, in_var, out_new, out_mean, out_var, gu_new, gu_mean, gu_var, down_new, dn_mean, dn_var, norms, value_norms)
```

```python
import functools

import jax
import jax.numpy as jnp
from jax import lax
from jax.experimental import pallas as pl
from jax.experimental.pallas import tpu as pltpu
from jax.sharding import PartitionSpec as P

HDIM = 64
STEP = 10


NORM_EPS = 1e-05
ROPE_BASE = 10000.0
BLEND = 0.5
BETA_ONE = 0.9
BETA_TWO = 0.999
ADAM_EPS = 1e-06
DECAY = 0.01
MATRIX_RATE = 0.25
GAIN_RATE = 0.7
NEG_LARGE = -1e30

BLOCK = 512
EXTRA = 16
SEGMENTS = 3
NN = ((1,), (0,))
NT = ((1,), (1,))
TN = ((0,), (0,))
F32 = jnp.float32
LOW = jnp.bfloat16


def dot(left, right, dims):
    return lax.dot_general(left, right, (dims, ((), ())), preferred_element_type=F32)


def tile_plan(length, block):
    tiles = []
    half = block // 2
    for begin in range(0, length, block):
        tiles.append((begin, half, begin, half, True))
        tiles.append((begin + half, half, begin, block, True))
        for key_begin in range(0, begin, block):
            tiles.append((begin, block, key_begin, block, False))
    return tiles


def diagonal_mask(scores, query_segs, key_segs, query_begin, key_begin):
    rows = lax.broadcasted_iota(jnp.int32, scores.shape, 0) + key_begin
    cols = lax.broadcasted_iota(jnp.int32, scores.shape, 1) + query_begin
    allowed = ((key_segs == query_segs) & (rows <= cols)) | (rows == cols)
    return jnp.where(allowed, scores, NEG_LARGE)


def segment_rows(query_segs, key_segs):
    shape = (EXTRA, query_segs.shape[1])
    row_ids = lax.broadcasted_iota(jnp.int32, shape, 0)
    query_rows = jnp.where(row_ids == query_segs, 1.0, 0.0)
    key_rows = jnp.where((row_ids < SEGMENTS) & (row_ids != key_segs), NEG_LARGE, 0.0)
    return (row_ids, query_rows, key_rows)


def attend_kernel(
    block, q_ref, k_ref, v_ref, qseg_ref, kseg_ref, ksegrow_ref, out_ref, lse_ref, q_ext, k_ext, v_ext
):
    length = q_ref.shape[1]
    row_ids, query_rows, key_rows = segment_rows(qseg_ref[...], ksegrow_ref[...])
    q_ext[0:HDIM, :] = q_ref[...]
    k_ext[0:HDIM, :] = k_ref[...]
    v_ext[0:HDIM, :] = v_ref[...]
    q_ext[HDIM:, :] = query_rows.astype(LOW)
    k_ext[HDIM:, :] = key_rows.astype(LOW)
    v_ext[HDIM:, :] = jnp.where(row_ids == 0, 1.0, 0.0).astype(LOW)
    tiles = tile_plan(length, block)

    def score(tile):
        q0, qn, k0, kn, diagonal = tile
        if diagonal:
            return dot(k_ref[:, k0 : k0 + kn], q_ref[:, q0 : q0 + qn], TN)
        return dot(k_ext[:, k0 : k0 + kn], q_ext[:, q0 : q0 + qn], TN)

    ahead = score(tiles[0])
    halves = []
    state = None
    for index, (q0, qn, k0, kn, diagonal) in enumerate(tiles):
        scores = ahead
        if index + 1 < len(tiles):
            ahead = score(tiles[index + 1])
        if diagonal:
            scores = diagonal_mask(
                scores, qseg_ref[:, q0 : q0 + qn], kseg_ref[k0 : k0 + kn, :], q0, k0
            )
        new_max = jnp.max(scores, axis=0, keepdims=True)
        if not diagonal:
            new_max = jnp.maximum(state[0], new_max)
        probs = jnp.exp(scores - new_max).astype(LOW)
        mixed = dot(v_ext[:, k0 : k0 + kn], probs, NN)
        if diagonal:
            halves.append((new_max, mixed))
            if len(halves) == 2:
                state = tuple(jnp.concatenate(pair, axis=1) for pair in zip(*halves))
                halves = []
        else:
            state = (new_max, state[1] * jnp.exp(state[0] - new_max) + mixed)
        if index + 1 == len(tiles) or (tiles[index + 1][4] and not halves):
            total = state[1][HDIM : HDIM + 1, :]
            begin = (q0 // block) * block
            out_ref[:, begin : begin + block] = (state[1][0:HDIM, :] / total).astype(LOW)
            lse_ref[0, :, begin : begin + block] = state[0] + jnp.log(total)


def head_specs(length):
    return (
        pl.BlockSpec((HDIM, length), lambda head: (head, 0)),
        pl.BlockSpec((1, length), lambda head: (0, 0)),
        pl.BlockSpec((length, 1), lambda head: (0, 0)),
        pl.BlockSpec((1, 1, length), lambda head: (head, 0, 0)),
    )


def attention_forward(queries, keys_rot, values, query_segs, key_segs):
    cols, length = queries.shape
    heads = cols // HDIM
    wide, row, column, per_head = head_specs(length)
    return pl.pallas_call(
        functools.partial(attend_kernel, min(BLOCK, length)),
        grid=(heads,),
        in_specs=[wide, wide, wide, row, column, row],
        out_specs=[wide, per_head],
        out_shape=[
            jax.ShapeDtypeStruct((cols, length), LOW),
            jax.ShapeDtypeStruct((heads, 1, length), F32),
        ],
        scratch_shapes=[pltpu.VMEM((HDIM + EXTRA, length), LOW)] * 3,
        compiler_params=pltpu.CompilerParams(vmem_limit_bytes=40 << 20),
        cost_estimate=pl.CostEstimate(
            flops=8 * cols * length * length,
            bytes_accessed=8 * cols * length,
            transcendentals=heads * length * length,
        ),
    )(queries, keys_rot, values, query_segs, key_segs.reshape(length, 1), key_segs)


def three_terms(value):
    high = value.astype(LOW).astype(F32)
    middle = (value - high).astype(LOW).astype(F32)
    return (high, middle, value - high - middle)


def attend_back_kernel(
    block,
    q_ref,
    k_ref,
    v_ref,
    grad_ref,
    out_ref,
    lse_ref,
    qseg_ref,
    kseg_ref,
    ksegrow_ref,
    dq_ref,
    dk_ref,
    dv_ref,
    q_ext,
    k_ext,
    v_ext,
    g_ext,
):
    length = q_ref.shape[1]
    half = block // 2
    row_ids, query_rows, key_rows = segment_rows(qseg_ref[...], ksegrow_ref[...])
    delta = jnp.sum(grad_ref[...].astype(F32) * out_ref[...].astype(F32), axis=0, keepdims=True)
    for row, term in enumerate(three_terms(-lse_ref[0])):
        query_rows = jnp.where(row_ids == SEGMENTS + row, term, query_rows)
    key_rows = jnp.where((row_ids >= SEGMENTS) & (row_ids < SEGMENTS + 3), 1.0, key_rows)
    grad_rows = jnp.zeros_like(query_rows)
    for row, term in enumerate(three_terms(-delta)):
        grad_rows = jnp.where(row_ids == row, term, grad_rows)
    q_ext[0:HDIM, :] = q_ref[...]
    k_ext[0:HDIM, :] = k_ref[...]
    v_ext[0:HDIM, :] = v_ref[...]
    g_ext[0:HDIM, :] = grad_ref[...]
    q_ext[HDIM:, :] = query_rows.astype(LOW)
    k_ext[HDIM:, :] = key_rows.astype(LOW)
    v_ext[HDIM:, :] = jnp.where(row_ids < 3, 1.0, 0.0).astype(LOW)
    g_ext[HDIM:, :] = grad_rows.astype(LOW)
    tiles = tile_plan(length, block)

    def score(tile):
        q0, qn, k0, kn, diagonal = tile
        rows, cols = slice(k0, k0 + kn), slice(q0, q0 + qn)
        if diagonal:
            scores = dot(k_ref[:, rows], q_ref[:, cols], TN)
        else:
            scores = dot(k_ext[:, rows], q_ext[:, cols], TN)
        return (scores, dot(v_ext[:, rows], g_ext[:, cols], TN))

    ahead = score(tiles[0])
    for index, (q0, qn, k0, kn, diagonal) in enumerate(tiles):
        scores, grad_probs = ahead
        if index + 1 < len(tiles):
            ahead = score(tiles[index + 1])
        rows, cols = slice(k0, k0 + kn), slice(q0, q0 + qn)
        if diagonal:
            scores = diagonal_mask(scores, qseg_ref[:, cols], kseg_ref[rows, :], q0, k0)
            scores = scores - lse_ref[0, :, cols]
        probs = jnp.exp(scores)
        grad_scores = (probs * grad_probs).astype(LOW)
        dv = dot(grad_ref[:, cols], probs.astype(LOW), NT)
        dk = dot(q_ref[:, cols], grad_scores, NT)
        dq = dot(k_ref[:, rows], grad_scores, NN)
        if not diagonal:
            dq_ref[:, cols] += dq
            dk_ref[:, rows] += dk
            dv_ref[:, rows] += dv
            continue
        dq_ref[:, cols] = dq
        if kn == half:
            dk_ref[:, rows] = dk
            dv_ref[:, rows] = dv
        else:
            low_rows, high_rows = slice(k0, k0 + half), slice(k0 + half, k0 + block)
            dk_ref[:, low_rows] += dk[:, :half]
            dv_ref[:, low_rows] += dv[:, :half]
            dk_ref[:, high_rows] = dk[:, half:]
            dv_ref[:, high_rows] = dv[:, half:]


def attention_backward(queries, keys_rot, values, grad_mixed, mixed, lse, query_segs, key_segs):
    cols, length = queries.shape
    heads = cols // HDIM
    wide, row, column, per_head = head_specs(length)
    return pl.pallas_call(
        functools.partial(attend_back_kernel, min(BLOCK, length)),
        grid=(heads,),
        in_specs=[wide] * 5 + [per_head, row, column, row],
        out_specs=[wide] * 3,
        out_shape=[jax.ShapeDtypeStruct((cols, length), F32)] * 3,
        scratch_shapes=[pltpu.VMEM((HDIM + EXTRA, length), LOW)] * 4,
        compiler_params=pltpu.CompilerParams(vmem_limit_bytes=40 << 20),
        cost_estimate=pl.CostEstimate(
            flops=20 * cols * length * length,
            bytes_accessed=22 * cols * length,
            transcendentals=heads * length * length,
        ),
    )(
        queries,
        keys_rot,
        values,
        grad_mixed,
        mixed,
        lse,
        query_segs,
        key_segs.reshape(length, 1),
        key_segs,
    )


def swap(value, axis, mask):
    return lax.ppermute(value, axis, [(i, i ^ mask) for i in range(lax.axis_size(axis))])


def ring(value, axis):
    size = lax.axis_size(axis)
    return lax.ppermute(value, axis, [(i, (i + 1) % size) for i in range(size)])


def masks_from_high(size):
    bit = size // 2
    while bit:
        yield bit
        bit //= 2


def gather_masks(value, axis, bits):
    held = {0: value}
    for bit in bits:
        held.update({mask ^ bit: swap(block, axis, bit) for mask, block in list(held.items())})
    return held


def total(value, axis):
    size = lax.axis_size(axis)
    bit = 1
    while bit < size:
        if bit * 4 <= size:
            one, two, three = (swap(value, axis, mask * bit) for mask in (1, 2, 3))
            value = (value + one) + (two + three)
            bit *= 4
        else:
            value = value + swap(value, axis, bit)
            bit *= 2
    return value


def after(value, other):
    return lax.optimization_barrier((value, other))[0]


def take(value, index, size, axis):
    return lax.dynamic_slice_in_dim(value, index * size, size, axis)


def put(buffer, value, index, axis):
    return lax.dynamic_update_slice_in_dim(buffer, value, index * value.shape[axis], axis)


def ring_scatter(block_of, axis):
    size = lax.axis_size(axis)
    me = lax.axis_index(axis)
    value = block_of(lax.rem(me + size - 1, size))
    for step in range(1, size):
        moved = ring(value.astype(LOW), axis)
        value = moved.astype(F32) + block_of(lax.rem(me + 2 * size - 1 - step, size))
    return value


def norm_backward(inputs, inverse, gain, grad_normed):
    scaled = gain * grad_normed
    inner_mean = jnp.mean(scaled * inputs, axis=-1, keepdims=True)
    grad_inputs = inverse * scaled - inputs * inverse**3 * inner_mean
    grad_gain = jnp.sum(grad_normed * inputs * inverse, axis=0)
    return (grad_inputs, grad_gain)


def adam_moments(mean_old, var_old, grad):
    mean_new = BETA_ONE * mean_old + (1.0 - BETA_ONE) * grad
    var_new = BETA_TWO * var_old + (1.0 - BETA_TWO) * grad * grad
    direction = (
        mean_new / (1.0 - BETA_ONE**STEP) / (jnp.sqrt(var_new / (1.0 - BETA_TWO**STEP)) + ADAM_EPS)
    )
    return (mean_new, var_new, direction)


def matrix_step(weight, mean_old, var_old, grad, axes):
    mean_new, var_new, direction = adam_moments(mean_old, var_old, grad)
    update = direction + DECAY * weight
    weight_sq = jnp.sum(weight * weight, axis=axes, keepdims=True)
    update_sq = jnp.sum(update * update, axis=axes, keepdims=True)
    return (mean_new, var_new, update, weight_sq, update_sq)


def rope_tables(position_ids):
    half_dim = HDIM // 2
    freqs = ROPE_BASE ** (-(jnp.arange(half_dim, dtype=jnp.float32) * 2.0 / HDIM))
    angles = freqs[:, None] * position_ids.astype(jnp.float32)[None, :]
    return (jnp.cos(angles), jnp.sin(angles))


def rotate(vectors, cosine, sine_table, direction_sign):
    cols, length = vectors.shape
    halves = vectors.reshape(cols // HDIM, 2, HDIM // 2, length)
    first_half, second_half = halves[:, 0], halves[:, 1]
    sine = direction_sign * sine_table
    return jnp.stack(
        [
            first_half * cosine - second_half * sine,
            second_half * cosine + first_half * sine,
        ],
        axis=1,
    ).reshape(cols, length)


def per_device(
    tokens_in,
    first_value,
    cotangent,
    counts,
    segments,
    positions,
    norm_gains,
    gain_mean,
    gain_var,
    heads_in,
    heads_in_mean,
    heads_in_var,
    heads_out,
    heads_out_mean,
    heads_out_var,
    gate_up,
    gate_up_mean,
    gate_up_var,
    down_proj,
    down_mean,
    down_var,
):
    n_seq, n_heads, n_hid = (lax.axis_size(name) for name in ("seq", "heads", "hid"))
    at_seq, at_heads, at_hid = (lax.axis_index(name) for name in ("seq", "heads", "hid"))
    own_rows = tokens_in[0].astype(F32)
    tok_rows, model_width = own_rows.shape
    length = tok_rows * n_heads
    head_cols = heads_in.shape[2]
    hidden_cols = gate_up.shape[2]
    query_scale = HDIM ** (-0.5)
    far_bits = [bit for bit in masks_from_high(n_heads) if bit > 1]
    near = 1

    inv_one = lax.rsqrt(jnp.mean(own_rows * own_rows, axis=-1, keepdims=True) + NORM_EPS)
    normed_one = (own_rows * inv_one * norm_gains[0]).astype(LOW)
    row_blocks = gather_masks(normed_one, "heads", far_bits)
    far_rows = row_blocks[n_heads // 2]
    row_blocks.update(
        {mask ^ near: swap(block, "heads", near) for mask, block in list(row_blocks.items())}
    )
    group_rows = jnp.zeros((length, model_width), LOW)
    for mask, block in row_blocks.items():
        group_rows = put(group_rows, block, at_heads ^ mask, 0)

    in_low = jnp.swapaxes(heads_in, 1, 2).astype(LOW)
    out_low = heads_out.astype(LOW)
    out_parts = gather_masks(out_low, "heads", far_bits)
    out_masks = list(out_parts)
    piece = jnp.concatenate([in_low] + [out_parts[mask][None] for mask in out_masks], axis=0)
    head_weights = jnp.zeros((piece.shape[0], head_cols, model_width), LOW)
    for step in range(n_seq):
        if step:
            piece = ring(piece, "seq")
        from_seq = lax.rem(at_seq + n_seq - step, n_seq)
        for mask, block in gather_masks(piece, "hid", masks_from_high(n_hid)).items():
            head_weights = put(head_weights, block, from_seq * n_hid + (at_hid ^ mask), 2)
    last_piece = piece
    in_w = head_weights[:3].reshape(3 * head_cols, model_width)
    out_here = head_weights[3:]
    out_near = swap(out_here, "heads", near)
    out_w = jnp.zeros((n_heads * head_cols, model_width), LOW)
    for slot, mask in enumerate(out_masks):
        out_w = put(out_w, out_here[slot], at_heads ^ mask, 0)
        out_w = put(out_w, out_near[slot], at_heads ^ mask ^ near, 0)

    ffn_piece = jnp.concatenate(
        [gate_up.astype(LOW), jnp.swapaxes(down_proj, 0, 1).astype(LOW)[None]], axis=0
    )
    ffn_piece = after(ffn_piece, last_piece)
    ffn_w = jnp.zeros((3, model_width, hidden_cols), LOW)
    for step in range(n_seq):
        if step:
            ffn_piece = ring(ffn_piece, "seq")
        from_seq = lax.rem(at_seq + n_seq - step, n_seq)
        blocks = gather_masks(after(ffn_piece, far_rows), "heads", masks_from_high(n_heads))
        for mask, block in blocks.items():
            ffn_w = put(ffn_w, block, from_seq * n_heads + (at_heads ^ mask), 1)

    projected = dot(in_w, group_rows, NT).reshape(3, head_cols, length)
    cosine, sine_table = rope_tables(positions[0])
    queries = (rotate(projected[0], cosine, sine_table, 1.0) * query_scale).astype(LOW)
    keys_rot = rotate(projected[1], cosine, sine_table, 1.0).astype(LOW)
    first_local = first_value[0].T.astype(F32)
    values = (BLEND * projected[2] + (1.0 - BLEND) * first_local).astype(LOW)
    row_ids = jnp.arange(length, dtype=jnp.int32)
    is_valid = row_ids % tok_rows < jnp.repeat(counts[0], tok_rows, total_repeat_length=length)
    query_segs = segments
    key_segs = jnp.where(is_valid[None], segments, -1)
    mixed, lse = attention_forward(queries, keys_rot, values, query_segs, key_segs)

    mixed_own = jnp.zeros((n_heads * head_cols, tok_rows), LOW)
    mixed_own = put(mixed_own, take(mixed, at_heads, tok_rows, 1), at_heads, 0)
    for mask in range(n_heads - 1, 0, -1):
        block = swap(take(mixed, at_heads ^ mask, tok_rows, 1), "heads", mask)
        mixed_own = put(mixed_own, block, at_heads ^ mask, 0)
    hidden = own_rows + dot(mixed_own, out_w, TN)
    inv_two = lax.rsqrt(jnp.mean(hidden * hidden, axis=-1, keepdims=True) + NORM_EPS)
    normed_two = (hidden * inv_two * norm_gains[1]).astype(LOW)

    back_other = swap(after(cotangent[0], last_piece), "hid", 1)
    ffn_in = jnp.concatenate([normed_two, swap(normed_two, "hid", 1)], axis=0)
    ffn_back = jnp.concatenate([cotangent[0], back_other], axis=0)
    gate_vals = dot(ffn_in, ffn_w[0], NN)
    up_vals = dot(ffn_in, ffn_w[1], NN)
    grad_act = dot(ffn_back, ffn_w[2], NN)
    gate_sigmoid = jax.nn.sigmoid(gate_vals)
    gate_silu = gate_vals * gate_sigmoid
    activation = (gate_silu * up_vals).astype(LOW)
    grad_gate = (
        grad_act * up_vals * gate_sigmoid * (1.0 + gate_vals * (1.0 - gate_sigmoid))
    ).astype(LOW)
    grad_up = (grad_act * gate_silu).astype(LOW)
    grad_normed_two = (dot(grad_gate, ffn_w[0], NT) + dot(grad_up, ffn_w[1], NT)).astype(LOW)
    grad_two_other = swap(grad_normed_two[tok_rows:], "hid", 1)
    ffn_part = dot(activation, ffn_w[2], NT).astype(LOW)
    ffn_other = swap(after(ffn_part[tok_rows:], grad_two_other), "hid", 1)
    grad_two = grad_normed_two[:tok_rows].astype(F32) + grad_two_other.astype(F32)
    block_out = (
        (hidden + (ffn_part[:tok_rows].astype(F32) + ffn_other.astype(F32))).astype(LOW)[None]
    )
    grad_norm_two, gain_grad_two = norm_backward(hidden, inv_two, norm_gains[1], grad_two)
    grad_hidden = cotangent[0].astype(F32) + grad_norm_two
    grad_hidden_low = grad_hidden.astype(LOW)

    grad_mixed_own = dot(out_w, grad_hidden_low, NT).astype(LOW)
    grad_mixed = jnp.zeros((head_cols, length), LOW)
    grad_mixed = put(grad_mixed, take(grad_mixed_own, at_heads, head_cols, 0), at_heads, 1)
    for mask in range(n_heads - 1, 0, -1):
        block = swap(take(grad_mixed_own, at_heads ^ mask, head_cols, 0), "heads", mask)
        grad_mixed = put(grad_mixed, block, at_heads ^ mask, 1)

    ffn_grads = []
    for left, right in ((ffn_in, grad_gate), (ffn_in, grad_up), (ffn_back, activation)):
        part = dot(after(left, grad_two_other), right, TN).astype(LOW)
        part = part.reshape(n_seq, n_heads, -1, hidden_cols)
        size = n_heads
        bit = 1
        part = part.reshape(n_seq, n_heads, -1, hidden_cols)
        while size > 1:
            pairs = part.reshape(n_seq, size // 2, 2, -1, hidden_cols)
            side = lax.rem(at_heads // bit, 2)
            mine = lax.dynamic_index_in_dim(pairs, side, 2, False)
            other = lax.dynamic_index_in_dim(pairs, 1 - side, 2, False)
            moved = swap(other, "heads", bit)
            part = (mine.astype(F32) + moved.astype(F32)).astype(LOW)
            size //= 2
            bit *= 2
        part = part.reshape(n_seq, -1, hidden_cols)
        ffn_grads.append(
            ring_scatter(
                lambda at, part=part: lax.dynamic_index_in_dim(part, at, 0, False).astype(F32), "seq"
            )
        )
    gu_grad = jnp.stack(ffn_grads[:2])
    down_grad = ffn_grads[2].T

    def to_owner(grad):
        cols = model_width // (n_seq * n_hid)
        lead = grad.shape[:-1]
        parts = grad.reshape(*lead, n_seq, n_hid, cols)
        axis = len(lead) + 1
        mine = lax.dynamic_index_in_dim(parts, at_hid, axis, False)
        if n_hid > 1:
            other = lax.dynamic_index_in_dim(parts, at_hid ^ 1, axis, False)
            mine = (mine.astype(F32) + swap(other, "hid", 1).astype(F32)).astype(LOW)
        return ring_scatter(
            lambda at: lax.dynamic_index_in_dim(mine, at, axis - 1, False).astype(F32), "seq"
        )

    out_part = dot(mixed_own, grad_hidden_low, NN).astype(LOW)
    size, bit = n_heads, 1
    while size > 1:
        pairs = out_part.reshape(size // 2, 2, head_cols, model_width)
        side = lax.rem(at_heads // bit, 2)
        mine = lax.dynamic_index_in_dim(pairs, side, 1, False)
        other = lax.dynamic_index_in_dim(pairs, 1 - side, 1, False)
        out_part = (mine.astype(F32) + swap(other, "heads", bit).astype(F32)).astype(LOW)
        size //= 2
        bit *= 2
    out_grad = to_owner(out_part.reshape(head_cols, model_width))

    grad_queries, grad_keys, grad_values = attention_backward(
        queries, keys_rot, values, grad_mixed, mixed, lse, query_segs, key_segs
    )
    first_grad = ((1.0 - BLEND) * grad_values).T[None]
    grad_projected = jnp.concatenate(
        [
            rotate(grad_queries * query_scale, cosine, sine_table, -1.0).astype(LOW),
            rotate(grad_keys, cosine, sine_table, -1.0).astype(LOW),
            (BLEND * grad_values).astype(LOW),
        ],
        axis=0,
    )

    def partial_of(mask):
        return dot(take(grad_projected, at_heads ^ mask, tok_rows, 1), in_w, TN)

    sums = {}
    for mask in range(n_heads - 1, 0, -2):
        moved = swap(partial_of(mask).astype(LOW), "heads", near)
        sums[mask ^ near] = partial_of(mask ^ near) + moved.astype(F32)
    for bit in far_bits:
        for mask in sorted(sums, reverse=True):
            if mask & bit:
                moved = swap(sums.pop(mask).astype(LOW), "heads", bit)
                sums[mask ^ bit] = sums[mask ^ bit] + moved.astype(F32)
    grad_one = sums[0]
    in_part = dot(grad_projected, group_rows, NN).astype(LOW)
    in_grad = jnp.swapaxes(to_owner(in_part.reshape(3, head_cols, model_width)), 1, 2)
    grad_norm_one, gain_grad_one = norm_backward(own_rows, inv_one, norm_gains[0], grad_one)
    input_grad = (grad_hidden + grad_norm_one)[None]

    in_mean, in_var, in_update, in_wsq, in_usq = matrix_step(
        heads_in, heads_in_mean, heads_in_var, in_grad, (1, 2)
    )
    out_mean, out_var, out_update, out_wsq, out_usq = matrix_step(
        heads_out, heads_out_mean, heads_out_var, out_grad, (0, 1)
    )
    gu_mean, gu_var, gu_update, gu_wsq, gu_usq = matrix_step(
        gate_up, gate_up_mean, gate_up_var, gu_grad, (1, 2)
    )
    dn_mean, dn_var, dn_update, dn_wsq, dn_usq = matrix_step(
        down_proj, down_mean, down_var, down_grad, (0, 1)
    )
    weight_local = jnp.concatenate(
        [in_wsq.reshape(-1), out_wsq.reshape(-1), gu_wsq.reshape(-1), dn_wsq.reshape(-1)]
    )
    update_local = jnp.concatenate(
        [in_usq.reshape(-1), out_usq.reshape(-1), gu_usq.reshape(-1), dn_usq.reshape(-1)]
    )
    blended_wide = values.astype(jnp.float32)
    value_local = jnp.stack(
        [jnp.sum(first_local * first_local), jnp.sum(blended_wide * blended_wide)]
    )
    packed = jnp.concatenate([gain_grad_one, gain_grad_two, weight_local, update_local, value_local])
    packed = jnp.pad(packed, (0, -packed.shape[0] % 128)).reshape(-1, 128)
    for axis in ("heads", "seq", "hid"):
        packed = total(packed, axis)
    packed = packed.reshape(-1)
    gain_grads = packed[: 2 * model_width].reshape(2, model_width)
    weight_tot, update_tot, value_tot = (
        packed[2 * model_width + begin : 2 * model_width + finish]
        for begin, finish in ((0, 7), (7, 14), (14, 16))
    )
    ratios = jnp.sqrt(weight_tot) / jnp.sqrt(update_tot + 1e-12)
    in_new = heads_in - MATRIX_RATE * ratios[0:3].reshape(3, 1, 1) * in_update
    out_new = heads_out - MATRIX_RATE * ratios[3] * out_update
    gu_new = gate_up - MATRIX_RATE * ratios[4:6].reshape(2, 1, 1) * gu_update
    dn_new = down_proj - MATRIX_RATE * ratios[6] * dn_update
    gmean_new, gvar_new, gain_dir = adam_moments(gain_mean, gain_var, gain_grads)
    gains_new = norm_gains - GAIN_RATE * gain_dir
    entries = float(
        length * head_cols * lax.axis_size("seq") * lax.axis_size("heads") * lax.axis_size("hid")
    )
    norms = jnp.concatenate([jnp.sqrt(weight_tot), jnp.sqrt(update_tot)])
    value_norms = jnp.sqrt(value_tot / entries)
    return (
        block_out,
        input_grad,
        first_grad,
        gains_new,
        gmean_new,
        gvar_new,
        in_new,
        in_mean,
        in_var,
        out_new,
        out_mean,
        out_var,
        gu_new,
        gu_mean,
        gu_var,
        dn_new,
        dn_mean,
        dn_var,
        norms,
        value_norms,
    )


def solution(mesh):
    placed = (
        P(("seq", "hid"), "heads", None),
        P(("seq", "hid"), None, "heads"),
        P(("seq", "hid"), "heads", None),
        P(("seq", "hid"), None),
        P(("seq", "hid"), None),
        P(("seq", "hid"), None),
        P(),
        P(),
        P(),
        P(None, ("seq", "hid"), "heads"),
        P(None, ("seq", "hid"), "heads"),
        P(None, ("seq", "hid"), "heads"),
        P("heads", ("seq", "hid")),
        P("heads", ("seq", "hid")),
        P("heads", ("seq", "hid")),
        P(None, ("seq", "heads"), "hid"),
        P(None, ("seq", "heads"), "hid"),
        P(None, ("seq", "heads"), "hid"),
        P("hid", ("seq", "heads")),
        P("hid", ("seq", "heads")),
        P("hid", ("seq", "heads")),
    )
    return jax.shard_map(
        per_device,
        mesh=mesh,
        in_specs=placed,
        out_specs=(
            P(("seq", "hid"), "heads", None),
            P(("seq", "hid"), "heads", None),
            P(("seq", "hid"), None, "heads"),
            P(),
            P(),
            P(),
            P(None, ("seq", "hid"), "heads"),
            P(None, ("seq", "hid"), "heads"),
            P(None, ("seq", "hid"), "heads"),
            P("heads", ("seq", "hid")),
            P("heads", ("seq", "hid")),
            P("heads", ("seq", "hid")),
            P(None, ("seq", "heads"), "hid"),
            P(None, ("seq", "heads"), "hid"),
            P(None, ("seq", "heads"), "hid"),
            P("hid", ("seq", "heads")),
            P("hid", ("seq", "heads")),
            P("hid", ("seq", "heads")),
            P(),
            P(),
        ),
        check_vma=False,
    )
```

```python
import functools

import jax
import jax.numpy as jnp
from jax import lax
from jax.experimental import pallas as pl
from jax.experimental.layout import Layout, with_layout_constraint
from jax.experimental.pallas import tpu as pltpu
from jax.sharding import PartitionSpec as P

HDIM = 64
STEP = 10


NORM_EPS = 1e-05
ROPE_BASE = 10000.0
BLEND = 0.5
BETA_ONE = 0.9
BETA_TWO = 0.999
ADAM_EPS = 1e-06
DECAY = 0.01
MATRIX_RATE = 0.25
GAIN_RATE = 0.7
NEG_LARGE = -1e30

BLOCK = 512
GROUP_HEADS = 2
EXTRA = 16
SEGMENTS = 3
MATRICES = 7
ROW = 1024
NN = ((1,), (0,))
NT = ((1,), (1,))
TN = ((0,), (0,))
VMEM_LIMIT = 62 << 20
F32 = jnp.float32
LOW = jnp.bfloat16


def dot(left, right, dims):
    return lax.dot_general(left, right, (dims, ((), ())), preferred_element_type=F32)


def ordered_call(deps, kernel, *, in_specs, **rest):
    extra = jax.tree.leaves(deps)
    count = len(in_specs)

    def body(*refs):
        kernel(*refs[:count], *refs[count + len(extra) :])

    in_specs = in_specs + [pl.BlockSpec(memory_space=pl.ANY)] * len(extra)
    call = pl.pallas_call(body, in_specs=in_specs, **rest)
    return lambda *operands: call(*operands, *extra)


def tile_plan(length, block):
    tiles = []
    half = block // 2
    for begin in range(0, length, block):
        tiles.append((begin, half, begin, half, True))
        tiles.append((begin + half, half, begin, block, True))
        for key_begin in range(0, begin, block):
            tiles.append((begin, block, key_begin, block, False))
    return tiles


def causal(scores, own_scores, query_begin, key_begin):
    rows = lax.broadcasted_iota(jnp.int32, scores.shape, 0) + (key_begin - query_begin)
    cols = lax.broadcasted_iota(jnp.int32, scores.shape, 1)
    return jnp.where(rows < cols, scores, jnp.where(rows == cols, own_scores, NEG_LARGE))


def segment_rows(query_segs, key_segs):
    shape = (EXTRA, query_segs.shape[1])
    row_ids = lax.broadcasted_iota(jnp.int32, shape, 0)
    query_rows = jnp.where(row_ids == query_segs, 1.0, 0.0)
    key_rows = jnp.where((row_ids < SEGMENTS) & (row_ids != key_segs), NEG_LARGE, 0.0)
    return (row_ids, query_rows, key_rows)


def move_all(moves, sems):
    copies = [
        pltpu.make_async_copy(source, target, sems.at[index])
        for index, (source, target) in enumerate(moves)
    ]
    for copy in copies:
        copy.start()
    for copy in copies:
        copy.wait()


def turn(rows, cosine, sine, sign):
    parts = []
    for begin in range(0, rows.shape[0], HDIM):
        middle = begin + HDIM // 2
        first, second = rows[begin:middle], rows[middle : begin + HDIM]
        parts.append(first * cosine - sign * (second * sine))
        parts.append(second * cosine + sign * (first * sine))
    return jnp.concatenate(parts, axis=0)


def project_kernel(n_heads, n_seq, where_ref, *refs):
    row_refs, refs = refs[:n_heads], refs[n_heads:]
    upper_ref, moved_ref, lower_ref, first_ref, cos_ref, sin_ref = refs[:6]
    rows_ref, turned, q_ref, k_ref, v_ref, w_ref, sems = refs[6:]
    half = upper_ref.shape[1]
    upper, lower = pl.ds(0, half), pl.ds(half, half)
    cols = q_ref.shape[0]
    tok_rows, width = row_refs[0].shape
    moves = [(row_refs[at], rows_ref.at[where_ref[at]]) for at in range(n_heads)]
    own, other = where_ref[n_heads + n_seq], where_ref[n_heads + n_seq + 1]
    for at in range(n_seq):
        slot = where_ref[n_heads + at]
        moves.append((upper_ref.at[at], w_ref.at[slot, own, upper]))
        moves.append((moved_ref.at[at], w_ref.at[slot, other, upper]))
        moves.append((lower_ref.at[at, 0], w_ref.at[slot, own, lower]))
        moves.append((lower_ref.at[at, 1], w_ref.at[slot, other, lower]))
    move_all(moves, sems)
    turned[...] = w_ref[...].reshape(width, 3 * cols).T
    for at in range(n_heads):
        here = slice(at * tok_rows, (at + 1) * tok_rows)
        projected = dot(turned[...], rows_ref[at], NT)
        cosine, sine = cos_ref[:, here], sin_ref[:, here]
        q_ref[:, here] = (turn(projected[:cols], cosine, sine, 1.0) * HDIM ** (-0.5)).astype(LOW)
        k_ref[:, here] = turn(projected[cols : 2 * cols], cosine, sine, 1.0).astype(LOW)
        first = first_ref[here, :].astype(F32).T
        v_ref[:, here] = (BLEND * projected[2 * cols :] + (1.0 - BLEND) * first).astype(LOW)


def project(where, row_blocks, upper, upper_moved, lower, first_local, cosine, sine, deps=()):
    n_heads, n_seq = len(row_blocks), upper.shape[0]
    tok_rows, width = row_blocks[0].shape
    length, cols = first_local.shape
    anywhere = pl.BlockSpec(memory_space=pl.ANY)
    vmem = pl.BlockSpec(memory_space=pltpu.VMEM)
    count = n_heads + 4 * n_seq
    head_rows = jax.ShapeDtypeStruct((cols, length), LOW)
    return ordered_call(
        deps,
        functools.partial(project_kernel, n_heads, n_seq),
        in_specs=[pl.BlockSpec(memory_space=pltpu.SMEM)]
        + [anywhere] * (n_heads + 3)
        + [vmem] * 3,
        out_specs=[vmem] * 5,
        out_shape=[
            jax.ShapeDtypeStruct((n_heads, tok_rows, width), LOW),
            jax.ShapeDtypeStruct((3 * cols, width), LOW),
            head_rows,
            head_rows,
            head_rows,
        ],
        scratch_shapes=[
            pltpu.VMEM((n_seq, 2, 2 * upper.shape[1], upper.shape[2]), LOW),
            pltpu.SemaphoreType.DMA((count,)),
        ],
        compiler_params=pltpu.CompilerParams(vmem_limit_bytes=VMEM_LIMIT),
    )(where, *row_blocks, upper, upper_moved, lower, first_local, cosine, sine)


def attend_kernel(block, n_heads, where_ref, *refs):
    q_ref, k_ref, v_ref, qseg_ref, ksegrow_ref, out_ref, lse_ref = refs[:7]
    send_refs, (q_ext, k_ext, v_ext) = refs[7 : 7 + n_heads], refs[7 + n_heads :]
    length = q_ref.shape[1]
    size = length // n_heads
    row_ids, query_rows, key_rows = segment_rows(qseg_ref[...], ksegrow_ref[...])
    q_ext[0:HDIM, :] = q_ref[...]
    k_ext[0:HDIM, :] = k_ref[...]
    v_ext[0:HDIM, :] = v_ref[...]
    q_ext[HDIM:, :] = query_rows.astype(LOW)
    k_ext[HDIM:, :] = key_rows.astype(LOW)
    v_ext[HDIM:, :] = jnp.where(row_ids == 0, 1.0, 0.0).astype(LOW)
    own_scores = jnp.sum(q_ref[...].astype(F32) * k_ref[...].astype(F32), axis=0, keepdims=True)
    tiles = tile_plan(length, block)

    def score(tile):
        q0, qn, k0, kn, _ = tile
        return dot(k_ext[:, k0 : k0 + kn], q_ext[:, q0 : q0 + qn], TN)

    ahead = score(tiles[0])
    halves = []
    state = None
    for index, (q0, qn, k0, kn, diagonal) in enumerate(tiles):
        scores = ahead
        if index + 1 < len(tiles):
            ahead = score(tiles[index + 1])
        if diagonal:
            scores = causal(scores, own_scores[:, q0 : q0 + qn], q0, k0)
        new_max = jnp.max(scores, axis=0, keepdims=True)
        if not diagonal:
            new_max = jnp.maximum(state[0], new_max)
        probs = jnp.exp(scores - new_max).astype(LOW)
        mixed = dot(v_ext[:, k0 : k0 + kn], probs, NN)
        if diagonal:
            halves.append((new_max, mixed))
            if len(halves) == 2:
                state = tuple(jnp.concatenate(pair, axis=1) for pair in zip(*halves))
                halves = []
        else:
            state = (new_max, state[1] * jnp.exp(state[0] - new_max) + mixed)
        if index + 1 == len(tiles) or (tiles[index + 1][4] and not halves):
            total_row = state[1][HDIM : HDIM + 1, :]
            begin = (q0 // block) * block
            out_ref[:, begin : begin + block] = (state[1][0:HDIM, :] / total_row).astype(LOW)
            lse_ref[0, :, begin : begin + block] = state[0] + jnp.log(total_row)
    for at in range(n_heads):
        for mask in range(n_heads):

            @pl.when(where_ref[at] == mask)
            def _(at=at, mask=mask):
                send_refs[mask][...] = out_ref[:, at * size : (at + 1) * size]


def head_specs(length, first_head):
    return (
        pl.BlockSpec((HDIM, length), lambda head: (head + first_head, 0)),
        pl.BlockSpec((1, length), lambda head: (0, 0)),
        pl.BlockSpec((1, 1, length), lambda head: (head + first_head, 0, 0)),
    )


def attention_forward(where, n_heads, queries, keys_rot, values, query_segs, key_segs, deps=()):
    cols, length = queries.shape
    heads = cols // HDIM
    wide, row, per_head = head_specs(length, 0)
    result = ordered_call(
        deps,
        functools.partial(attend_kernel, min(BLOCK, length), n_heads),
        grid=(heads,),
        in_specs=[pl.BlockSpec(memory_space=pltpu.SMEM), wide, wide, wide, row, row],
        out_specs=[pl.BlockSpec((HDIM, length), lambda head: (head, 0)), per_head]
        + [pl.BlockSpec((HDIM, length // n_heads), lambda head: (head, 0))] * n_heads,
        out_shape=[
            jax.ShapeDtypeStruct((heads * HDIM, length), LOW),
            jax.ShapeDtypeStruct((heads, 1, length), F32),
        ]
        + [jax.ShapeDtypeStruct((heads * HDIM, length // n_heads), LOW)] * n_heads,
        scratch_shapes=[pltpu.VMEM((HDIM + EXTRA, length), LOW)] * 3,
        compiler_params=pltpu.CompilerParams(vmem_limit_bytes=VMEM_LIMIT),
    )(where, queries, keys_rot, values, query_segs, key_segs)
    return (result[0], result[2:], result[1])


def three_terms(value):
    high = value.astype(LOW).astype(F32)
    middle = (value - high).astype(LOW).astype(F32)
    return (high, middle, value - high - middle)


def attend_back_kernel(block, pieces, where_ref, *refs):
    grad_refs, refs = refs[:pieces], refs[pieces:]
    q_ref, k_ref, v_ref, out_ref, lse_ref, qseg_ref, ksegrow_ref = refs[:7]
    cos_ref, sin_ref, grads_ref, first_ref = refs[7:11]
    dq_ref, dk_ref, dv_ref, q_ext, k_ext, v_ext, g_ext = refs[11:]
    length = q_ref.shape[1]
    half = block // 2
    size = length // pieces
    for index in range(pieces):
        begin = pl.multiple_of(where_ref[index] * size, size)
        g_ext[0:HDIM, pl.ds(begin, size)] = grad_refs[index][...]
    grad_ref = g_ext.at[0:HDIM]
    row_ids, query_rows, key_rows = segment_rows(qseg_ref[...], ksegrow_ref[...])
    delta = jnp.sum(grad_ref[...].astype(F32) * out_ref[...].astype(F32), axis=0, keepdims=True)
    for row, term in enumerate(three_terms(-lse_ref[0])):
        query_rows = jnp.where(row_ids == SEGMENTS + row, term, query_rows)
    key_rows = jnp.where((row_ids >= SEGMENTS) & (row_ids < SEGMENTS + 3), 1.0, key_rows)
    grad_rows = jnp.zeros_like(query_rows)
    for row, term in enumerate(three_terms(-delta)):
        grad_rows = jnp.where(row_ids == row, term, grad_rows)
    q_ext[0:HDIM, :] = q_ref[...]
    k_ext[0:HDIM, :] = k_ref[...]
    v_ext[0:HDIM, :] = v_ref[...]
    q_ext[HDIM:, :] = query_rows.astype(LOW)
    k_ext[HDIM:, :] = key_rows.astype(LOW)
    v_ext[HDIM:, :] = jnp.where(row_ids < 3, 1.0, 0.0).astype(LOW)
    g_ext[HDIM:, :] = grad_rows.astype(LOW)
    own_scores = jnp.sum(q_ref[...].astype(F32) * k_ref[...].astype(F32), axis=0, keepdims=True)
    own_scores = own_scores - lse_ref[0]
    tiles = tile_plan(length, block)

    def score(tile):
        q0, qn, k0, kn, _ = tile
        rows, cols = slice(k0, k0 + kn), slice(q0, q0 + qn)
        scores = dot(k_ext[:, rows], q_ext[:, cols], TN)
        return (scores, dot(v_ext[:, rows], g_ext[:, cols], TN))

    ahead = score(tiles[0])
    for index, (q0, qn, k0, kn, diagonal) in enumerate(tiles):
        scores, grad_probs = ahead
        if index + 1 < len(tiles):
            ahead = score(tiles[index + 1])
        rows, cols = slice(k0, k0 + kn), slice(q0, q0 + qn)
        if diagonal:
            scores = causal(scores, own_scores[:, cols], q0, k0)
        probs = jnp.exp(scores)
        grad_scores = (probs * grad_probs).astype(LOW)
        dv = dot(grad_ref[:, cols], probs.astype(LOW), NT)
        dk = dot(q_ref[:, cols], grad_scores, NT)
        dq = dot(k_ref[:, rows], grad_scores, NN)
        if not diagonal:
            dq_ref[:, cols] += dq
            dk_ref[:, rows] += dk
            dv_ref[:, rows] += dv
            continue
        dq_ref[:, cols] = dq
        if kn == half:
            dk_ref[:, rows] = dk
            dv_ref[:, rows] = dv
        else:
            low_rows, high_rows = slice(k0, k0 + half), slice(k0 + half, k0 + block)
            dk_ref[:, low_rows] += dk[:, :half]
            dv_ref[:, low_rows] += dv[:, :half]
            dk_ref[:, high_rows] = dk[:, half:]
            dv_ref[:, high_rows] = dv[:, half:]
    cosine, sine = cos_ref[...], sin_ref[...]
    grads_ref[0] = turn(dq_ref[...] * HDIM ** (-0.5), cosine, sine, -1.0).astype(LOW)
    grads_ref[1] = turn(dk_ref[...], cosine, sine, -1.0).astype(LOW)
    blended = BLEND * dv_ref[...]
    grads_ref[2] = blended.astype(LOW)
    first_ref[...] = (1.0 - BLEND) * dv_ref[...]


def attention_backward(
    where, group, grad_pieces, queries, keys_rot, values, mixed, lse, segs, cosine, sine, deps=()
):
    query_segs, key_segs = segs
    cols, length = queries.shape
    heads = min(GROUP_HEADS, cols // HDIM)
    wide, row, per_head = head_specs(length, group * heads)
    local = pl.BlockSpec((HDIM, length), lambda head: (head, 0))
    table = pl.BlockSpec((HDIM // 2, length), lambda head: (0, 0))
    piece = pl.BlockSpec((HDIM, length // len(grad_pieces)), lambda head: (head, 0))
    return ordered_call(
        deps,
        functools.partial(attend_back_kernel, min(BLOCK, length), len(grad_pieces)),
        grid=(heads,),
        in_specs=[pl.BlockSpec(memory_space=pltpu.SMEM)]
        + [piece] * len(grad_pieces)
        + [wide, wide, wide, wide, per_head, row, row, table, table],
        out_specs=[pl.BlockSpec((3, HDIM, length), lambda head: (0, head, 0)), local],
        out_shape=[
            jax.ShapeDtypeStruct((3, heads * HDIM, length), LOW),
            jax.ShapeDtypeStruct((heads * HDIM, length), F32),
        ],
        scratch_shapes=[pltpu.VMEM((HDIM, length), F32)] * 3
        + [pltpu.VMEM((HDIM + EXTRA, length), LOW)] * 4,
        compiler_params=pltpu.CompilerParams(vmem_limit_bytes=VMEM_LIMIT),
    )(
        where,
        *grad_pieces,
        queries,
        keys_rot,
        values,
        mixed,
        lse,
        query_segs,
        key_segs,
        cosine,
        sine,
    )


def inverse_root(rows):
    return lax.rsqrt(jnp.mean(rows * rows, axis=-1, keepdims=True) + NORM_EPS)


def join_kernel(n_heads, where_ref, *refs):
    piece_refs, (own_ref, gain_ref, w_ref, hidden_ref, normed_ref) = refs[:n_heads], refs[n_heads:]
    hidden = own_ref[...].astype(F32)
    for mask in range(n_heads):
        hidden += dot(piece_refs[mask][...].T, w_ref[where_ref[mask]], NT)
    hidden_ref[...] = hidden
    normed_ref[...] = (hidden * inverse_root(hidden) * gain_ref[1:2, :]).astype(LOW)


def join_heads(where, pieces, own_rows, gains, out_w, deps=()):
    n_heads = len(pieces)
    tok_rows, width = own_rows.shape
    vmem = pl.BlockSpec(memory_space=pltpu.VMEM)
    return ordered_call(
        deps,
        functools.partial(join_kernel, n_heads),
        in_specs=[pl.BlockSpec(memory_space=pltpu.SMEM)] + [vmem] * (n_heads + 3),
        out_specs=[vmem] * 2,
        out_shape=[
            jax.ShapeDtypeStruct((tok_rows, width), F32),
            jax.ShapeDtypeStruct((tok_rows, width), LOW),
        ],
        compiler_params=pltpu.CompilerParams(vmem_limit_bytes=VMEM_LIMIT),
    )(where, *pieces, own_rows, gains, out_w)


def part_kernel(n_heads, groups, where_ref, *refs):
    own_ref, arrived_ref, hidden_ref, cot_ref, gain_ref, w_ref, grad_ref, gain_grad_ref = refs[:8]
    low_ref, piece_refs = refs[8], refs[9:]
    hidden = hidden_ref[...]
    inverse = inverse_root(hidden)
    grad_two = own_ref[...].astype(F32) + arrived_ref[...].astype(F32)
    scaled = gain_ref[1:2, :] * grad_two
    inner = jnp.mean(scaled * hidden, axis=-1, keepdims=True)
    grad = cot_ref[...].astype(F32) + inverse * scaled - hidden * (inverse**3 * inner)
    gain_grad_ref[...] = jnp.sum(grad_two * hidden * inverse, axis=0, keepdims=True)
    grad_ref[...] = grad
    low = grad.astype(LOW)
    low_ref[...] = low
    rows = piece_refs[0].shape[0]
    for mask in range(n_heads):
        piece = dot(low, w_ref[where_ref[mask]], NN).astype(LOW).T
        for at in range(groups):
            piece_refs[mask * groups + at][...] = piece[at * rows : (at + 1) * rows]


def part_heads(where, groups, back_own, back_arrived, hidden, cotangent, gains, out_w, deps=()):
    n_heads = out_w.shape[0]
    tok_rows, width = hidden.shape
    cols = out_w.shape[-1]
    vmem = pl.BlockSpec(memory_space=pltpu.VMEM)
    result = ordered_call(
        deps,
        functools.partial(part_kernel, n_heads, groups),
        in_specs=[pl.BlockSpec(memory_space=pltpu.SMEM)] + [vmem] * 6,
        out_specs=[vmem] * (3 + n_heads * groups),
        out_shape=[
            jax.ShapeDtypeStruct((tok_rows, width), F32),
            jax.ShapeDtypeStruct((1, width), F32),
            jax.ShapeDtypeStruct((tok_rows, width), LOW),
        ]
        + [jax.ShapeDtypeStruct((cols // groups, tok_rows), LOW)] * (n_heads * groups),
        compiler_params=pltpu.CompilerParams(vmem_limit_bytes=VMEM_LIMIT),
    )(where, back_own, back_arrived, hidden, cotangent, gains, out_w)
    flat = result[3:]
    pieces = [flat[mask * groups : (mask + 1) * groups] for mask in range(n_heads)]
    return result[:3] + [pieces] if isinstance(result, list) else tuple(result[:3]) + (pieces,)


def out_grad_kernel(low_ref, *refs):
    piece_refs, (mine_ref, send_ref) = refs[:-2], refs[-2:]
    turned = low_ref[...].T
    n_seq, n_hid, shares, rows, cols = mine_ref.shape
    for mask in range(2 * shares):
        product = dot(turned, piece_refs[mask][...], NT).astype(LOW).reshape(n_seq, n_hid, rows, cols)
        (send_ref if mask % 2 else mine_ref)[:, :, mask // 2] = product


def out_gradient(low, pieces, n_seq, n_hid, deps=()):
    shares, cols = len(pieces) // 2, pieces[0].shape[0]
    width = low.shape[1]
    vmem = pl.BlockSpec(memory_space=pltpu.VMEM)
    shape = (n_seq, n_hid, shares, width // (n_seq * n_hid), cols)
    return ordered_call(
        deps,
        out_grad_kernel,
        in_specs=[vmem] * (1 + len(pieces)),
        out_specs=[vmem, vmem],
        out_shape=[jax.ShapeDtypeStruct(shape, LOW)] * 2,
        compiler_params=pltpu.CompilerParams(vmem_limit_bytes=VMEM_LIMIT),
    )(low, *pieces)


def ffn_chunks(width):
    return [slice(begin, min(begin + 512, width)) for begin in range(0, width, 512)]


def ffn_kernel(n_heads, n_seq, where_ref, x_ref, c_ref, near_ref, far_ref, gathered_ref, *refs):
    part_ref, back_ref, act_ref, dgate_ref, dup_ref, gate_all, up_w, down_w, sems = refs
    units = act_ref.shape[1]
    copies = [
        pltpu.make_async_copy(gathered_ref.at[:, pl.ds(0, units)], up_w, sems.at[0]),
        pltpu.make_async_copy(gathered_ref.at[:, pl.ds(units, units)], down_w, sems.at[1]),
    ]
    for at in range(n_seq):
        seq_slot = where_ref[n_heads + at]
        for mask in range(n_heads):
            copies.append(
                pltpu.make_async_copy(
                    (far_ref if mask % 2 else near_ref).at[mask // 2, at],
                    gate_all.at[seq_slot, where_ref[mask]],
                    sems.at[len(copies)],
                )
            )
    for copy in copies:
        copy.start()
    rows, model_width = x_ref.shape
    x, c = x_ref[...], c_ref[...]
    for copy in copies:
        copy.wait()
    chunks = ffn_chunks(units)
    for cols in chunks:
        gate = dot(x, gate_all[..., cols].reshape(model_width, -1), NN)
        up = dot(x, up_w[:, cols], NN)
        grad = dot(c, down_w[:, cols], NN)
        sigmoid = jax.nn.sigmoid(gate)
        silu = gate * sigmoid
        act_ref[:, cols] = (silu * up).astype(LOW)
        dgate_ref[:, cols] = (grad * up * (sigmoid + silu * (1.0 - sigmoid))).astype(LOW)
        dup_ref[:, cols] = (grad * silu).astype(LOW)
    per_seq = model_width // n_seq
    for at in range(n_seq):
        here = slice(at * per_seq, (at + 1) * per_seq)
        gate_w = gate_all[at].reshape(per_seq, units)
        back = dot(dgate_ref[...], gate_w, NT) + dot(dup_ref[...], up_w[here, :], NT)
        back_ref[:, here] = back.astype(LOW)
        part_ref[:, here] = dot(act_ref[...], down_w[here, :], NT).astype(LOW)


def feed_forward(where, normed, cotangent, gate_groups, gathered, deps=()):
    rows, width = normed.shape
    shares, n_seq, piece_rows, units = gate_groups[0].shape
    anywhere = pl.BlockSpec(memory_space=pl.ANY)
    vmem = pl.BlockSpec(memory_space=pltpu.VMEM)
    wide = jax.ShapeDtypeStruct((rows, width), LOW)
    narrow = jax.ShapeDtypeStruct((rows, units), LOW)
    return ordered_call(
        deps,
        functools.partial(ffn_kernel, 2 * shares, n_seq),
        in_specs=[pl.BlockSpec(memory_space=pltpu.SMEM), vmem, vmem] + [anywhere] * 3,
        out_specs=[vmem] * 5,
        out_shape=[wide, wide, narrow, narrow, narrow],
        scratch_shapes=[
            pltpu.VMEM((n_seq, 2 * shares, piece_rows, units), LOW),
            pltpu.VMEM((width, units), LOW),
            pltpu.VMEM((width, units), LOW),
            pltpu.SemaphoreType.DMA((2 * shares * n_seq + 2,)),
        ],
        compiler_params=pltpu.CompilerParams(vmem_limit_bytes=VMEM_LIMIT),
    )(where, normed, cotangent, *gate_groups, gathered)


def ffn_grad_kernel(n_heads, *refs):
    (*left_refs, right_refs), out_ref = (refs[:2], refs[2:4], refs[4:8]), refs[8]
    size = out_ref.shape[3]
    for kind, (near_ref, far_ref) in enumerate(left_refs):
        turned = jnp.concatenate([near_ref[...].T, far_ref[...].T], axis=1)
        rows = near_ref.shape[0]
        own_ref, other_ref = right_refs[2 * kind : 2 * kind + 2]
        for cols in ffn_chunks(own_ref.shape[1]):
            both = dot(turned[:, :rows], own_ref[:, cols], NN) + dot(
                turned[:, rows:], other_ref[:, cols], NN
            )
            both = both.astype(LOW)
            for at in range(n_heads):
                out_ref[0, at, kind, :, cols] = both[at * size : (at + 1) * size]


def ffn_gradients(n_heads, n_seq, lefts, rights, deps=()):
    rows, width = lefts[0][0].shape
    units = rights[0][0].shape[1]
    tile = width // n_seq
    left = pl.BlockSpec((rows, tile), lambda at: (0, at))
    right = pl.BlockSpec((rows, units), lambda at: (0, 0))
    shape = (n_heads, 2, tile // n_heads, units)
    return ordered_call(
        deps,
        functools.partial(ffn_grad_kernel, n_heads),
        grid=(n_seq,),
        in_specs=[left] * 4 + [right] * 4,
        out_specs=pl.BlockSpec((1,) + shape, lambda at: (at, 0, 0, 0, 0)),
        out_shape=jax.ShapeDtypeStruct((n_seq,) + shape, LOW),
        compiler_params=pltpu.CompilerParams(vmem_limit_bytes=VMEM_LIMIT),
    )(*lefts[0], *lefts[1], *rights[0], *rights[1])


def by_side(side, first, second):
    return (jnp.where(side == 0, first, second), jnp.where(side == 0, second, first))


def ffn_half_kernel(n_heads, side_at, where_ref, near_ref, far_ref, own_ref, other_ref, mine_ref, send_ref):
    turned = jnp.concatenate([near_ref[...].T, far_ref[...].T], axis=1)
    rows = near_ref.shape[0]
    side = where_ref[side_at]
    size = turned.shape[0] // n_heads
    for cols in ffn_chunks(own_ref.shape[1]):
        both = dot(turned[:, :rows], own_ref[:, cols], NN) + dot(
            turned[:, rows:], other_ref[:, cols], NN
        )
        both = both.astype(LOW)
        for at in range(n_heads // 2):
            begin = 2 * at * size
            first, second = both[begin : begin + size], both[begin + size : begin + 2 * size]
            mine_ref[0, at, :, cols], send_ref[0, at, :, cols] = by_side(side, first, second)


def ffn_halves(where, n_heads, n_seq, side_at, left, right, deps=()):
    rows, width = left[0].shape
    units = right[0].shape[1]
    tile = width // n_seq
    left_tile = pl.BlockSpec((rows, tile), lambda at: (0, at))
    whole = pl.BlockSpec((rows, units), lambda at: (0, 0))
    shape = (n_heads // 2, tile // n_heads, units)
    out = pl.BlockSpec((1,) + shape, lambda at: (at, 0, 0, 0))
    return ordered_call(
        deps,
        functools.partial(ffn_half_kernel, n_heads, side_at),
        grid=(n_seq,),
        in_specs=[pl.BlockSpec(memory_space=pltpu.SMEM), left_tile, left_tile, whole, whole],
        out_specs=[out, out],
        out_shape=[jax.ShapeDtypeStruct((n_seq,) + shape, LOW)] * 2,
        compiler_params=pltpu.CompilerParams(vmem_limit_bytes=VMEM_LIMIT),
    )(where, *left, *right)


def add_halves_kernel(side_at, where_ref, mine_ref, arrived_ref, keep_ref, send_ref):
    side = where_ref[side_at]
    for lead in range(mine_ref.shape[0]):
        for pair in range(mine_ref.shape[1]):
            first, second = (
                (
                    mine_ref[lead, pair, half].astype(F32) + arrived_ref[lead, pair, half].astype(F32)
                ).astype(LOW)
                for half in range(2)
            )
            keep_ref[lead, pair], send_ref[lead, pair] = by_side(side, first, second)


def add_halves(where, side_at, mine, arrived, deps=()):
    lead, pairs, _, rows, cols = mine.shape
    vmem = pl.BlockSpec(memory_space=pltpu.VMEM)
    return ordered_call(
        deps,
        functools.partial(add_halves_kernel, side_at),
        in_specs=[pl.BlockSpec(memory_space=pltpu.SMEM), vmem, vmem],
        out_specs=[vmem, vmem],
        out_shape=[jax.ShapeDtypeStruct((lead, pairs, rows, cols), LOW)] * 2,
        compiler_params=pltpu.CompilerParams(vmem_limit_bytes=VMEM_LIMIT),
    )(where, mine, arrived)


def add_split_kernel(count, first_slot, where_ref, *refs):
    pairs, out_refs = refs[: 2 * count], refs[2 * count :]
    for step, out_ref in enumerate(out_refs):
        at = where_ref[first_slot + step]
        begin = 0
        for mine_ref, arrived_ref in zip(pairs[::2], pairs[1::2]):
            for part in range(mine_ref.shape[1]):
                cols = mine_ref.shape[3]
                both = mine_ref[at, part].astype(F32) + arrived_ref[at, part].astype(F32)
                out_ref[:, begin : begin + cols] = both.astype(LOW)
                begin += cols


def add_split(where, first_slot, *pairs, deps=()):
    vmem = pl.BlockSpec(memory_space=pltpu.VMEM)
    steps, _, rows, _ = pairs[0][0].shape
    width = sum(mine.shape[1] * mine.shape[3] for mine, _ in pairs)
    return ordered_call(
        deps,
        functools.partial(add_split_kernel, len(pairs), first_slot),
        in_specs=[pl.BlockSpec(memory_space=pltpu.SMEM)] + [vmem] * (2 * len(pairs)),
        out_specs=[vmem] * steps,
        out_shape=[jax.ShapeDtypeStruct((rows, width), LOW)] * steps,
        compiler_params=pltpu.CompilerParams(vmem_limit_bytes=VMEM_LIMIT),
    )(where, *[half for pair in pairs for half in pair])


def one_grad_kernel(n_heads, groups, where_ref, *refs):
    grad_refs, w_ref, (mine_ref, send_ref) = refs[:groups], refs[groups], refs[groups + 1 :]
    size = grad_refs[0].shape[2] // n_heads
    for mask in range(n_heads - 1, -1, -1):
        cols = pl.ds(pl.multiple_of(where_ref[mask] * size, size), size)
        grads = jnp.concatenate(
            [grad_refs[at][kind, :, cols] for kind in range(3) for at in range(groups)], axis=0
        )
        (send_ref if mask % 2 else mine_ref)[mask // 2] = dot(grads, w_ref[...], TN).astype(LOW)


def one_gradient(where, n_heads, grads, in_w, deps=()):
    groups = len(grads)
    length = grads[0].shape[2]
    vmem = pl.BlockSpec(memory_space=pltpu.VMEM)
    shape = (n_heads // 2, length // n_heads, in_w.shape[1])
    return ordered_call(
        deps,
        functools.partial(one_grad_kernel, n_heads, groups),
        in_specs=[pl.BlockSpec(memory_space=pltpu.SMEM)] + [vmem] * (groups + 1),
        out_specs=[vmem, vmem],
        out_shape=[jax.ShapeDtypeStruct(shape, LOW)] * 2,
        compiler_params=pltpu.CompilerParams(vmem_limit_bytes=VMEM_LIMIT),
    )(where, *grads, in_w)


def in_grad_kernel(side_at, where_ref, rows_ref, *refs):
    grad_refs, (mine_ref, send_ref) = refs[:-2], refs[-2:]
    n_seq, rows, _ = mine_ref.shape
    side = where_ref[side_at]
    for at, grad_ref in enumerate(grad_refs):
        kinds, cols, length = grad_ref.shape
        grads = grad_ref[...].reshape(kinds * cols, length)
        product = dot(grads, rows_ref[...], NN).astype(LOW).T.reshape(n_seq, 2, rows, kinds * cols)
        here = slice(at * kinds * cols, (at + 1) * kinds * cols)
        mine_ref[:, :, here], send_ref[:, :, here] = by_side(side, product[:, 0], product[:, 1])


def in_gradient(where, side_at, n_seq, group_rows, grads, deps=()):
    groups = len(grads)
    length, width = group_rows.shape
    cols = grads[0].shape[1]
    vmem = pl.BlockSpec(memory_space=pltpu.VMEM)
    shape = (n_seq, width // (2 * n_seq), 3 * cols * groups)
    return ordered_call(
        deps,
        functools.partial(in_grad_kernel, side_at),
        in_specs=[pl.BlockSpec(memory_space=pltpu.SMEM)] + [vmem] * (1 + groups),
        out_specs=[vmem, vmem],
        out_shape=[jax.ShapeDtypeStruct(shape, LOW)] * 2,
        compiler_params=pltpu.CompilerParams(vmem_limit_bytes=VMEM_LIMIT),
    )(where, group_rows, *grads)


def swap(value, axis, mask):
    return lax.ppermute(value, axis, [(i, i ^ mask) for i in range(lax.axis_size(axis))])


def shift(value, axis, step):
    size = lax.axis_size(axis)
    return lax.ppermute(value, axis, [(i, (i + step) % size) for i in range(size)])


def bits_from_high(size):
    bit = size // 2
    while bit:
        yield bit
        bit //= 2


def gather_masks(value, axis, bits):
    held = {0: value}
    for bit in bits:
        held.update({mask ^ bit: swap(block, axis, bit) for mask, block in list(held.items())})
    return held


def from_all(value, axis):
    return [value] + [shift(value, axis, step) for step in range(1, lax.axis_size(axis))]


def total(value, axis):
    size = lax.axis_size(axis)
    bit = 1
    while bit < size:
        if bit * 4 <= size:
            one, two, three = (swap(value, axis, mask * bit) for mask in (1, 2, 3))
            value = (value + one) + (two + three)
            bit *= 4
        else:
            value = value + swap(value, axis, bit)
            bit *= 2
    return value


def tie(*values):
    return lax.optimization_barrier(values)


def send_blocks(blocks, name):
    return [blocks[0]] + [shift(block, name, step) for step, block in enumerate(blocks) if step]


def add_up(blocks):
    result = blocks[0].astype(F32)
    for block in blocks[1:]:
        result = result + block.astype(F32)
    return result


def fold_masks(blocks, bits):
    sums = dict(blocks)
    for bit in bits:
        for mask in sorted(sums, reverse=True):
            if mask & bit:
                moved = swap(sums.pop(mask), "heads", bit)
                if bit == bits[-1]:
                    return (sums[0], moved)
                sums[mask ^ bit] = (sums[mask ^ bit].astype(F32) + moved.astype(F32)).astype(LOW)


def rows_by_default(value):
    return with_layout_constraint(value, Layout(tuple(range(value.ndim))))


def adam_moments(mean_old, var_old, grad):
    mean_new = BETA_ONE * mean_old + (1.0 - BETA_ONE) * grad
    var_new = BETA_TWO * var_old + (1.0 - BETA_TWO) * grad * grad
    direction = (
        mean_new / (1.0 - BETA_ONE**STEP) / (jnp.sqrt(var_new / (1.0 - BETA_TWO**STEP)) + ADAM_EPS)
    )
    return (mean_new, var_new, direction)


def lane_row(values):
    lanes = lax.broadcasted_iota(jnp.int32, (1, ROW), 1)
    row = jnp.zeros((1, ROW), F32)
    for lane, value in values.items():
        row = jnp.where(lanes == lane, value, row)
    return row


def total_of(value):
    return jnp.sum(jnp.sum(value, axis=1, keepdims=True), axis=0, keepdims=True)


def step_part(weight, mean_old, var_old, grad):
    mean_new, var_new, direction = adam_moments(mean_old, var_old, grad)
    update = direction + DECAY * weight
    return (mean_new, var_new, update, total_of(weight * weight), total_of(update * update))


def sum_blocks(refs, rows, cols):
    result = refs[0][rows, cols].astype(F32)
    for ref in refs[1:]:
        result = result + ref[rows, cols].astype(F32)
    return result


def in_step_kernel(n_blocks, groups, *refs):
    block_refs, (w_ref, m_ref, v_ref) = refs[:n_blocks], refs[n_blocks : n_blocks + 3]
    mean_ref, var_ref, update_ref, row_ref = refs[n_blocks + 3 :]
    size = w_ref.shape[2] // groups
    values = {}
    for kind in range(w_ref.shape[0]):
        for at in range(groups):
            here = (kind, slice(None), slice(at * size, (at + 1) * size))
            begin = (at * w_ref.shape[0] + kind) * size
            grad = sum_blocks(block_refs, slice(None), slice(begin, begin + size))
            mean, var, update, weight_sq, update_sq = step_part(
                w_ref[here], m_ref[here], v_ref[here], grad
            )
            mean_ref[here], var_ref[here], update_ref[here] = mean, var, update
            values[kind] = weight_sq + values[kind] if at else weight_sq
            values[MATRICES + kind] = update_sq + values[MATRICES + kind] if at else update_sq
    row_ref[...] = lane_row(values)


def ffn_step_kernel(n_blocks, *refs):
    block_refs, refs = refs[:n_blocks], refs[n_blocks:]
    two_ref, gu_refs, down_refs, out_refs = refs[0], refs[1:4], refs[4:7], refs[7:]
    row_ref = out_refs[6]
    rows = down_refs[0].shape[0]
    values = {}
    for kind in range(3):
        if kind == 1:
            grad = sum_blocks(block_refs, slice(None), slice(None))
        else:
            begin = 0 if kind == 2 else rows
            grad = two_ref[begin : begin + rows, :].astype(F32)
        here = (kind,) if kind < 2 else (slice(None),)
        ins, outs = (gu_refs, out_refs[:3]) if kind < 2 else (down_refs, out_refs[3:6])
        results = step_part(*[ref[here] for ref in ins], grad)
        for ref, result in zip(outs, results[:3]):
            ref[here] = result
        values[4 + kind], values[MATRICES + 4 + kind] = results[3:]
    row_ref[...] = lane_row(values)


def out_step_kernel(own_ref, arrived_ref, w_ref, m_ref, v_ref, mean_ref, var_ref, update_ref, row_ref):
    grad = (own_ref[...].astype(F32) + arrived_ref[...].astype(F32)).T
    mean, var, update, weight_sq, update_sq = step_part(w_ref[...], m_ref[...], v_ref[...], grad)
    mean_ref[...], var_ref[...], update_ref[...] = mean, var, update
    row_ref[...] = lane_row({3: weight_sq, MATRICES + 3: update_sq})


def step_call(kernel, arrays, like, deps=()):
    vmem = pl.BlockSpec(memory_space=pltpu.VMEM)
    shapes = [jax.ShapeDtypeStruct(array.shape, F32) for array in like for _ in range(3)]
    return ordered_call(
        deps,
        kernel,
        in_specs=[vmem] * len(arrays),
        out_specs=[vmem] * (len(shapes) + 1),
        out_shape=shapes + [jax.ShapeDtypeStruct((1, ROW), F32)],
        compiler_params=pltpu.CompilerParams(vmem_limit_bytes=VMEM_LIMIT),
    )(*arrays)


def last_step_kernel(*refs):
    sums_ref, gain_refs, refs = refs[0], refs[1:4], refs[4:]
    weight_refs, update_refs, gain_outs, new_refs = refs[:4], refs[4:8], refs[8:11], refs[11:]
    sums = sums_ref[2:3, :]
    lanes = lax.broadcasted_iota(jnp.int32, sums.shape, 1)

    def lane(at):
        return total_of(jnp.where(lanes == at, sums, 0.0))

    mean_new, var_new, direction = adam_moments(gain_refs[1][...], gain_refs[2][...], sums_ref[0:2, :])
    gain_outs[0][...] = gain_refs[0][...] - GAIN_RATE * direction
    gain_outs[1][...], gain_outs[2][...] = mean_new, var_new
    at = 0
    for weight_ref, update_ref, new_ref in zip(weight_refs, update_refs, new_refs):
        parts = [(kind,) for kind in range(weight_ref.shape[0])]
        for here in parts if len(weight_ref.shape) == 3 else [(slice(None),)]:
            ratio = jnp.sqrt(lane(at)) / jnp.sqrt(lane(MATRICES + at) + 1e-12)
            new_ref[here] = weight_ref[here] - MATRIX_RATE * ratio * update_ref[here]
            at += 1


def last_step(sums, gains, weights, updates):
    vmem = pl.BlockSpec(memory_space=pltpu.VMEM)
    arrays = [sums, *gains, *weights, *updates]
    outs = [jax.ShapeDtypeStruct(array.shape, F32) for array in (*gains, *weights)]
    return ordered_call(
        (),
        last_step_kernel,
        in_specs=[vmem] * len(arrays),
        out_specs=[vmem] * len(outs),
        out_shape=outs,
        compiler_params=pltpu.CompilerParams(vmem_limit_bytes=VMEM_LIMIT),
    )(*arrays)


def input_grad_kernel(own_ref, arrived_ref, tokens_ref, gain_ref, grad_ref, out_ref, gain_grad_ref):
    rows = tokens_ref[...].astype(F32)
    inverse = inverse_root(rows)
    grad_one = own_ref[...].astype(F32) + arrived_ref[...].astype(F32)
    scaled = gain_ref[0:1, :] * grad_one
    inner = jnp.mean(scaled * rows, axis=-1, keepdims=True)
    out_ref[...] = grad_ref[...] + inverse * scaled - rows * (inverse**3 * inner)
    gain_grad_ref[...] = jnp.sum(grad_one * rows * inverse, axis=0, keepdims=True)


def input_gradient(own, arrived, tokens, gains, grad_hidden):
    rows, width = tokens.shape
    vmem = pl.BlockSpec(memory_space=pltpu.VMEM)
    return ordered_call(
        (),
        input_grad_kernel,
        in_specs=[vmem] * 5,
        out_specs=[vmem] * 2,
        out_shape=[
            jax.ShapeDtypeStruct((rows, width), F32),
            jax.ShapeDtypeStruct((1, width), F32),
        ],
        compiler_params=pltpu.CompilerParams(vmem_limit_bytes=VMEM_LIMIT),
    )(own, arrived, tokens, gains, grad_hidden)


def rope_tables(position_ids):
    half_dim = HDIM // 2
    freqs = ROPE_BASE ** (-(jnp.arange(half_dim, dtype=jnp.float32) * 2.0 / HDIM))
    angles = freqs[:, None] * position_ids.astype(jnp.float32)[None, :]
    return (jnp.cos(angles), jnp.sin(angles))


def per_device(
    tokens_in,
    first_value,
    cotangent,
    counts,
    segments,
    positions,
    norm_gains,
    gain_mean,
    gain_var,
    heads_in,
    heads_in_mean,
    heads_in_var,
    heads_out,
    heads_out_mean,
    heads_out_var,
    gate_up,
    gate_up_mean,
    gate_up_var,
    down_proj,
    down_mean,
    down_var,
):
    n_seq, n_heads, n_hid = (lax.axis_size(name) for name in ("seq", "heads", "hid"))
    at_seq, at_heads, at_hid = (lax.axis_index(name) for name in ("seq", "heads", "hid"))
    own_rows = tokens_in[0].astype(F32)
    tok_rows, model_width = own_rows.shape
    length = tok_rows * n_heads
    head_cols = heads_in.shape[2]
    hidden_cols = gate_up.shape[2]
    near = 1
    far_bits = [bit for bit in bits_from_high(n_heads) if bit > near]
    masks = list(range(n_heads))
    groups = max(1, head_cols // HDIM // GROUP_HEADS)
    seq_slots = [lax.rem(at_seq + n_seq - step, n_seq) for step in range(n_seq)]
    where = jnp.stack(
        [at_heads ^ mask for mask in masks]
        + seq_slots
        + [at_hid, at_hid ^ 1]
        + [lax.rem(at_seq + step, n_seq) for step in range(n_seq)]
        + [lax.rem(at_heads // bit, 2) for bit in [near] + far_bits[::-1]]
    ).astype(jnp.int32)
    hid_side = n_heads + n_seq
    seq_steps = hid_side + 2
    heads_sides = seq_steps + n_seq

    head_low, own_rows = tie(
        jnp.concatenate(
            [jnp.swapaxes(heads_in, 0, 1).reshape(-1, 3 * head_cols), heads_out.T], axis=1
        ).astype(LOW),
        own_rows,
    )
    in_low, out_low = head_low[:, : 3 * head_cols], head_low[:, 3 * head_cols :]
    half = in_low.shape[0] // 2
    upper_pieces = from_all(in_low[:half], "seq")
    out_flat = out_low.reshape(half, -1)
    lower_sent = jnp.concatenate([in_low[half:], out_flat], axis=1)
    lower_moved = swap(lower_sent, "hid", 1)

    inv_one = inverse_root(own_rows)
    normed_one = (own_rows * inv_one * norm_gains[0]).astype(LOW)

    piece_rows = gate_up.shape[1]
    out_pair = jnp.stack([out_flat, lower_moved[:, 3 * head_cols :]]).reshape(piece_rows, -1)
    far_blocks = gather_masks(normed_one, "heads", far_bits)
    lower_moved, far_blocks[0] = tie(lower_moved, far_blocks[0])

    piece_rows = gate_up.shape[1]
    out_pair = jnp.stack([out_flat, lower_moved[:, 3 * head_cols :]]).reshape(piece_rows, -1)
    gathered = lax.all_gather(
        jnp.concatenate([gate_up[1].astype(LOW), down_proj.T.astype(LOW), out_pair], axis=1),
        ("seq", "heads"),
        axis=0,
        tiled=True,
    )

    upper_pieces, lower_pair = tie(
        upper_pieces, jnp.stack([in_low[half:], lower_moved[:, : 3 * head_cols]])
    )
    upper, lower_pair = tie(jnp.stack(upper_pieces), lower_pair)
    upper_moved = swap(upper, "hid", 1)
    lower_pieces = from_all(lower_pair, "seq")
    far_blocks, lower_pieces, gate_low = tie(
        far_blocks, lower_pieces, gate_up[0].astype(LOW)
    )
    gate_pieces = from_all(gate_low, "seq")
    far_rows = jnp.stack([far_blocks[mask] for mask in masks[::2]])
    near_rows = swap(far_rows, "heads", near)
    lower = jnp.stack(lower_pieces)
    row_blocks = [(near_rows if mask % 2 else far_rows)[mask // 2] for mask in masks]
    cosine, sine_table = rope_tables(positions[0])
    row_ids = jnp.arange(length, dtype=jnp.int32)
    is_valid = row_ids % tok_rows < jnp.repeat(counts[0], tok_rows, total_repeat_length=length)
    segs = (segments, jnp.where(is_valid[None], segments, -1))
    group_rows, in_w, queries, keys_rot, values = project(
        where,
        row_blocks,
        upper,
        upper_moved,
        lower,
        first_value[0],
        cosine,
        sine_table,
        deps=segs,
    )
    group_rows = group_rows.reshape(length, model_width)
    cot_low, queries = tie(cotangent[0], queries)
    back_other = swap(cot_low, "hid", 1)

    mixed, sends, lse = attention_forward(where, n_heads, queries, keys_rot, values, *segs)
    gate_pieces, back_other, lse = tie(gate_pieces, back_other, lse)
    gate_stack = jnp.stack(gate_pieces)
    gate_blocks = gather_masks(gate_stack, "heads", far_bits)
    arrived = [swap(sends[mask], "heads", mask) if mask else sends[mask] for mask in masks]
    out_w = gathered[:, 2 * hidden_cols :].reshape(n_seq, n_heads, 2, 2 * half, head_cols)
    out_w = jnp.where(at_hid == 0, out_w, out_w[:, :, ::-1])
    out_w = jnp.moveaxis(out_w, 1, 0).reshape(n_heads, model_width, head_cols)
    gate_blocks, arrived, out_w = tie(gate_blocks, arrived, out_w)
    gate_near = jnp.stack([gate_blocks[mask] for mask in masks[::2]])
    gate_far = swap(gate_near, "heads", near)
    hidden, normed_two = join_heads(where, arrived, tokens_in[0], norm_gains, out_w)
    normed_other = swap(normed_two, "hid", 1)
    weights = ((gate_near, gate_far), gathered)

    ffn_own, back_own, act_own, dgate_own, dup_own = feed_forward(
        where, normed_two, cotangent[0], *weights
    )
    ffn_far, back_far, act_far, dgate_far, dup_far = feed_forward(
        where, normed_other, back_other, *weights, deps=back_own
    )
    back_arrived = swap(back_far, "hid", 1)

    lefts = ((cotangent[0], back_other), (normed_two, normed_other))
    made = ffn_gradients(
        n_heads, n_seq, lefts, ((act_own, act_far), (dgate_own, dgate_far)), deps=back_far
    )
    up_mine, up_sent = ffn_halves(
        where, n_heads, n_seq, heads_sides, lefts[1], (dup_own, dup_far), deps=made
    )

    def next_halves(mine, arrived_half, bit_at, deps=()):
        lead, blocks, rows, cols = mine.shape
        shape = (lead, blocks // 2, 2, rows, cols)
        return add_halves(
            where, heads_sides + bit_at, mine.reshape(shape), arrived_half.reshape(shape), deps=deps
        )

    grad_hidden, gain_grad_two, grad_hidden_low, grad_pieces = part_heads(
        where,
        groups,
        back_own,
        back_arrived,
        hidden,
        cotangent[0],
        norm_gains,
        out_w,
        deps=up_sent,
    )
    up_sent, made, ffn_far, grad_hidden_low = tie(up_sent, made, ffn_far, grad_hidden_low)
    first_two = lax.psum_scatter(
        made.reshape(-1, hidden_cols), ("seq", "heads"), scatter_dimension=0, tiled=True
    )
    grad_arrived = []
    for group in range(groups):
        pieces = [grad_pieces[mask][group] for mask in masks]
        if grad_arrived:
            pieces, out_sent, grad_arrived[-1] = tie(pieces, out_sent, grad_arrived[-1])
            out_half = swap(out_sent, "heads", near)
        grad_arrived.append(
            [pieces[0]] + [swap(pieces[mask], "heads", mask) for mask in masks[1:]]
        )
        if not group:
            up_half = swap(up_sent, "heads", near)
            ffn_arrived = swap(ffn_far, "hid", 1)
            up_mine, up_sent = next_halves(up_mine, up_half, 1)
            out_mine, out_sent = out_gradient(
                grad_hidden_low, arrived, n_seq, n_hid, deps=up_sent
            )
    if groups == 1:
        out_half = swap(out_sent, "heads", near)
    back = []
    deps = ()
    for group in range(groups):
        back.append(
            attention_backward(
                where,
                group,
                grad_arrived[group],
                queries,
                keys_rot,
                values,
                mixed,
                lse,
                segs,
                cosine,
                sine_table,
                deps=deps,
            )
        )
        if group == 0:
            out_mine, out_sent = add_halves(
                where,
                hid_side,
                out_mine.reshape(n_seq, 1, 2, -1, head_cols),
                out_half.reshape(n_seq, 1, 2, -1, head_cols),
                deps=(back[0][1], ffn_arrived),
            )
            up_sent, out_sent = tie(up_sent, out_sent)
            out_half = swap(out_sent, "hid", 1)
            up_half = swap(up_sent, "heads", 2)
            for bit_at, bit in enumerate(far_bits[::-1][1:], 2):
                up_mine, up_sent = next_halves(up_mine, up_half, bit_at)
                up_half = swap(up_sent, "heads", bit)
            deps = (out_sent, up_sent)
    block_out = (hidden + (ffn_own.astype(F32) + ffn_arrived.astype(F32))).astype(LOW)[None]
    grads = [pair[0] for pair in back]
    in_mine, in_sent = in_gradient(where, hid_side, n_seq, group_rows, grads)
    in_half = swap(in_sent, "hid", 1)
    shares_shape = (n_seq, n_heads // 2, -1, head_cols)
    out_blocks = add_split(
        where,
        seq_steps,
        (out_mine.reshape(shares_shape), out_half.reshape(shares_shape)),
        deps=in_sent,
    )
    out_blocks = send_blocks(out_blocks, "seq")
    one_mine, one_sent = one_gradient(where, n_heads, grads, in_w, deps=out_blocks[0])
    one_moved = swap(one_sent, "heads", near)
    up_blocks = add_split(where, seq_steps, (up_mine, up_half), deps=one_sent)
    one_moved, up_blocks, out_blocks = tie(one_moved, up_blocks, out_blocks)
    up_blocks = send_blocks(up_blocks, "seq")
    near_sums = (one_mine.astype(F32) + one_moved.astype(F32)).astype(LOW)
    one_own, one_arrived = fold_masks({mask: near_sums[mask // 2] for mask in masks[::2]}, far_bits)
    in_half, near_sums = tie(in_half, near_sums)
    in_blocks = add_split(where, seq_steps, (in_mine[:, None], in_half[:, None]), deps=near_sums)
    up_blocks, in_blocks = tie(up_blocks, in_blocks)
    in_blocks = send_blocks(in_blocks, "seq")

    gu = (gate_up, gate_up_mean, gate_up_var)
    dn = [array.T for array in (down_proj, down_mean, down_var)]
    gu_mean, gu_var, gu_update, dn_mean, dn_var, dn_update, ffn_row = step_call(
        functools.partial(ffn_step_kernel, n_seq),
        [*up_blocks, first_two, *gu, *dn],
        (gate_up, dn[0]),
        deps=in_blocks[0],
    )
    out_blocks, out_first = tie(out_blocks, in_blocks[0])
    out_part = add_up(out_blocks).astype(LOW).reshape(-1, n_heads // 2, head_cols)
    out_own, out_arrived = fold_masks({mask: out_part[:, mask // 2] for mask in masks[::2]}, far_bits)
    out_mean, out_var, out_update, out_row = step_call(
        out_step_kernel,
        [out_own, out_arrived, heads_out, heads_out_mean, heads_out_var],
        (heads_out,),
        deps=ffn_row,
    )
    first_grad = jnp.concatenate([first for _, first in back], axis=0).T[None]
    in_blocks, out_row, first_grad, block_out = tie(
        [out_first, *in_blocks[1:]], out_row, first_grad, block_out
    )
    in_mean, in_var, in_update, in_row = step_call(
        functools.partial(in_step_kernel, n_seq, groups),
        [*in_blocks, heads_in, heads_in_mean, heads_in_var],
        (heads_in,),
    )
    input_grad, gain_grad_one = input_gradient(
        one_own, one_arrived, tokens_in[0], norm_gains, grad_hidden
    )
    first_wide, blended_wide = first_value[0].astype(F32), values.astype(F32)
    value_row = lane_row(
        {
            2 * MATRICES: jnp.sum(first_wide * first_wide),
            2 * MATRICES + 1: jnp.sum(blended_wide * blended_wide),
        }
    )
    packed = jnp.concatenate(
        [gain_grad_one, gain_grad_two, ffn_row + out_row + (in_row + value_row)], axis=0
    )
    for axis in ("heads", "seq", "hid"):
        packed = total(packed, axis)
    gains_new, gmean_new, gvar_new, in_new, out_new, gu_new, dn_new = last_step(
        packed,
        (norm_gains, gain_mean, gain_var),
        (heads_in, heads_out, gate_up, dn[0]),
        (in_update, out_update, gu_update, dn_update),
    )
    dn_new, dn_mean, dn_var = (array.T for array in (dn_new, dn_mean, dn_var))
    entries = float(
        length * head_cols * lax.axis_size("seq") * lax.axis_size("heads") * lax.axis_size("hid")
    )
    norms = jnp.sqrt(packed[2, : 2 * MATRICES])
    value_norms = jnp.sqrt(packed[2, 2 * MATRICES : 2 * MATRICES + 2] / entries)
    return (
        block_out,
        input_grad[None],
        first_grad,
        gains_new,
        gmean_new,
        gvar_new,
        in_new,
        in_mean,
        in_var,
        out_new,
        out_mean,
        out_var,
        gu_new,
        gu_mean,
        gu_var,
        dn_new,
        dn_mean,
        dn_var,
        norms,
        value_norms,
    )


def solution(mesh):
    placed = (
        P(("seq", "hid"), "heads", None),
        P(("seq", "hid"), None, "heads"),
        P(("seq", "hid"), "heads", None),
        P(("seq", "hid"), None),
        P(("seq", "hid"), None),
        P(("seq", "hid"), None),
        P(),
        P(),
        P(),
        P(None, ("seq", "hid"), "heads"),
        P(None, ("seq", "hid"), "heads"),
        P(None, ("seq", "hid"), "heads"),
        P("heads", ("seq", "hid")),
        P("heads", ("seq", "hid")),
        P("heads", ("seq", "hid")),
        P(None, ("seq", "heads"), "hid"),
        P(None, ("seq", "heads"), "hid"),
        P(None, ("seq", "heads"), "hid"),
        P("hid", ("seq", "heads")),
        P("hid", ("seq", "heads")),
        P("hid", ("seq", "heads")),
    )
    return jax.shard_map(
        per_device,
        mesh=mesh,
        in_specs=placed,
        out_specs=(
            P(("seq", "hid"), "heads", None),
            P(("seq", "hid"), "heads", None),
            P(("seq", "hid"), None, "heads"),
            P(),
            P(),
            P(),
            P(None, ("seq", "hid"), "heads"),
            P(None, ("seq", "hid"), "heads"),
            P(None, ("seq", "hid"), "heads"),
            P("heads", ("seq", "hid")),
            P("heads", ("seq", "hid")),
            P("heads", ("seq", "hid")),
            P(None, ("seq", "heads"), "hid"),
            P(None, ("seq", "heads"), "hid"),
            P(None, ("seq", "heads"), "hid"),
            P("hid", ("seq", "heads")),
            P("hid", ("seq", "heads")),
            P("hid", ("seq", "heads")),
            P(),
            P(),
        ),
        check_vma=False,
    )
```

```python
import functools

import jax
import jax.numpy as jnp
from jax import lax
from jax.experimental import pallas as pl
from jax.experimental.layout import Layout, with_layout_constraint
from jax.experimental.pallas import tpu as pltpu
from jax.sharding import PartitionSpec as P

HDIM = 64
STEP = 10


NORM_EPS = 1e-05
ROPE_BASE = 10000.0
BLEND = 0.5
BETA_ONE = 0.9
BETA_TWO = 0.999
ADAM_EPS = 1e-06
DECAY = 0.01
MATRIX_RATE = 0.25
GAIN_RATE = 0.7
NEG_LARGE = -1e30

BLOCK = 512
EXTRA = 16
SEGMENTS = 3
MATRICES = 7
ROW = 1024
NN = ((1,), (0,))
NT = ((1,), (1,))
TN = ((0,), (0,))
VMEM_LIMIT = 62 << 20
F32 = jnp.float32
LOW = jnp.bfloat16


def dot(left, right, dims):
    return lax.dot_general(left, right, (dims, ((), ())), preferred_element_type=F32)


def ordered_call(deps, kernel, *, in_specs, **rest):
    extra = jax.tree.leaves(deps)
    count = len(in_specs)

    def body(*refs):
        kernel(*refs[:count], *refs[count + len(extra) :])

    in_specs = in_specs + [pl.BlockSpec(memory_space=pl.ANY)] * len(extra)
    call = pl.pallas_call(body, in_specs=in_specs, **rest)
    return lambda *operands: call(*operands, *extra)


def tile_plan(length, block):
    tiles = []
    half = block // 2
    for begin in range(0, length, block):
        tiles.append((begin, half, begin, half, True))
        tiles.append((begin + half, half, begin, block, True))
        for key_begin in range(0, begin, block):
            tiles.append((begin, block, key_begin, block, False))
    return tiles


def causal(scores, own_scores, query_begin, key_begin):
    rows = lax.broadcasted_iota(jnp.int32, scores.shape, 0) + (key_begin - query_begin)
    cols = lax.broadcasted_iota(jnp.int32, scores.shape, 1)
    return jnp.where(rows < cols, scores, jnp.where(rows == cols, own_scores, NEG_LARGE))


def segment_rows(query_segs, key_segs):
    shape = (EXTRA, query_segs.shape[1])
    row_ids = lax.broadcasted_iota(jnp.int32, shape, 0)
    query_rows = jnp.where(row_ids == query_segs, 1.0, 0.0)
    key_rows = jnp.where((row_ids < SEGMENTS) & (row_ids != key_segs), NEG_LARGE, 0.0)
    return (row_ids, query_rows, key_rows)


def move_all(moves, sems):
    copies = [
        pltpu.make_async_copy(source, target, sems.at[index])
        for index, (source, target) in enumerate(moves)
    ]
    for copy in copies:
        copy.start()
    for copy in copies:
        copy.wait()


def turn(rows, cosine, sine, sign):
    parts = []
    for begin in range(0, rows.shape[0], HDIM):
        middle = begin + HDIM // 2
        first, second = rows[begin:middle], rows[middle : begin + HDIM]
        parts.append(first * cosine - sign * (second * sine))
        parts.append(second * cosine + sign * (first * sine))
    return jnp.concatenate(parts, axis=0)


def project_kernel(n_heads, n_seq, where_ref, *refs):
    near_ref, far_ref, refs = refs[0], refs[1], refs[2:]
    upper_ref, moved_ref, lower_ref, first_ref, cos_ref, sin_ref = refs[:6]
    rows_ref, turned, q_ref, k_ref, v_ref, w_ref, sems = refs[6:]
    half = upper_ref.shape[1]
    upper, lower = pl.ds(0, half), pl.ds(half, half)
    cols = q_ref.shape[0]
    tok_rows, width = near_ref.shape[1:]
    moves = [
        ((far_ref if mask % 2 else near_ref).at[mask // 2], rows_ref.at[where_ref[mask]])
        for mask in range(n_heads)
    ]
    own, other = where_ref[n_heads + n_seq], where_ref[n_heads + n_seq + 1]
    for at in range(n_seq):
        slot = where_ref[n_heads + at]
        moves.append((upper_ref.at[at], w_ref.at[slot, own, upper]))
        moves.append((moved_ref.at[at], w_ref.at[slot, other, upper]))
        moves.append((lower_ref.at[at, 0], w_ref.at[slot, own, lower]))
        moves.append((lower_ref.at[at, 1], w_ref.at[slot, other, lower]))
    move_all(moves, sems)
    turned[...] = w_ref[...].reshape(width, 3 * cols).T
    for at in range(n_heads):
        here = slice(at * tok_rows, (at + 1) * tok_rows)
        projected = dot(turned[...], rows_ref[at], NT)
        cosine, sine = cos_ref[:, here], sin_ref[:, here]
        q_ref[:, here] = (turn(projected[:cols], cosine, sine, 1.0) * HDIM ** (-0.5)).astype(LOW)
        k_ref[:, here] = turn(projected[cols : 2 * cols], cosine, sine, 1.0).astype(LOW)
        first = first_ref[here, :].astype(F32).T
        v_ref[:, here] = (BLEND * projected[2 * cols :] + (1.0 - BLEND) * first).astype(LOW)


def project(where, near_rows, far_rows, upper, upper_moved, lower, first_local, cosine, sine, deps=()):
    n_heads, n_seq = 2 * near_rows.shape[0], upper.shape[0]
    tok_rows, width = near_rows.shape[1:]
    length, cols = first_local.shape
    anywhere = pl.BlockSpec(memory_space=pl.ANY)
    vmem = pl.BlockSpec(memory_space=pltpu.VMEM)
    count = n_heads + 4 * n_seq
    head_rows = jax.ShapeDtypeStruct((cols, length), LOW)
    return ordered_call(
        deps,
        functools.partial(project_kernel, n_heads, n_seq),
        in_specs=[pl.BlockSpec(memory_space=pltpu.SMEM)]
        + [anywhere] * 5
        + [vmem] * 3,
        out_specs=[vmem] * 5,
        out_shape=[
            jax.ShapeDtypeStruct((n_heads, tok_rows, width), LOW),
            jax.ShapeDtypeStruct((3 * cols, width), LOW),
            head_rows,
            head_rows,
            head_rows,
        ],
        scratch_shapes=[
            pltpu.VMEM((n_seq, 2, 2 * upper.shape[1], upper.shape[2]), LOW),
            pltpu.SemaphoreType.DMA((count,)),
        ],
        compiler_params=pltpu.CompilerParams(vmem_limit_bytes=VMEM_LIMIT),
    )(where, near_rows, far_rows, upper, upper_moved, lower, first_local, cosine, sine)


def attend_kernel(block, n_heads, where_ref, *refs):
    q_ref, k_ref, v_ref, qseg_ref, ksegrow_ref, out_ref, lse_ref = refs[:7]
    send_refs, (q_ext, k_ext, v_ext) = refs[7 : 7 + n_heads], refs[7 + n_heads :]
    length = q_ref.shape[1]
    size = length // n_heads
    row_ids, query_rows, key_rows = segment_rows(qseg_ref[...], ksegrow_ref[...])
    q_ext[0:HDIM, :] = q_ref[...]
    k_ext[0:HDIM, :] = k_ref[...]
    v_ext[0:HDIM, :] = v_ref[...]
    q_ext[HDIM:, :] = query_rows.astype(LOW)
    k_ext[HDIM:, :] = key_rows.astype(LOW)
    v_ext[HDIM:, :] = jnp.where(row_ids == 0, 1.0, 0.0).astype(LOW)
    own_scores = jnp.sum(q_ref[...].astype(F32) * k_ref[...].astype(F32), axis=0, keepdims=True)
    tiles = tile_plan(length, block)

    def score(tile):
        q0, qn, k0, kn, _ = tile
        return dot(k_ext[:, k0 : k0 + kn], q_ext[:, q0 : q0 + qn], TN)

    ahead = score(tiles[0])
    halves = []
    state = None
    for index, (q0, qn, k0, kn, diagonal) in enumerate(tiles):
        scores = ahead
        if index + 1 < len(tiles):
            ahead = score(tiles[index + 1])
        if diagonal:
            scores = causal(scores, own_scores[:, q0 : q0 + qn], q0, k0)
        new_max = jnp.max(scores, axis=0, keepdims=True)
        if not diagonal:
            new_max = jnp.maximum(state[0], new_max)
        probs = jnp.exp(scores - new_max).astype(LOW)
        mixed = dot(v_ext[:, k0 : k0 + kn], probs, NN)
        if diagonal:
            halves.append((new_max, mixed))
            if len(halves) == 2:
                state = tuple(jnp.concatenate(pair, axis=1) for pair in zip(*halves))
                halves = []
        else:
            state = (new_max, state[1] * jnp.exp(state[0] - new_max) + mixed)
        if index + 1 == len(tiles) or (tiles[index + 1][4] and not halves):
            total_row = state[1][HDIM : HDIM + 1, :]
            begin = (q0 // block) * block
            out_ref[:, begin : begin + block] = (state[1][0:HDIM, :] / total_row).astype(LOW)
            lse_ref[0, :, begin : begin + block] = state[0] + jnp.log(total_row)
    for at in range(n_heads):
        for mask in range(n_heads):

            @pl.when(where_ref[at] == mask)
            def _(at=at, mask=mask):
                send_refs[mask][...] = out_ref[:, at * size : (at + 1) * size]


def head_specs(length, first_head):
    return (
        pl.BlockSpec((HDIM, length), lambda head: (head + first_head, 0)),
        pl.BlockSpec((1, length), lambda head: (0, 0)),
        pl.BlockSpec((1, 1, length), lambda head: (head + first_head, 0, 0)),
    )


def attention_forward(where, n_heads, queries, keys_rot, values, query_segs, key_segs, deps=()):
    cols, length = queries.shape
    heads = cols // HDIM
    wide, row, per_head = head_specs(length, 0)
    result = ordered_call(
        deps,
        functools.partial(attend_kernel, min(BLOCK, length), n_heads),
        grid=(heads,),
        in_specs=[pl.BlockSpec(memory_space=pltpu.SMEM), wide, wide, wide, row, row],
        out_specs=[pl.BlockSpec((HDIM, length), lambda head: (head, 0)), per_head]
        + [pl.BlockSpec((HDIM, length // n_heads), lambda head: (head, 0))] * n_heads,
        out_shape=[
            jax.ShapeDtypeStruct((heads * HDIM, length), LOW),
            jax.ShapeDtypeStruct((heads, 1, length), F32),
        ]
        + [jax.ShapeDtypeStruct((heads * HDIM, length // n_heads), LOW)] * n_heads,
        scratch_shapes=[pltpu.VMEM((HDIM + EXTRA, length), LOW)] * 3,
        compiler_params=pltpu.CompilerParams(vmem_limit_bytes=VMEM_LIMIT),
    )(where, queries, keys_rot, values, query_segs, key_segs)
    return (result[0], result[2:], result[1])


def three_terms(value):
    high = value.astype(LOW).astype(F32)
    middle = (value - high).astype(LOW).astype(F32)
    return (high, middle, value - high - middle)


def attend_back_kernel(block, pieces, where_ref, *refs):
    grad_refs, refs = refs[:pieces], refs[pieces:]
    q_ref, k_ref, v_ref, out_ref, lse_ref, qseg_ref, ksegrow_ref = refs[:7]
    cos_ref, sin_ref, grads_ref, first_ref = refs[7:11]
    dq_ref, dk_ref, dv_ref, q_ext, k_ext, v_ext, g_ext = refs[11:]
    length = q_ref.shape[1]
    half = block // 2
    size = length // pieces
    for index in range(pieces):
        begin = pl.multiple_of(where_ref[index] * size, size)
        g_ext[0:HDIM, pl.ds(begin, size)] = grad_refs[index][...]
    grad_ref = g_ext.at[0:HDIM]
    row_ids, query_rows, key_rows = segment_rows(qseg_ref[...], ksegrow_ref[...])
    delta = jnp.sum(grad_ref[...].astype(F32) * out_ref[...].astype(F32), axis=0, keepdims=True)
    for row, term in enumerate(three_terms(-lse_ref[0])):
        query_rows = jnp.where(row_ids == SEGMENTS + row, term, query_rows)
    key_rows = jnp.where((row_ids >= SEGMENTS) & (row_ids < SEGMENTS + 3), 1.0, key_rows)
    grad_rows = jnp.zeros_like(query_rows)
    for row, term in enumerate(three_terms(-delta)):
        grad_rows = jnp.where(row_ids == row, term, grad_rows)
    q_ext[0:HDIM, :] = q_ref[...]
    k_ext[0:HDIM, :] = k_ref[...]
    v_ext[0:HDIM, :] = v_ref[...]
    q_ext[HDIM:, :] = query_rows.astype(LOW)
    k_ext[HDIM:, :] = key_rows.astype(LOW)
    v_ext[HDIM:, :] = jnp.where(row_ids < 3, 1.0, 0.0).astype(LOW)
    g_ext[HDIM:, :] = grad_rows.astype(LOW)
    own_scores = jnp.sum(q_ref[...].astype(F32) * k_ref[...].astype(F32), axis=0, keepdims=True)
    own_scores = own_scores - lse_ref[0]
    tiles = tile_plan(length, block)

    def score(tile):
        q0, qn, k0, kn, _ = tile
        rows, cols = slice(k0, k0 + kn), slice(q0, q0 + qn)
        scores = dot(k_ext[:, rows], q_ext[:, cols], TN)
        return (scores, dot(v_ext[:, rows], g_ext[:, cols], TN))

    ahead = score(tiles[0])
    for index, (q0, qn, k0, kn, diagonal) in enumerate(tiles):
        scores, grad_probs = ahead
        if index + 1 < len(tiles):
            ahead = score(tiles[index + 1])
        rows, cols = slice(k0, k0 + kn), slice(q0, q0 + qn)
        if diagonal:
            scores = causal(scores, own_scores[:, cols], q0, k0)
        probs = jnp.exp(scores)
        grad_scores = (probs * grad_probs).astype(LOW)
        dv = dot(grad_ref[:, cols], probs.astype(LOW), NT)
        dk = dot(q_ref[:, cols], grad_scores, NT)
        dq = dot(k_ref[:, rows], grad_scores, NN)
        if not diagonal:
            dq_ref[:, cols] += dq
            dk_ref[:, rows] += dk
            dv_ref[:, rows] += dv
            continue
        dq_ref[:, cols] = dq
        if kn == half:
            dk_ref[:, rows] = dk
            dv_ref[:, rows] = dv
        else:
            low_rows, high_rows = slice(k0, k0 + half), slice(k0 + half, k0 + block)
            dk_ref[:, low_rows] += dk[:, :half]
            dv_ref[:, low_rows] += dv[:, :half]
            dk_ref[:, high_rows] = dk[:, half:]
            dv_ref[:, high_rows] = dv[:, half:]
    cosine, sine = cos_ref[...], sin_ref[...]
    grads_ref[0] = turn(dq_ref[...] * HDIM ** (-0.5), cosine, sine, -1.0).astype(LOW)
    grads_ref[1] = turn(dk_ref[...], cosine, sine, -1.0).astype(LOW)
    blended = BLEND * dv_ref[...]
    grads_ref[2] = blended.astype(LOW)
    first_ref[...] = (1.0 - BLEND) * dv_ref[...]


def attention_backward(
    where, group, grad_pieces, queries, keys_rot, values, mixed, lse, segs, cosine, sine, deps=()
):
    query_segs, key_segs = segs
    cols, length = queries.shape
    heads = cols // HDIM
    wide, row, per_head = head_specs(length, group * heads)
    local = pl.BlockSpec((HDIM, length), lambda head: (head, 0))
    table = pl.BlockSpec((HDIM // 2, length), lambda head: (0, 0))
    piece = pl.BlockSpec((HDIM, length // len(grad_pieces)), lambda head: (head, 0))
    return ordered_call(
        deps,
        functools.partial(attend_back_kernel, min(BLOCK, length), len(grad_pieces)),
        grid=(heads,),
        in_specs=[pl.BlockSpec(memory_space=pltpu.SMEM)]
        + [piece] * len(grad_pieces)
        + [wide, wide, wide, wide, per_head, row, row, table, table],
        out_specs=[pl.BlockSpec((3, HDIM, length), lambda head: (0, head, 0)), local],
        out_shape=[
            jax.ShapeDtypeStruct((3, heads * HDIM, length), LOW),
            jax.ShapeDtypeStruct((heads * HDIM, length), F32),
        ],
        scratch_shapes=[pltpu.VMEM((HDIM, length), F32)] * 3
        + [pltpu.VMEM((HDIM + EXTRA, length), LOW)] * 4,
        compiler_params=pltpu.CompilerParams(vmem_limit_bytes=VMEM_LIMIT),
    )(
        where,
        *grad_pieces,
        queries,
        keys_rot,
        values,
        mixed,
        lse,
        query_segs,
        key_segs,
        cosine,
        sine,
    )


def inverse_root(rows):
    return lax.rsqrt(jnp.mean(rows * rows, axis=-1, keepdims=True) + NORM_EPS)


def join_kernel(n_heads, n_seq, where_ref, *refs):
    piece_refs, refs = refs[:n_heads], refs[n_heads:]
    own_ref, gain_ref, gathered_ref, w_ref, hidden_ref, normed_ref = refs[:6]
    half_refs, (placed, sems) = refs[6:8], refs[8:]
    width, cols = w_ref.shape[1:]
    rows = gathered_ref.shape[0] // (n_seq * n_heads)
    flats = placed.shape[3]
    first_lane = gathered_ref.shape[1] - 2 * flats * cols
    moves = []
    for seq in range(n_seq):
        for head in range(n_heads):
            here = pl.ds((seq * n_heads + head) * rows, rows)
            for side in range(2):
                slot = where_ref[n_heads + n_seq + side]
                for flat in range(flats):
                    lanes = pl.ds(first_lane + (side * flats + flat) * cols, cols)
                    moves.append((gathered_ref.at[here, lanes], placed.at[head, seq, slot, flat]))
    move_all(moves, sems)
    hidden = own_ref[...].astype(F32)
    for mask in range(n_heads):
        weight = placed[where_ref[mask]].reshape(width, cols)
        hidden += dot(piece_refs[mask][...].T, weight, NT)
    for head in range(n_heads):
        w_ref[head] = placed[head].reshape(width, cols)
    hidden_ref[...] = hidden
    normed_ref[...] = (hidden * inverse_root(hidden) * gain_ref[1:2, :]).astype(LOW)
    for part, half_ref in enumerate(half_refs):
        rows = half_ref.shape[0]
        half_ref[...] = normed_ref[part * rows : (part + 1) * rows, :]


def ordered_join_kernel(n_heads, where_ref, *refs):
    piece_refs, refs = refs[:n_heads], refs[n_heads:]
    (own_ref, gain_ref, w_ref, hidden_ref, normed_ref), half_refs = refs[:5], refs[5:]
    hidden = own_ref[...].astype(F32)
    for mask in range(n_heads):
        hidden += dot(piece_refs[mask][...].T, w_ref[where_ref[mask]], NT)
    hidden_ref[...] = hidden
    normed_ref[...] = (hidden * inverse_root(hidden) * gain_ref[1:2, :]).astype(LOW)
    for part, half_ref in enumerate(half_refs):
        rows = half_ref.shape[0]
        half_ref[...] = normed_ref[part * rows : (part + 1) * rows, :]


def join_heads(where, n_seq, pieces, own_rows, gains, gathered, deps=()):
    n_heads, cols = len(pieces), pieces[0].shape[0]
    tok_rows, width = own_rows.shape
    rows = gathered.shape[0] // (n_seq * n_heads)
    flats = width // (2 * n_seq * rows)
    vmem = pl.BlockSpec(memory_space=pltpu.VMEM)
    smem = pl.BlockSpec(memory_space=pltpu.SMEM)
    params = pltpu.CompilerParams(vmem_limit_bytes=VMEM_LIMIT)
    outs = [
        jax.ShapeDtypeStruct((tok_rows, width), F32),
        jax.ShapeDtypeStruct((tok_rows, width), LOW),
    ] + [jax.ShapeDtypeStruct((tok_rows // 2, width), LOW)] * 2
    if cols % 128 == 0:
        return ordered_call(
            deps,
            functools.partial(join_kernel, n_heads, n_seq),
            in_specs=[smem]
            + [vmem] * (n_heads + 2)
            + [pl.BlockSpec(memory_space=pl.ANY)],
            out_specs=[vmem] * 5,
            out_shape=[jax.ShapeDtypeStruct((n_heads, width, cols), LOW)] + outs,
            scratch_shapes=[
                pltpu.VMEM((n_heads, n_seq, 2, flats, rows, cols), LOW),
                pltpu.SemaphoreType.DMA((n_seq * n_heads * 2 * flats,)),
            ],
            compiler_params=params,
        )(where, *pieces, own_rows, gains, gathered)
    out_w = gathered[:, -2 * flats * cols :].reshape(n_seq, n_heads, rows, 2, flats, cols)
    out_w = jnp.where(where[n_heads + n_seq] == 0, out_w, out_w[:, :, :, ::-1])
    out_w = jnp.transpose(out_w, (1, 0, 3, 4, 2, 5)).reshape(n_heads, width, cols)
    joined = ordered_call(
        deps,
        functools.partial(ordered_join_kernel, n_heads),
        in_specs=[smem] + [vmem] * (n_heads + 3),
        out_specs=[vmem] * 4,
        out_shape=outs,
        compiler_params=params,
    )(where, *pieces, own_rows, gains, out_w)
    return (out_w, *joined)


def part_kernel(n_heads, groups, where_ref, *refs):
    own_ref, arrived_refs, refs = refs[0], refs[1:3], refs[3:]
    hidden_ref, cot_ref, gain_ref, w_ref, grad_ref, gain_grad_ref = refs[:6]
    low_ref, piece_refs = refs[6], refs[7:]
    hidden = hidden_ref[...]
    inverse = inverse_root(hidden)
    arrived = jnp.concatenate([ref[...] for ref in arrived_refs], axis=0)
    grad_two = own_ref[...].astype(F32) + arrived.astype(F32)
    scaled = gain_ref[1:2, :] * grad_two
    inner = jnp.mean(scaled * hidden, axis=-1, keepdims=True)
    grad = cot_ref[...].astype(F32) + inverse * scaled - hidden * (inverse**3 * inner)
    gain_grad_ref[...] = jnp.sum(grad_two * hidden * inverse, axis=0, keepdims=True)
    grad_ref[...] = grad
    low = grad.astype(LOW)
    low_ref[...] = low
    rows = piece_refs[0].shape[0]
    for mask in range(n_heads):
        piece = dot(low, w_ref[where_ref[mask]], NN).astype(LOW).T
        for at in range(groups):
            piece_refs[mask * groups + at][...] = piece[at * rows : (at + 1) * rows]


def part_heads(where, groups, back_own, back_arrived, hidden, cotangent, gains, out_w, deps=()):
    n_heads = out_w.shape[0]
    tok_rows, width = hidden.shape
    cols = out_w.shape[-1]
    vmem = pl.BlockSpec(memory_space=pltpu.VMEM)
    result = ordered_call(
        deps,
        functools.partial(part_kernel, n_heads, groups),
        in_specs=[pl.BlockSpec(memory_space=pltpu.SMEM)] + [vmem] * 7,
        out_specs=[vmem] * (3 + n_heads * groups),
        out_shape=[
            jax.ShapeDtypeStruct((tok_rows, width), F32),
            jax.ShapeDtypeStruct((1, width), F32),
            jax.ShapeDtypeStruct((tok_rows, width), LOW),
        ]
        + [jax.ShapeDtypeStruct((cols // groups, tok_rows), LOW)] * (n_heads * groups),
        compiler_params=pltpu.CompilerParams(vmem_limit_bytes=VMEM_LIMIT),
    )(where, back_own, *back_arrived, hidden, cotangent, gains, out_w)
    flat = result[3:]
    pieces = [flat[mask * groups : (mask + 1) * groups] for mask in range(n_heads)]
    return result[:3] + [pieces] if isinstance(result, list) else tuple(result[:3]) + (pieces,)


def out_grad_kernel(low_ref, *refs):
    piece_refs, (mine_ref, send_ref) = refs[:-2], refs[-2:]
    turned = low_ref[...].T
    n_seq, n_hid, shares, rows, cols = mine_ref.shape
    for mask in range(2 * shares):
        product = dot(turned, piece_refs[mask][...], NT).astype(LOW).reshape(n_seq, n_hid, rows, cols)
        (send_ref if mask % 2 else mine_ref)[:, :, mask // 2] = product


def out_gradient(low, pieces, n_seq, n_hid, deps=()):
    shares, cols = len(pieces) // 2, pieces[0].shape[0]
    width = low.shape[1]
    vmem = pl.BlockSpec(memory_space=pltpu.VMEM)
    shape = (n_seq, n_hid, shares, width // (n_seq * n_hid), cols)
    return ordered_call(
        deps,
        out_grad_kernel,
        in_specs=[vmem] * (1 + len(pieces)),
        out_specs=[vmem, vmem],
        out_shape=[jax.ShapeDtypeStruct(shape, LOW)] * 2,
        compiler_params=pltpu.CompilerParams(vmem_limit_bytes=VMEM_LIMIT),
    )(low, *pieces)


def ffn_chunks(width):
    return [slice(begin, min(begin + 512, width)) for begin in range(0, width, 512)]


def ffn_kernel(n_heads, n_seq, where_ref, x_ref, c_ref, near_ref, far_ref, gathered_ref, *refs):
    part_ref, back_ref, units_ref, gate_all, up_w, down_w, sems = refs
    act_ref, dgate_ref, dup_ref = (units_ref.at[kind] for kind in range(3))
    units = units_ref.shape[2]
    copies = [
        pltpu.make_async_copy(gathered_ref.at[:, pl.ds(0, units)], up_w, sems.at[0]),
        pltpu.make_async_copy(gathered_ref.at[:, pl.ds(units, units)], down_w, sems.at[1]),
    ]
    for at in range(n_seq):
        seq_slot = where_ref[n_heads + at]
        for mask in range(n_heads):
            copies.append(
                pltpu.make_async_copy(
                    (far_ref if mask % 2 else near_ref).at[mask // 2, at],
                    gate_all.at[seq_slot, where_ref[mask]],
                    sems.at[len(copies)],
                )
            )
    for copy in copies:
        copy.start()
    rows, model_width = x_ref.shape
    x, c = x_ref[...], c_ref[...]
    for copy in copies:
        copy.wait()
    chunks = ffn_chunks(units)
    for cols in chunks:
        gate = dot(x, gate_all[..., cols].reshape(model_width, -1), NN)
        up = dot(x, up_w[:, cols], NN)
        grad = dot(c, down_w[:, cols], NN)
        sigmoid = jax.nn.sigmoid(gate)
        silu = gate * sigmoid
        act_ref[:, cols] = (silu * up).astype(LOW)
        dgate_ref[:, cols] = (grad * up * (sigmoid + silu * (1.0 - sigmoid))).astype(LOW)
        dup_ref[:, cols] = (grad * silu).astype(LOW)
    per_seq = model_width // n_seq
    for at in range(n_seq):
        here = slice(at * per_seq, (at + 1) * per_seq)
        gate_w = gate_all[at].reshape(per_seq, units)
        back = dot(dgate_ref[...], gate_w, NT) + dot(dup_ref[...], up_w[here, :], NT)
        back_ref[:, here] = back.astype(LOW)
        part_ref[:, here] = dot(act_ref[...], down_w[here, :], NT).astype(LOW)


def feed_forward(where, normed, cotangent, part, gate_groups, gathered, deps=()):
    rows, width = normed.shape
    shares, n_seq, piece_rows, units = gate_groups[0].shape
    anywhere = pl.BlockSpec(memory_space=pl.ANY)
    vmem = pl.BlockSpec(memory_space=pltpu.VMEM)
    wide = jax.ShapeDtypeStruct((rows, width), LOW)
    narrow = jax.ShapeDtypeStruct((3, rows, units), LOW)
    return ordered_call(
        deps,
        functools.partial(ffn_kernel, 2 * shares, n_seq),
        grid=(1,),
        in_specs=[
            pl.BlockSpec(memory_space=pltpu.SMEM),
            vmem,
            pl.BlockSpec((rows, width), lambda at: (part, 0)),
        ]
        + [anywhere] * 3,
        out_specs=[vmem] * 3,
        out_shape=[wide, wide, narrow],
        scratch_shapes=[
            pltpu.VMEM((n_seq, 2 * shares, piece_rows, units), LOW),
            pltpu.VMEM((width, units), LOW),
            pltpu.VMEM((width, units), LOW),
            pltpu.SemaphoreType.DMA((2 * shares * n_seq + 2,)),
        ],
        compiler_params=pltpu.CompilerParams(vmem_limit_bytes=VMEM_LIMIT),
    )(where, normed, cotangent, *gate_groups, gathered)


def ffn_grad_kernel(n_heads, runs, *refs):
    left_refs, unit_refs, out_ref = (refs[:2], refs[2 : 2 + runs]), refs[2 + runs : -1], refs[-1]
    size = out_ref.shape[3]
    turned = [jnp.concatenate([left[...].T for left in lefts], axis=1) for lefts in left_refs]
    for kind in range(3):
        left = turned[min(kind, 1)]
        for cols in ffn_chunks(out_ref.shape[4]):
            both, begin = None, 0
            for units in unit_refs:
                rows = units.shape[1]
                term = dot(left[:, begin : begin + rows], units[kind, :, cols], NN)
                both, begin = term if both is None else both + term, begin + rows
            both = both.astype(LOW)
            for at in range(n_heads):
                out_ref[0, at, kind, :, cols] = both[at * size : (at + 1) * size]


def ffn_gradients(n_heads, n_seq, back_rows, normed_rows, units, deps=()):
    width, n_units = normed_rows[0].shape[1], units[0].shape[2]
    tile = width // n_seq
    lefts = [
        pl.BlockSpec((rows.shape[0], tile), lambda at: (0, at)) for rows in (*back_rows, *normed_rows)
    ]
    rights = [pl.BlockSpec(run.shape, lambda at: (0, 0, 0)) for run in units]
    shape = (n_heads, 3, tile // n_heads, n_units)
    return ordered_call(
        deps,
        functools.partial(ffn_grad_kernel, n_heads, len(normed_rows)),
        grid=(n_seq,),
        in_specs=lefts + rights,
        out_specs=pl.BlockSpec((1,) + shape, lambda at: (at, 0, 0, 0, 0)),
        out_shape=jax.ShapeDtypeStruct((n_seq,) + shape, LOW),
        compiler_params=pltpu.CompilerParams(vmem_limit_bytes=VMEM_LIMIT),
    )(*back_rows, *normed_rows, *units)


def by_side(side, first, second):
    return (jnp.where(side == 0, first, second), jnp.where(side == 0, second, first))


def add_halves_kernel(side_at, where_ref, mine_ref, arrived_ref, keep_ref, send_ref):
    side = where_ref[side_at]
    for lead in range(mine_ref.shape[0]):
        for pair in range(mine_ref.shape[1]):
            first, second = (
                (
                    mine_ref[lead, pair, half].astype(F32) + arrived_ref[lead, pair, half].astype(F32)
                ).astype(LOW)
                for half in range(2)
            )
            keep_ref[lead, pair], send_ref[lead, pair] = by_side(side, first, second)


def add_halves(where, side_at, mine, arrived, deps=()):
    lead, pairs, _, rows, cols = mine.shape
    vmem = pl.BlockSpec(memory_space=pltpu.VMEM)
    return ordered_call(
        deps,
        functools.partial(add_halves_kernel, side_at),
        in_specs=[pl.BlockSpec(memory_space=pltpu.SMEM), vmem, vmem],
        out_specs=[vmem, vmem],
        out_shape=[jax.ShapeDtypeStruct((lead, pairs, rows, cols), LOW)] * 2,
        compiler_params=pltpu.CompilerParams(vmem_limit_bytes=VMEM_LIMIT),
    )(where, mine, arrived)


def add_split_kernel(count, first_slot, where_ref, *refs):
    pairs, out_refs = refs[: 2 * count], refs[2 * count :]
    for step, out_ref in enumerate(out_refs):
        at = where_ref[first_slot + step]
        begin = 0
        for mine_ref, arrived_ref in zip(pairs[::2], pairs[1::2]):
            for part in range(mine_ref.shape[1]):
                cols = mine_ref.shape[3]
                both = mine_ref[at, part].astype(F32) + arrived_ref[at, part].astype(F32)
                out_ref[:, begin : begin + cols] = both.astype(LOW)
                begin += cols


def add_split(where, first_slot, *pairs, deps=()):
    vmem = pl.BlockSpec(memory_space=pltpu.VMEM)
    steps, _, rows, _ = pairs[0][0].shape
    width = sum(mine.shape[1] * mine.shape[3] for mine, _ in pairs)
    return ordered_call(
        deps,
        functools.partial(add_split_kernel, len(pairs), first_slot),
        in_specs=[pl.BlockSpec(memory_space=pltpu.SMEM)] + [vmem] * (2 * len(pairs)),
        out_specs=[vmem] * steps,
        out_shape=[jax.ShapeDtypeStruct((rows, width), LOW)] * steps,
        compiler_params=pltpu.CompilerParams(vmem_limit_bytes=VMEM_LIMIT),
    )(where, *[half for pair in pairs for half in pair])


def one_grad_kernel(n_heads, groups, where_ref, *refs):
    grad_refs, w_ref, mine_ref, send_refs = refs[:groups], refs[groups], refs[groups + 1], refs[groups + 2 :]
    size = grad_refs[0].shape[2] // n_heads
    half = size // 2
    for mask in range(n_heads - 1, -1, -1):
        cols = pl.ds(pl.multiple_of(where_ref[mask] * size, size), size)
        grads = jnp.concatenate(
            [grad_refs[at][kind, :, cols] for kind in range(3) for at in range(groups)], axis=0
        )
        product = dot(grads, w_ref[...], TN).astype(LOW)
        if mask % 2:
            send_refs[mask - 1][...], send_refs[mask][...] = product[:half], product[half:]
        else:
            mine_ref[mask // 2] = product


def one_gradient(where, n_heads, grads, in_w, deps=()):
    groups = len(grads)
    length, width = grads[0].shape[2], in_w.shape[1]
    vmem = pl.BlockSpec(memory_space=pltpu.VMEM)
    size = length // n_heads
    result = ordered_call(
        deps,
        functools.partial(one_grad_kernel, n_heads, groups),
        in_specs=[pl.BlockSpec(memory_space=pltpu.SMEM)] + [vmem] * (groups + 1),
        out_specs=[vmem] * (1 + n_heads),
        out_shape=[jax.ShapeDtypeStruct((n_heads // 2, size, width), LOW)]
        + [jax.ShapeDtypeStruct((size // 2, width), LOW)] * n_heads,
        compiler_params=pltpu.CompilerParams(vmem_limit_bytes=VMEM_LIMIT),
    )(where, *grads, in_w)
    return (result[0], list(result[1:]))


def near_sum_kernel(shares, mine_ref, *refs):
    moved_refs, out_refs = refs[: 2 * shares], refs[2 * shares :]
    half = moved_refs[0].shape[0]
    for at in range(shares):
        for part in range(2):
            here = slice(part * half, (part + 1) * half)
            both = mine_ref[at, here].astype(F32) + moved_refs[2 * at + part][...].astype(F32)
            out_refs[at][here] = both.astype(LOW)


def near_sum(mine, moved, deps=()):
    shares, rows, width = mine.shape
    vmem = pl.BlockSpec(memory_space=pltpu.VMEM)
    return ordered_call(
        deps,
        functools.partial(near_sum_kernel, shares),
        in_specs=[vmem] * (1 + len(moved)),
        out_specs=[vmem] * shares,
        out_shape=[jax.ShapeDtypeStruct((rows, width), LOW)] * shares,
        compiler_params=pltpu.CompilerParams(vmem_limit_bytes=VMEM_LIMIT),
    )(mine, *moved)


def in_grad_kernel(side_at, where_ref, rows_ref, *refs):
    grad_refs, (mine_ref, send_ref) = refs[:-2], refs[-2:]
    n_seq, rows, _ = mine_ref.shape
    side = where_ref[side_at]
    for at, grad_ref in enumerate(grad_refs):
        kinds, cols, length = grad_ref.shape
        grads = grad_ref[...].reshape(kinds * cols, length)
        product = dot(grads, rows_ref[...], NN).astype(LOW).T.reshape(n_seq, 2, rows, kinds * cols)
        here = slice(at * kinds * cols, (at + 1) * kinds * cols)
        mine_ref[:, :, here], send_ref[:, :, here] = by_side(side, product[:, 0], product[:, 1])


def in_gradient(where, side_at, n_seq, group_rows, grads, deps=()):
    groups = len(grads)
    length, width = group_rows.shape
    cols = grads[0].shape[1]
    vmem = pl.BlockSpec(memory_space=pltpu.VMEM)
    shape = (n_seq, width // (2 * n_seq), 3 * cols * groups)
    return ordered_call(
        deps,
        functools.partial(in_grad_kernel, side_at),
        in_specs=[pl.BlockSpec(memory_space=pltpu.SMEM)] + [vmem] * (1 + groups),
        out_specs=[vmem, vmem],
        out_shape=[jax.ShapeDtypeStruct(shape, LOW)] * 2,
        compiler_params=pltpu.CompilerParams(vmem_limit_bytes=VMEM_LIMIT),
    )(where, group_rows, *grads)


def swap(value, axis, mask):
    return lax.ppermute(value, axis, [(i, i ^ mask) for i in range(lax.axis_size(axis))])


def shift(value, axis, step):
    size = lax.axis_size(axis)
    return lax.ppermute(value, axis, [(i, (i + step) % size) for i in range(size)])


def bits_from_high(size):
    bit = size // 2
    while bit:
        yield bit
        bit //= 2


def gather_masks(value, axis, bits):
    held = {0: value}
    for bit in bits:
        held.update({mask ^ bit: swap(block, axis, bit) for mask, block in list(held.items())})
    return held


def from_all(value, axis):
    return [value] + [shift(value, axis, step) for step in range(1, lax.axis_size(axis))]


def total(value, axis):
    size = lax.axis_size(axis)
    bit = 1
    while bit < size:
        if bit * 4 <= size:
            one, two, three = (swap(value, axis, mask * bit) for mask in (1, 2, 3))
            value = (value + one) + (two + three)
            bit *= 4
        else:
            value = value + swap(value, axis, bit)
            bit *= 2
    return value


def tie(*values):
    return lax.optimization_barrier(values)


def send_blocks(blocks, name):
    return [blocks[0]] + [shift(block, name, step) for step, block in enumerate(blocks) if step]


def add_up(blocks):
    result = blocks[0].astype(F32)
    for block in blocks[1:]:
        result = result + block.astype(F32)
    return result


def fold_masks(blocks, bits):
    sums = dict(blocks)
    for bit in bits:
        for mask in sorted(sums, reverse=True):
            if mask & bit:
                moved = swap(sums.pop(mask), "heads", bit)
                if bit == bits[-1]:
                    return (sums[0], moved)
                sums[mask ^ bit] = (sums[mask ^ bit].astype(F32) + moved.astype(F32)).astype(LOW)


def rows_by_default(value):
    return with_layout_constraint(value, Layout(tuple(range(value.ndim))))


def adam_moments(mean_old, var_old, grad):
    mean_new = BETA_ONE * mean_old + (1.0 - BETA_ONE) * grad
    var_new = BETA_TWO * var_old + (1.0 - BETA_TWO) * grad * grad
    direction = (
        mean_new / (1.0 - BETA_ONE**STEP) / (jnp.sqrt(var_new / (1.0 - BETA_TWO**STEP)) + ADAM_EPS)
    )
    return (mean_new, var_new, direction)


def lane_row(values):
    lanes = lax.broadcasted_iota(jnp.int32, (1, ROW), 1)
    row = jnp.zeros((1, ROW), F32)
    for lane, value in values.items():
        row = jnp.where(lanes == lane, value, row)
    return row


def total_of(value):
    return jnp.sum(jnp.sum(value, axis=1, keepdims=True), axis=0, keepdims=True)


def step_part(weight, mean_old, var_old, grad):
    mean_new, var_new, direction = adam_moments(mean_old, var_old, grad)
    update = direction + DECAY * weight
    return (mean_new, var_new, update, total_of(weight * weight), total_of(update * update))


def sum_blocks(refs, rows, cols):
    result = refs[0][rows, cols].astype(F32)
    for ref in refs[1:]:
        result = result + ref[rows, cols].astype(F32)
    return result


def in_step_kernel(n_blocks, groups, *refs):
    block_refs, (w_ref, m_ref, v_ref) = refs[:n_blocks], refs[n_blocks : n_blocks + 3]
    mean_ref, var_ref, update_ref, row_ref = refs[n_blocks + 3 :]
    size = w_ref.shape[2] // groups
    values = {}
    for kind in range(w_ref.shape[0]):
        for at in range(groups):
            here = (kind, slice(None), slice(at * size, (at + 1) * size))
            begin = (at * w_ref.shape[0] + kind) * size
            grad = sum_blocks(block_refs, slice(None), slice(begin, begin + size))
            mean, var, update, weight_sq, update_sq = step_part(
                w_ref[here], m_ref[here], v_ref[here], grad
            )
            mean_ref[here], var_ref[here], update_ref[here] = mean, var, update
            values[kind] = weight_sq + values[kind] if at else weight_sq
            values[MATRICES + kind] = update_sq + values[MATRICES + kind] if at else update_sq
    row_ref[...] = lane_row(values)


def ffn_step_kernel(*refs):
    grad_ref, gu_refs, down_refs, out_refs = refs[0], refs[1:4], refs[4:7], refs[7:]
    row_ref = out_refs[6]
    rows = down_refs[0].shape[0]
    values = {}
    for kind in range(3):
        begin = (kind + 1) % 3 * rows
        grad = grad_ref[begin : begin + rows, :].astype(F32)
        here = (kind,) if kind < 2 else (slice(None),)
        ins, outs = (gu_refs, out_refs[:3]) if kind < 2 else (down_refs, out_refs[3:6])
        results = step_part(*[ref[here] for ref in ins], grad)
        for ref, result in zip(outs, results[:3]):
            ref[here] = result
        values[4 + kind], values[MATRICES + 4 + kind] = results[3:]
    row_ref[...] = lane_row(values)


def out_step_kernel(own_ref, arrived_ref, w_ref, m_ref, v_ref, mean_ref, var_ref, update_ref, row_ref):
    grad = (own_ref[...].astype(F32) + arrived_ref[...].astype(F32)).T
    mean, var, update, weight_sq, update_sq = step_part(w_ref[...], m_ref[...], v_ref[...], grad)
    mean_ref[...], var_ref[...], update_ref[...] = mean, var, update
    row_ref[...] = lane_row({3: weight_sq, MATRICES + 3: update_sq})


def step_call(kernel, arrays, like, deps=()):
    vmem = pl.BlockSpec(memory_space=pltpu.VMEM)
    shapes = [jax.ShapeDtypeStruct(array.shape, F32) for array in like for _ in range(3)]
    return ordered_call(
        deps,
        kernel,
        in_specs=[vmem] * len(arrays),
        out_specs=[vmem] * (len(shapes) + 1),
        out_shape=shapes + [jax.ShapeDtypeStruct((1, ROW), F32)],
        compiler_params=pltpu.CompilerParams(vmem_limit_bytes=VMEM_LIMIT),
    )(*arrays)


def last_step_kernel(*refs):
    sums_ref, gain_refs, refs = refs[0], refs[1:4], refs[4:]
    weight_refs, update_refs, gain_outs, new_refs = refs[:4], refs[4:8], refs[8:11], refs[11:]
    sums = sums_ref[2:3, :]
    lanes = lax.broadcasted_iota(jnp.int32, sums.shape, 1)

    def lane(at):
        return total_of(jnp.where(lanes == at, sums, 0.0))

    mean_new, var_new, direction = adam_moments(gain_refs[1][...], gain_refs[2][...], sums_ref[0:2, :])
    gain_outs[0][...] = gain_refs[0][...] - GAIN_RATE * direction
    gain_outs[1][...], gain_outs[2][...] = mean_new, var_new
    at = 0
    for weight_ref, update_ref, new_ref in zip(weight_refs, update_refs, new_refs):
        parts = [(kind,) for kind in range(weight_ref.shape[0])]
        for here in parts if len(weight_ref.shape) == 3 else [(slice(None),)]:
            ratio = jnp.sqrt(lane(at)) / jnp.sqrt(lane(MATRICES + at) + 1e-12)
            new_ref[here] = weight_ref[here] - MATRIX_RATE * ratio * update_ref[here]
            at += 1


def last_step(sums, gains, weights, updates):
    vmem = pl.BlockSpec(memory_space=pltpu.VMEM)
    arrays = [sums, *gains, *weights, *updates]
    outs = [jax.ShapeDtypeStruct(array.shape, F32) for array in (*gains, *weights)]
    return ordered_call(
        (),
        last_step_kernel,
        in_specs=[vmem] * len(arrays),
        out_specs=[vmem] * len(outs),
        out_shape=outs,
        compiler_params=pltpu.CompilerParams(vmem_limit_bytes=VMEM_LIMIT),
    )(*arrays)


def input_grad_kernel(own_ref, arrived_ref, tokens_ref, gain_ref, grad_ref, out_ref, gain_grad_ref):
    rows = tokens_ref[...].astype(F32)
    inverse = inverse_root(rows)
    grad_one = own_ref[...].astype(F32) + arrived_ref[...].astype(F32)
    scaled = gain_ref[0:1, :] * grad_one
    inner = jnp.mean(scaled * rows, axis=-1, keepdims=True)
    out_ref[...] = grad_ref[...] + inverse * scaled - rows * (inverse**3 * inner)
    gain_grad_ref[...] = jnp.sum(grad_one * rows * inverse, axis=0, keepdims=True)


def input_gradient(own, arrived, tokens, gains, grad_hidden):
    rows, width = tokens.shape
    vmem = pl.BlockSpec(memory_space=pltpu.VMEM)
    return ordered_call(
        (),
        input_grad_kernel,
        in_specs=[vmem] * 5,
        out_specs=[vmem] * 2,
        out_shape=[
            jax.ShapeDtypeStruct((rows, width), F32),
            jax.ShapeDtypeStruct((1, width), F32),
        ],
        compiler_params=pltpu.CompilerParams(vmem_limit_bytes=VMEM_LIMIT),
    )(own, arrived, tokens, gains, grad_hidden)


def rope_tables(position_ids):
    half_dim = HDIM // 2
    freqs = ROPE_BASE ** (-(jnp.arange(half_dim, dtype=jnp.float32) * 2.0 / HDIM))
    angles = freqs[:, None] * position_ids.astype(jnp.float32)[None, :]
    return (jnp.cos(angles), jnp.sin(angles))


def per_device(
    tokens_in,
    first_value,
    cotangent,
    counts,
    segments,
    positions,
    norm_gains,
    gain_mean,
    gain_var,
    heads_in,
    heads_in_mean,
    heads_in_var,
    heads_out,
    heads_out_mean,
    heads_out_var,
    gate_up,
    gate_up_mean,
    gate_up_var,
    down_proj,
    down_mean,
    down_var,
):
    n_seq, n_heads, n_hid = (lax.axis_size(name) for name in ("seq", "heads", "hid"))
    at_seq, at_heads, at_hid = (lax.axis_index(name) for name in ("seq", "heads", "hid"))
    own_rows = tokens_in[0].astype(F32)
    tok_rows, model_width = own_rows.shape
    length = tok_rows * n_heads
    head_cols = heads_in.shape[2]
    hidden_cols = gate_up.shape[2]
    near = 1
    far_bits = [bit for bit in bits_from_high(n_heads) if bit > near]
    masks = list(range(n_heads))
    groups = 1
    seq_slots = [lax.rem(at_seq + n_seq - step, n_seq) for step in range(n_seq)]
    where = jnp.stack(
        [at_heads ^ mask for mask in masks]
        + seq_slots
        + [at_hid, at_hid ^ 1]
        + [lax.rem(at_seq + step, n_seq) for step in range(n_seq)]
        + [lax.rem(at_heads // bit, 2) for bit in [near] + far_bits[::-1]]
    ).astype(jnp.int32)
    hid_side = n_heads + n_seq
    seq_steps = hid_side + 2
    heads_sides = seq_steps + n_seq

    head_low, own_rows = tie(
        jnp.concatenate(
            [jnp.swapaxes(heads_in, 0, 1).reshape(-1, 3 * head_cols), heads_out.T], axis=1
        ).astype(LOW),
        own_rows,
    )
    in_low, out_low = head_low[:, : 3 * head_cols], head_low[:, 3 * head_cols :]
    half = in_low.shape[0] // 2
    upper_pieces = from_all(in_low[:half], "seq")
    piece_rows = gate_up.shape[1]
    flats = out_low.shape[0] // piece_rows

    def flat(rows):
        return jnp.moveaxis(rows.reshape(flats, piece_rows, head_cols), 0, 1).reshape(piece_rows, -1)

    lower_sent = jnp.concatenate([in_low[half:], out_low[:half], out_low[half:]], axis=1)
    lower_moved = swap(lower_sent, "hid", 1)

    inv_one = inverse_root(own_rows)
    normed_one = (own_rows * inv_one * norm_gains[0]).astype(LOW)
    far_blocks = gather_masks(normed_one, "heads", far_bits)
    lower_moved, far_blocks[0] = tie(lower_moved, far_blocks[0])
    out_moved = jnp.concatenate(
        [lower_moved[:, 3 * head_cols : 4 * head_cols], lower_moved[:, 4 * head_cols :]], axis=0
    )

    gathered = lax.all_gather(
        jnp.concatenate(
            [gate_up[1].astype(LOW), down_proj.T.astype(LOW), flat(out_low), flat(out_moved)],
            axis=1,
        ),
        ("seq", "heads"),
        axis=0,
        tiled=True,
    )

    upper_pieces, lower_pair = tie(
        upper_pieces, jnp.stack([in_low[half:], lower_moved[:, : 3 * head_cols]])
    )
    upper, lower_pair = tie(jnp.stack(upper_pieces), lower_pair)
    upper_moved = swap(upper, "hid", 1)
    lower_pieces = from_all(lower_pair, "seq")
    cosine, sine_table = rope_tables(positions[0])
    row_ids = jnp.arange(length, dtype=jnp.int32)
    is_valid = row_ids % tok_rows < jnp.repeat(counts[0], tok_rows, total_repeat_length=length)
    segs = (segments, jnp.where(is_valid[None], segments, -1))
    far_blocks, lower_pieces, upper_moved, gate_low, cosine, sine_table, segs = tie(
        far_blocks,
        lower_pieces,
        upper_moved,
        gate_up[0].astype(LOW),
        cosine,
        sine_table,
        segs,
    )
    gate_pieces = from_all(gate_low, "seq")
    near_rows = jnp.stack([far_blocks[mask] for mask in masks[::2]])
    far_rows = swap(near_rows, "heads", near)
    lower = jnp.stack(lower_pieces)

    group_rows, in_w, queries, keys_rot, values = project(
        where,
        near_rows,
        far_rows,
        upper,
        upper_moved,
        lower,
        first_value[0],
        cosine,
        sine_table,
    )
    group_rows = group_rows.reshape(length, model_width)
    cot_low, queries = tie(cotangent[0], queries)
    back_other = swap(cot_low, "hid", 1)

    mixed, sends, lse = attention_forward(
        where, n_heads, queries, keys_rot, values, *segs
    )
    back_other, sends = tie(back_other, sends)
    arrived = [swap(sends[mask], "heads", mask) if mask else sends[mask] for mask in masks]
    gate_pieces, arrived = tie(gate_pieces, arrived)
    gate_stack = jnp.stack(gate_pieces)
    gate_blocks = gather_masks(gate_stack, "heads", far_bits)
    out_w, hidden, normed_two, *normed_halves = join_heads(
        where, n_seq, arrived, tokens_in[0], norm_gains, gathered, deps=gate_stack
    )
    gate_blocks, normed_two = tie(gate_blocks, normed_two)
    gate_near = jnp.stack([gate_blocks[mask] for mask in masks[::2]])
    gate_far = swap(gate_near, "heads", near)
    normed_other = [swap(half, "hid", 1) for half in normed_halves]
    weights = ((gate_near, gate_far), gathered)

    ffn_own, back_own, units_own = feed_forward(where, normed_two, cotangent[0], 0, *weights)
    units, ffn_far, back_arrived = [units_own], [], []
    deps = back_own
    for part in range(2):
        ffn_part, back_part, units_part = feed_forward(
            where, normed_other[part], back_other, part, *weights, deps=deps
        )
        deps = back_part
        units.append(units_part)
        ffn_far.append(ffn_part)
        back_arrived.append(swap(back_part, "hid", 1))

    made = ffn_gradients(
        n_heads,
        n_seq,
        (cotangent[0], back_other),
        (normed_two, *normed_other),
        units,
        deps=(deps, back_arrived[0]),
    )
    made, back_arrived[1] = tie(made, back_arrived[1])
    ffn_grads = lax.psum_scatter(
        made.reshape(-1, hidden_cols), ("seq", "heads"), scatter_dimension=0, tiled=True
    )

    grad_hidden, gain_grad_two, grad_hidden_low, grad_pieces = part_heads(
        where,
        groups,
        back_own,
        back_arrived,
        hidden,
        cotangent[0],
        norm_gains,
        out_w,
    )
    ffn_far, grad_hidden_low = tie(ffn_far, grad_hidden_low)
    grad_arrived = [grad_pieces[0][0]] + [
        swap(grad_pieces[mask][0], "heads", mask) for mask in masks[1:]
    ]
    out_mine, out_sent = out_gradient(grad_hidden_low, arrived, n_seq, n_hid)
    out_half = swap(out_sent, "heads", near)
    out_mine, out_sent = add_halves(
        where,
        hid_side,
        out_mine.reshape(n_seq, 1, 2, -1, head_cols),
        out_half.reshape(n_seq, 1, 2, -1, head_cols),
    )
    out_half = swap(out_sent, "hid", 1)
    grad_arrived, ffn_far = tie(grad_arrived, jnp.concatenate(ffn_far, axis=0))
    ffn_arrived = swap(ffn_far, "hid", 1)
    grads, first_grad = attention_backward(
        where,
        0,
        grad_arrived,
        queries,
        keys_rot,
        values,
        mixed,
        lse,
        segs,
        cosine,
        sine_table,
        deps=out_sent,
    )
    grads = [grads]
    in_mine, in_sent = in_gradient(where, hid_side, n_seq, group_rows, grads)
    in_sent, ffn_arrived = tie(in_sent, ffn_arrived)
    in_half = swap(in_sent, "hid", 1)
    one_mine, one_sent = one_gradient(where, n_heads, grads, in_w, deps=in_sent)
    one_moved = [swap(part, "heads", near) for part in one_sent]
    shares_shape = (n_seq, n_heads // 2, -1, head_cols)
    out_blocks = add_split(
        where,
        seq_steps,
        (out_mine.reshape(shares_shape), out_half.reshape(shares_shape)),
        deps=one_sent[0],
    )
    one_moved, out_blocks = tie(one_moved, out_blocks)
    near_sums, out_blocks = tie(near_sum(one_mine, one_moved), out_blocks)
    out_blocks = send_blocks(out_blocks, "seq")
    one_own, one_arrived = fold_masks({mask: near_sums[mask // 2] for mask in masks[::2]}, far_bits)
    in_blocks = add_split(
        where, seq_steps, (in_mine[:, None], in_half[:, None]), deps=out_blocks[0]
    )
    out_blocks, in_blocks = tie(out_blocks, in_blocks)
    in_blocks = send_blocks(in_blocks, "seq")

    gu = (gate_up, gate_up_mean, gate_up_var)
    dn = [array.T for array in (down_proj, down_mean, down_var)]
    gu_mean, gu_var, gu_update, dn_mean, dn_var, dn_update, ffn_row = step_call(
        ffn_step_kernel,
        [ffn_grads, *gu, *dn],
        (gate_up, dn[0]),
        deps=in_blocks[0],
    )
    out_blocks, out_first = tie(out_blocks, in_blocks[0])
    out_part = add_up(out_blocks).astype(LOW).reshape(-1, n_heads // 2, head_cols)
    out_own, out_arrived = fold_masks({mask: out_part[:, mask // 2] for mask in masks[::2]}, far_bits)
    out_mean, out_var, out_update, out_row = step_call(
        out_step_kernel,
        [out_own, out_arrived, heads_out, heads_out_mean, heads_out_var],
        (heads_out,),
        deps=ffn_row,
    )
    first_grad = first_grad.T[None]
    block_out = (hidden + (ffn_own.astype(F32) + ffn_arrived.astype(F32))).astype(LOW)[None]
    in_blocks, out_row, first_grad, block_out = tie(
        [out_first, *in_blocks[1:]], out_row, first_grad, block_out
    )
    in_mean, in_var, in_update, in_row = step_call(
        functools.partial(in_step_kernel, n_seq, groups),
        [*in_blocks, heads_in, heads_in_mean, heads_in_var],
        (heads_in,),
    )
    input_grad, gain_grad_one = input_gradient(
        one_own, one_arrived, tokens_in[0], norm_gains, grad_hidden
    )
    first_wide, blended_wide = first_value[0].astype(F32), values.astype(F32)
    value_row = lane_row(
        {
            2 * MATRICES: jnp.sum(first_wide * first_wide),
            2 * MATRICES + 1: jnp.sum(blended_wide * blended_wide),
        }
    )
    packed = jnp.concatenate(
        [gain_grad_one, gain_grad_two, ffn_row + out_row + (in_row + value_row)], axis=0
    )
    for axis in ("heads", "seq", "hid"):
        packed = total(packed, axis)
    gains_new, gmean_new, gvar_new, in_new, out_new, gu_new, dn_new = last_step(
        packed,
        (norm_gains, gain_mean, gain_var),
        (heads_in, heads_out, gate_up, dn[0]),
        (in_update, out_update, gu_update, dn_update),
    )
    dn_new, dn_mean, dn_var = (array.T for array in (dn_new, dn_mean, dn_var))
    entries = float(
        length * head_cols * lax.axis_size("seq") * lax.axis_size("heads") * lax.axis_size("hid")
    )
    norms = jnp.sqrt(packed[2, : 2 * MATRICES])
    value_norms = jnp.sqrt(packed[2, 2 * MATRICES : 2 * MATRICES + 2] / entries)
    return (
        block_out,
        input_grad[None],
        first_grad,
        gains_new,
        gmean_new,
        gvar_new,
        in_new,
        in_mean,
        in_var,
        out_new,
        out_mean,
        out_var,
        gu_new,
        gu_mean,
        gu_var,
        dn_new,
        dn_mean,
        dn_var,
        norms,
        value_norms,
    )


def solution(mesh):
    placed = (
        P(("seq", "hid"), "heads", None),
        P(("seq", "hid"), None, "heads"),
        P(("seq", "hid"), "heads", None),
        P(("seq", "hid"), None),
        P(("seq", "hid"), None),
        P(("seq", "hid"), None),
        P(),
        P(),
        P(),
        P(None, ("seq", "hid"), "heads"),
        P(None, ("seq", "hid"), "heads"),
        P(None, ("seq", "hid"), "heads"),
        P("heads", ("seq", "hid")),
        P("heads", ("seq", "hid")),
        P("heads", ("seq", "hid")),
        P(None, ("seq", "heads"), "hid"),
        P(None, ("seq", "heads"), "hid"),
        P(None, ("seq", "heads"), "hid"),
        P("hid", ("seq", "heads")),
        P("hid", ("seq", "heads")),
        P("hid", ("seq", "heads")),
    )
    return jax.shard_map(
        per_device,
        mesh=mesh,
        in_specs=placed,
        out_specs=(
            P(("seq", "hid"), "heads", None),
            P(("seq", "hid"), "heads", None),
            P(("seq", "hid"), None, "heads"),
            P(),
            P(),
            P(),
            P(None, ("seq", "hid"), "heads"),
            P(None, ("seq", "hid"), "heads"),
            P(None, ("seq", "hid"), "heads"),
            P("heads", ("seq", "hid")),
            P("heads", ("seq", "hid")),
            P("heads", ("seq", "hid")),
            P(None, ("seq", "heads"), "hid"),
            P(None, ("seq", "heads"), "hid"),
            P(None, ("seq", "heads"), "hid"),
            P("hid", ("seq", "heads")),
            P("hid", ("seq", "heads")),
            P("hid", ("seq", "heads")),
            P(),
            P(),
        ),
        check_vma=False,
    )
```

```python
import functools

import jax
import jax.numpy as jnp
from jax import lax
from jax.experimental import pallas as pl
from jax.experimental.layout import Layout, with_layout_constraint
from jax.experimental.pallas import tpu as pltpu
from jax.sharding import PartitionSpec as P

HDIM = 64
STEP = 10


NORM_EPS = 1e-05
ROPE_BASE = 10000.0
BLEND = 0.5
BETA_ONE = 0.9
BETA_TWO = 0.999
ADAM_EPS = 1e-06
DECAY = 0.01
MATRIX_RATE = 0.25
GAIN_RATE = 0.7
NEG_LARGE = -1e30

BLOCK = 512
EXTRA = 16
SEGMENTS = 3
MATRICES = 7
ROW = 1024
NN = ((1,), (0,))
NT = ((1,), (1,))
TN = ((0,), (0,))
VMEM_LIMIT = 62 << 20
F32 = jnp.float32
LOW = jnp.bfloat16


def dot(left, right, dims):
    return lax.dot_general(left, right, (dims, ((), ())), preferred_element_type=F32)


def ordered_call(deps, kernel, *, in_specs, **rest):
    extra = jax.tree.leaves(deps)
    count = len(in_specs)

    def body(*refs):
        kernel(*refs[:count], *refs[count + len(extra) :])

    in_specs = in_specs + [pl.BlockSpec(memory_space=pl.ANY)] * len(extra)
    call = pl.pallas_call(body, in_specs=in_specs, **rest)
    return lambda *operands: call(*operands, *extra)


def tile_plan(length, block):
    tiles = []
    half = block // 2
    for begin in range(0, length, block):
        tiles.append((begin, half, begin, half, True))
        tiles.append((begin + half, half, begin, block, True))
        for key_begin in range(0, begin, block):
            tiles.append((begin, block, key_begin, block, False))
    return tiles


def causal(scores, own_scores, query_begin, key_begin):
    rows = lax.broadcasted_iota(jnp.int32, scores.shape, 0) + (key_begin - query_begin)
    cols = lax.broadcasted_iota(jnp.int32, scores.shape, 1)
    return jnp.where(rows < cols, scores, jnp.where(rows == cols, own_scores, NEG_LARGE))


def segment_rows(query_segs, key_segs):
    shape = (EXTRA, query_segs.shape[1])
    row_ids = lax.broadcasted_iota(jnp.int32, shape, 0)
    query_rows = jnp.where(row_ids == query_segs, 1.0, 0.0)
    key_rows = jnp.where((row_ids < SEGMENTS) & (row_ids != key_segs), NEG_LARGE, 0.0)
    return (row_ids, query_rows, key_rows)


def move_all(moves, sems):
    copies = [
        pltpu.make_async_copy(source, target, sems.at[index])
        for index, (source, target) in enumerate(moves)
    ]
    for copy in copies:
        copy.start()
    for copy in copies:
        copy.wait()


def turn(rows, cosine, sine, sign):
    parts = []
    for begin in range(0, rows.shape[0], HDIM):
        middle = begin + HDIM // 2
        first, second = rows[begin:middle], rows[middle : begin + HDIM]
        parts.append(first * cosine - sign * (second * sine))
        parts.append(second * cosine + sign * (first * sine))
    return jnp.concatenate(parts, axis=0)


def project_kernel(n_heads, n_seq, where_ref, *refs):
    near_ref, far_ref, refs = refs[0], refs[1], refs[2:]
    upper_ref, moved_ref, lower_ref, first_ref, cos_ref, sin_ref = refs[:6]
    rows_ref, turned, q_ref, k_ref, v_ref, w_ref, sems = refs[6:]
    half = upper_ref.shape[1]
    upper, lower = pl.ds(0, half), pl.ds(half, half)
    cols = q_ref.shape[0]
    tok_rows, width = near_ref.shape[1:]
    moves = [
        ((far_ref if mask % 2 else near_ref).at[mask // 2], rows_ref.at[where_ref[mask]])
        for mask in range(n_heads)
    ]
    own, other = where_ref[n_heads + n_seq], where_ref[n_heads + n_seq + 1]
    for at in range(n_seq):
        slot = where_ref[n_heads + at]
        moves.append((upper_ref.at[at], w_ref.at[slot, own, upper]))
        moves.append((moved_ref.at[at], w_ref.at[slot, other, upper]))
        moves.append((lower_ref.at[at, 0], w_ref.at[slot, own, lower]))
        moves.append((lower_ref.at[at, 1], w_ref.at[slot, other, lower]))
    move_all(moves, sems)
    turned[...] = w_ref[...].reshape(width, 3 * cols).T
    for at in range(n_heads):
        here = slice(at * tok_rows, (at + 1) * tok_rows)
        projected = dot(turned[...], rows_ref[at], NT)
        cosine, sine = cos_ref[:, here], sin_ref[:, here]
        q_ref[:, here] = (turn(projected[:cols], cosine, sine, 1.0) * HDIM ** (-0.5)).astype(LOW)
        k_ref[:, here] = turn(projected[cols : 2 * cols], cosine, sine, 1.0).astype(LOW)
        first = first_ref[here, :].astype(F32).T
        v_ref[:, here] = (BLEND * projected[2 * cols :] + (1.0 - BLEND) * first).astype(LOW)


def project(where, near_rows, far_rows, upper, upper_moved, lower, first_local, cosine, sine, deps=()):
    n_heads, n_seq = 2 * near_rows.shape[0], upper.shape[0]
    tok_rows, width = near_rows.shape[1:]
    length, cols = first_local.shape
    anywhere = pl.BlockSpec(memory_space=pl.ANY)
    vmem = pl.BlockSpec(memory_space=pltpu.VMEM)
    count = n_heads + 4 * n_seq
    head_rows = jax.ShapeDtypeStruct((cols, length), LOW)
    return ordered_call(
        deps,
        functools.partial(project_kernel, n_heads, n_seq),
        in_specs=[pl.BlockSpec(memory_space=pltpu.SMEM)]
        + [anywhere] * 5
        + [vmem] * 3,
        out_specs=[vmem] * 5,
        out_shape=[
            jax.ShapeDtypeStruct((n_heads, tok_rows, width), LOW),
            jax.ShapeDtypeStruct((3 * cols, width), LOW),
            head_rows,
            head_rows,
            head_rows,
        ],
        scratch_shapes=[
            pltpu.VMEM((n_seq, 2, 2 * upper.shape[1], upper.shape[2]), LOW),
            pltpu.SemaphoreType.DMA((count,)),
        ],
        compiler_params=pltpu.CompilerParams(vmem_limit_bytes=VMEM_LIMIT),
    )(where, near_rows, far_rows, upper, upper_moved, lower, first_local, cosine, sine)


def attend_kernel(block, n_heads, where_ref, *refs):
    q_ref, k_ref, v_ref, qseg_ref, ksegrow_ref, out_ref, lse_ref = refs[:7]
    send_refs, (q_ext, k_ext, v_ext) = refs[7 : 7 + n_heads], refs[7 + n_heads :]
    length = q_ref.shape[1]
    size = length // n_heads
    row_ids, query_rows, key_rows = segment_rows(qseg_ref[...], ksegrow_ref[...])
    q_ext[0:HDIM, :] = q_ref[...]
    k_ext[0:HDIM, :] = k_ref[...]
    v_ext[0:HDIM, :] = v_ref[...]
    q_ext[HDIM:, :] = query_rows.astype(LOW)
    k_ext[HDIM:, :] = key_rows.astype(LOW)
    v_ext[HDIM:, :] = jnp.where(row_ids == 0, 1.0, 0.0).astype(LOW)
    own_scores = jnp.sum(q_ref[...].astype(F32) * k_ref[...].astype(F32), axis=0, keepdims=True)
    tiles = tile_plan(length, block)

    def score(tile):
        q0, qn, k0, kn, _ = tile
        return dot(k_ext[:, k0 : k0 + kn], q_ext[:, q0 : q0 + qn], TN)

    ahead = score(tiles[0])
    halves = []
    state = None
    for index, (q0, qn, k0, kn, diagonal) in enumerate(tiles):
        scores = ahead
        if index + 1 < len(tiles):
            ahead = score(tiles[index + 1])
        if diagonal:
            scores = causal(scores, own_scores[:, q0 : q0 + qn], q0, k0)
        new_max = jnp.max(scores, axis=0, keepdims=True)
        if not diagonal:
            new_max = jnp.maximum(state[0], new_max)
        probs = jnp.exp(scores - new_max).astype(LOW)
        mixed = dot(v_ext[:, k0 : k0 + kn], probs, NN)
        if diagonal:
            halves.append((new_max, mixed))
            if len(halves) == 2:
                state = tuple(jnp.concatenate(pair, axis=1) for pair in zip(*halves))
                halves = []
        else:
            state = (new_max, state[1] * jnp.exp(state[0] - new_max) + mixed)
        if index + 1 == len(tiles) or (tiles[index + 1][4] and not halves):
            total_row = state[1][HDIM : HDIM + 1, :]
            begin = (q0 // block) * block
            out_ref[:, begin : begin + block] = (state[1][0:HDIM, :] / total_row).astype(LOW)
            lse_ref[0, :, begin : begin + block] = state[0] + jnp.log(total_row)
    for at in range(n_heads):
        for mask in range(n_heads):

            @pl.when(where_ref[at] == mask)
            def _(at=at, mask=mask):
                send_refs[mask][...] = out_ref[:, at * size : (at + 1) * size]


def head_specs(length, first_head):
    return (
        pl.BlockSpec((HDIM, length), lambda head: (head + first_head, 0)),
        pl.BlockSpec((1, length), lambda head: (0, 0)),
        pl.BlockSpec((1, 1, length), lambda head: (head + first_head, 0, 0)),
    )


def attention_forward(where, n_heads, queries, keys_rot, values, query_segs, key_segs, deps=()):
    cols, length = queries.shape
    heads = cols // HDIM
    wide, row, per_head = head_specs(length, 0)
    result = ordered_call(
        deps,
        functools.partial(attend_kernel, min(BLOCK, length), n_heads),
        grid=(heads,),
        in_specs=[pl.BlockSpec(memory_space=pltpu.SMEM), wide, wide, wide, row, row],
        out_specs=[pl.BlockSpec((HDIM, length), lambda head: (head, 0)), per_head]
        + [pl.BlockSpec((HDIM, length // n_heads), lambda head: (head, 0))] * n_heads,
        out_shape=[
            jax.ShapeDtypeStruct((heads * HDIM, length), LOW),
            jax.ShapeDtypeStruct((heads, 1, length), F32),
        ]
        + [jax.ShapeDtypeStruct((heads * HDIM, length // n_heads), LOW)] * n_heads,
        scratch_shapes=[pltpu.VMEM((HDIM + EXTRA, length), LOW)] * 3,
        compiler_params=pltpu.CompilerParams(vmem_limit_bytes=VMEM_LIMIT),
    )(where, queries, keys_rot, values, query_segs, key_segs)
    return (result[0], result[2:], result[1])


def three_terms(value):
    high = value.astype(LOW).astype(F32)
    middle = (value - high).astype(LOW).astype(F32)
    return (high, middle, value - high - middle)


def attend_back_kernel(block, pieces, where_ref, *refs):
    grad_refs, refs = refs[:pieces], refs[pieces:]
    q_ref, k_ref, v_ref, out_ref, lse_ref, qseg_ref, ksegrow_ref = refs[:7]
    cos_ref, sin_ref, grads_ref, first_ref = refs[7:11]
    dq_ref, dk_ref, dv_ref, q_ext, k_ext, v_ext, g_ext = refs[11:]
    length = q_ref.shape[1]
    half = block // 2
    size = length // pieces
    for index in range(pieces):
        begin = pl.multiple_of(where_ref[index] * size, size)
        g_ext[0:HDIM, pl.ds(begin, size)] = grad_refs[index][...]
    grad_ref = g_ext.at[0:HDIM]
    row_ids, query_rows, key_rows = segment_rows(qseg_ref[...], ksegrow_ref[...])
    delta = jnp.sum(grad_ref[...].astype(F32) * out_ref[...].astype(F32), axis=0, keepdims=True)
    for row, term in enumerate(three_terms(-lse_ref[0])):
        query_rows = jnp.where(row_ids == SEGMENTS + row, term, query_rows)
    key_rows = jnp.where((row_ids >= SEGMENTS) & (row_ids < SEGMENTS + 3), 1.0, key_rows)
    grad_rows = jnp.zeros_like(query_rows)
    for row, term in enumerate(three_terms(-delta)):
        grad_rows = jnp.where(row_ids == row, term, grad_rows)
    q_ext[0:HDIM, :] = q_ref[...]
    k_ext[0:HDIM, :] = k_ref[...]
    v_ext[0:HDIM, :] = v_ref[...]
    q_ext[HDIM:, :] = query_rows.astype(LOW)
    k_ext[HDIM:, :] = key_rows.astype(LOW)
    v_ext[HDIM:, :] = jnp.where(row_ids < 3, 1.0, 0.0).astype(LOW)
    g_ext[HDIM:, :] = grad_rows.astype(LOW)
    own_scores = jnp.sum(q_ref[...].astype(F32) * k_ref[...].astype(F32), axis=0, keepdims=True)
    own_scores = own_scores - lse_ref[0]
    tiles = tile_plan(length, block)

    def score(tile):
        q0, qn, k0, kn, _ = tile
        rows, cols = slice(k0, k0 + kn), slice(q0, q0 + qn)
        scores = dot(k_ext[:, rows], q_ext[:, cols], TN)
        return (scores, dot(v_ext[:, rows], g_ext[:, cols], TN))

    ahead = score(tiles[0])
    for index, (q0, qn, k0, kn, diagonal) in enumerate(tiles):
        scores, grad_probs = ahead
        if index + 1 < len(tiles):
            ahead = score(tiles[index + 1])
        rows, cols = slice(k0, k0 + kn), slice(q0, q0 + qn)
        if diagonal:
            scores = causal(scores, own_scores[:, cols], q0, k0)
        probs = jnp.exp(scores)
        grad_scores = (probs * grad_probs).astype(LOW)
        dv = dot(grad_ref[:, cols], probs.astype(LOW), NT)
        dk = dot(q_ref[:, cols], grad_scores, NT)
        dq = dot(k_ref[:, rows], grad_scores, NN)
        if not diagonal:
            dq_ref[:, cols] += dq
            dk_ref[:, rows] += dk
            dv_ref[:, rows] += dv
            continue
        dq_ref[:, cols] = dq
        if kn == half:
            dk_ref[:, rows] = dk
            dv_ref[:, rows] = dv
        else:
            low_rows, high_rows = slice(k0, k0 + half), slice(k0 + half, k0 + block)
            dk_ref[:, low_rows] += dk[:, :half]
            dv_ref[:, low_rows] += dv[:, :half]
            dk_ref[:, high_rows] = dk[:, half:]
            dv_ref[:, high_rows] = dv[:, half:]
    cosine, sine = cos_ref[...], sin_ref[...]
    grads_ref[0] = turn(dq_ref[...] * HDIM ** (-0.5), cosine, sine, -1.0).astype(LOW)
    grads_ref[1] = turn(dk_ref[...], cosine, sine, -1.0).astype(LOW)
    blended = BLEND * dv_ref[...]
    grads_ref[2] = blended.astype(LOW)
    first_ref[...] = (1.0 - BLEND) * dv_ref[...]


def attention_backward(
    where, group, grad_pieces, queries, keys_rot, values, mixed, lse, segs, cosine, sine, deps=()
):
    query_segs, key_segs = segs
    cols, length = queries.shape
    heads = cols // HDIM
    wide, row, per_head = head_specs(length, group * heads)
    local = pl.BlockSpec((HDIM, length), lambda head: (head, 0))
    table = pl.BlockSpec((HDIM // 2, length), lambda head: (0, 0))
    piece = pl.BlockSpec((HDIM, length // len(grad_pieces)), lambda head: (head, 0))
    return ordered_call(
        deps,
        functools.partial(attend_back_kernel, min(BLOCK, length), len(grad_pieces)),
        grid=(heads,),
        in_specs=[pl.BlockSpec(memory_space=pltpu.SMEM)]
        + [piece] * len(grad_pieces)
        + [wide, wide, wide, wide, per_head, row, row, table, table],
        out_specs=[pl.BlockSpec((3, HDIM, length), lambda head: (0, head, 0)), local],
        out_shape=[
            jax.ShapeDtypeStruct((3, heads * HDIM, length), LOW),
            jax.ShapeDtypeStruct((heads * HDIM, length), F32),
        ],
        scratch_shapes=[pltpu.VMEM((HDIM, length), F32)] * 3
        + [pltpu.VMEM((HDIM + EXTRA, length), LOW)] * 4,
        compiler_params=pltpu.CompilerParams(vmem_limit_bytes=VMEM_LIMIT),
    )(
        where,
        *grad_pieces,
        queries,
        keys_rot,
        values,
        mixed,
        lse,
        query_segs,
        key_segs,
        cosine,
        sine,
    )


def inverse_root(rows):
    return lax.rsqrt(jnp.mean(rows * rows, axis=-1, keepdims=True) + NORM_EPS)


def join_kernel(n_heads, n_seq, where_ref, *refs):
    piece_refs, refs = refs[:n_heads], refs[n_heads:]
    own_ref, gain_ref, gathered_ref, w_ref, hidden_ref, normed_ref = refs[:6]
    half_refs, (placed, sems) = refs[6:8], refs[8:]
    width, cols = w_ref.shape[1:]
    rows = gathered_ref.shape[0] // (n_seq * n_heads)
    flats = placed.shape[3]
    first_lane = gathered_ref.shape[1] - 2 * flats * cols
    moves = []
    for seq in range(n_seq):
        for head in range(n_heads):
            here = pl.ds((seq * n_heads + head) * rows, rows)
            for side in range(2):
                slot = where_ref[n_heads + n_seq + side]
                for flat in range(flats):
                    lanes = pl.ds(first_lane + (side * flats + flat) * cols, cols)
                    moves.append((gathered_ref.at[here, lanes], placed.at[head, seq, slot, flat]))
    move_all(moves, sems)
    hidden = own_ref[...].astype(F32)
    for mask in range(n_heads):
        weight = placed[where_ref[mask]].reshape(width, cols)
        hidden += dot(piece_refs[mask][...].T, weight, NT)
    for head in range(n_heads):
        w_ref[head] = placed[head].reshape(width, cols)
    hidden_ref[...] = hidden
    normed_ref[...] = (hidden * inverse_root(hidden) * gain_ref[1:2, :]).astype(LOW)
    for part, half_ref in enumerate(half_refs):
        rows = half_ref.shape[0]
        half_ref[...] = normed_ref[part * rows : (part + 1) * rows, :]


def ordered_join_kernel(n_heads, where_ref, *refs):
    piece_refs, refs = refs[:n_heads], refs[n_heads:]
    (own_ref, gain_ref, w_ref, hidden_ref, normed_ref), half_refs = refs[:5], refs[5:]
    hidden = own_ref[...].astype(F32)
    for mask in range(n_heads):
        hidden += dot(piece_refs[mask][...].T, w_ref[where_ref[mask]], NT)
    hidden_ref[...] = hidden
    normed_ref[...] = (hidden * inverse_root(hidden) * gain_ref[1:2, :]).astype(LOW)
    for part, half_ref in enumerate(half_refs):
        rows = half_ref.shape[0]
        half_ref[...] = normed_ref[part * rows : (part + 1) * rows, :]


def join_heads(where, n_seq, pieces, own_rows, gains, gathered, deps=()):
    n_heads, cols = len(pieces), pieces[0].shape[0]
    tok_rows, width = own_rows.shape
    rows = gathered.shape[0] // (n_seq * n_heads)
    flats = width // (2 * n_seq * rows)
    vmem = pl.BlockSpec(memory_space=pltpu.VMEM)
    smem = pl.BlockSpec(memory_space=pltpu.SMEM)
    params = pltpu.CompilerParams(vmem_limit_bytes=VMEM_LIMIT)
    outs = [
        jax.ShapeDtypeStruct((tok_rows, width), F32),
        jax.ShapeDtypeStruct((tok_rows, width), LOW),
    ] + [jax.ShapeDtypeStruct((tok_rows // 2, width), LOW)] * 2
    if cols % 128 == 0:
        return ordered_call(
            deps,
            functools.partial(join_kernel, n_heads, n_seq),
            in_specs=[smem]
            + [vmem] * (n_heads + 2)
            + [pl.BlockSpec(memory_space=pl.ANY)],
            out_specs=[vmem] * 5,
            out_shape=[jax.ShapeDtypeStruct((n_heads, width, cols), LOW)] + outs,
            scratch_shapes=[
                pltpu.VMEM((n_heads, n_seq, 2, flats, rows, cols), LOW),
                pltpu.SemaphoreType.DMA((n_seq * n_heads * 2 * flats,)),
            ],
            compiler_params=params,
        )(where, *pieces, own_rows, gains, gathered)
    out_w = gathered[:, -2 * flats * cols :].reshape(n_seq, n_heads, rows, 2, flats, cols)
    out_w = jnp.where(where[n_heads + n_seq] == 0, out_w, out_w[:, :, :, ::-1])
    out_w = jnp.transpose(out_w, (1, 0, 3, 4, 2, 5)).reshape(n_heads, width, cols)
    joined = ordered_call(
        deps,
        functools.partial(ordered_join_kernel, n_heads),
        in_specs=[smem] + [vmem] * (n_heads + 3),
        out_specs=[vmem] * 4,
        out_shape=outs,
        compiler_params=params,
    )(where, *pieces, own_rows, gains, out_w)
    return (out_w, *joined)


def part_kernel(n_heads, groups, where_ref, *refs):
    own_ref, arrived_refs, refs = refs[0], refs[1:3], refs[3:]
    hidden_ref, cot_ref, gain_ref, w_ref, grad_ref, gain_grad_ref = refs[:6]
    low_ref, piece_refs = refs[6], refs[7:]
    hidden = hidden_ref[...]
    inverse = inverse_root(hidden)
    arrived = jnp.concatenate([ref[...] for ref in arrived_refs], axis=0)
    grad_two = own_ref[...].astype(F32) + arrived.astype(F32)
    scaled = gain_ref[1:2, :] * grad_two
    inner = jnp.mean(scaled * hidden, axis=-1, keepdims=True)
    grad = cot_ref[...].astype(F32) + inverse * scaled - hidden * (inverse**3 * inner)
    gain_grad_ref[...] = jnp.sum(grad_two * hidden * inverse, axis=0, keepdims=True)
    grad_ref[...] = grad
    low = grad.astype(LOW)
    low_ref[...] = low
    rows = piece_refs[0].shape[0]
    for mask in range(n_heads):
        piece = dot(low, w_ref[where_ref[mask]], NN).astype(LOW).T
        for at in range(groups):
            piece_refs[mask * groups + at][...] = piece[at * rows : (at + 1) * rows]


def part_heads(where, groups, back_own, back_arrived, hidden, cotangent, gains, out_w, deps=()):
    n_heads = out_w.shape[0]
    tok_rows, width = hidden.shape
    cols = out_w.shape[-1]
    vmem = pl.BlockSpec(memory_space=pltpu.VMEM)
    result = ordered_call(
        deps,
        functools.partial(part_kernel, n_heads, groups),
        in_specs=[pl.BlockSpec(memory_space=pltpu.SMEM)] + [vmem] * 7,
        out_specs=[vmem] * (3 + n_heads * groups),
        out_shape=[
            jax.ShapeDtypeStruct((tok_rows, width), F32),
            jax.ShapeDtypeStruct((1, width), F32),
            jax.ShapeDtypeStruct((tok_rows, width), LOW),
        ]
        + [jax.ShapeDtypeStruct((cols // groups, tok_rows), LOW)] * (n_heads * groups),
        compiler_params=pltpu.CompilerParams(vmem_limit_bytes=VMEM_LIMIT),
    )(where, back_own, *back_arrived, hidden, cotangent, gains, out_w)
    flat = result[3:]
    pieces = [flat[mask * groups : (mask + 1) * groups] for mask in range(n_heads)]
    return result[:3] + [pieces] if isinstance(result, list) else tuple(result[:3]) + (pieces,)


def out_grad_kernel(low_ref, *refs):
    piece_refs, (mine_ref, send_ref) = refs[:-2], refs[-2:]
    turned = low_ref[...].T
    n_seq, n_hid, shares, rows, cols = mine_ref.shape
    for mask in range(2 * shares):
        product = dot(turned, piece_refs[mask][...], NT).astype(LOW).reshape(n_seq, n_hid, rows, cols)
        (send_ref if mask % 2 else mine_ref)[:, :, mask // 2] = product


def out_gradient(low, pieces, n_seq, n_hid, deps=()):
    shares, cols = len(pieces) // 2, pieces[0].shape[0]
    width = low.shape[1]
    vmem = pl.BlockSpec(memory_space=pltpu.VMEM)
    shape = (n_seq, n_hid, shares, width // (n_seq * n_hid), cols)
    return ordered_call(
        deps,
        out_grad_kernel,
        in_specs=[vmem] * (1 + len(pieces)),
        out_specs=[vmem, vmem],
        out_shape=[jax.ShapeDtypeStruct(shape, LOW)] * 2,
        compiler_params=pltpu.CompilerParams(vmem_limit_bytes=VMEM_LIMIT),
    )(low, *pieces)


def ffn_chunks(width):
    return [slice(begin, min(begin + 512, width)) for begin in range(0, width, 512)]


def ffn_kernel(n_heads, n_seq, where_ref, x_ref, c_ref, near_ref, far_ref, gathered_ref, *refs):
    part_ref, back_ref, units_ref, gate_all, up_w, down_w, sems = refs
    act_ref, dgate_ref, dup_ref = (units_ref.at[kind] for kind in range(3))
    units = units_ref.shape[2]
    copies = [
        pltpu.make_async_copy(gathered_ref.at[:, pl.ds(0, units)], up_w, sems.at[0]),
        pltpu.make_async_copy(gathered_ref.at[:, pl.ds(units, units)], down_w, sems.at[1]),
    ]
    for at in range(n_seq):
        seq_slot = where_ref[n_heads + at]
        for mask in range(n_heads):
            copies.append(
                pltpu.make_async_copy(
                    (far_ref if mask % 2 else near_ref).at[mask // 2, at],
                    gate_all.at[seq_slot, where_ref[mask]],
                    sems.at[len(copies)],
                )
            )
    for copy in copies:
        copy.start()
    rows, model_width = x_ref.shape
    x, c = x_ref[...], c_ref[...]
    for copy in copies:
        copy.wait()
    chunks = ffn_chunks(units)
    for cols in chunks:
        gate = dot(x, gate_all[..., cols].reshape(model_width, -1), NN)
        up = dot(x, up_w[:, cols], NN)
        grad = dot(c, down_w[:, cols], NN)
        sigmoid = jax.nn.sigmoid(gate)
        silu = gate * sigmoid
        act_ref[:, cols] = (silu * up).astype(LOW)
        dgate_ref[:, cols] = (grad * up * (sigmoid + silu * (1.0 - sigmoid))).astype(LOW)
        dup_ref[:, cols] = (grad * silu).astype(LOW)
    per_seq = model_width // n_seq
    for at in range(n_seq):
        here = slice(at * per_seq, (at + 1) * per_seq)
        gate_w = gate_all[at].reshape(per_seq, units)
        back = dot(dgate_ref[...], gate_w, NT) + dot(dup_ref[...], up_w[here, :], NT)
        back_ref[:, here] = back.astype(LOW)
        part_ref[:, here] = dot(act_ref[...], down_w[here, :], NT).astype(LOW)


def feed_forward(where, normed, cotangent, part, gate_groups, gathered, deps=()):
    rows, width = normed.shape
    shares, n_seq, piece_rows, units = gate_groups[0].shape
    anywhere = pl.BlockSpec(memory_space=pl.ANY)
    vmem = pl.BlockSpec(memory_space=pltpu.VMEM)
    wide = jax.ShapeDtypeStruct((rows, width), LOW)
    narrow = jax.ShapeDtypeStruct((3, rows, units), LOW)
    return ordered_call(
        deps,
        functools.partial(ffn_kernel, 2 * shares, n_seq),
        grid=(1,),
        in_specs=[
            pl.BlockSpec(memory_space=pltpu.SMEM),
            vmem,
            pl.BlockSpec((rows, width), lambda at: (part, 0)),
        ]
        + [anywhere] * 3,
        out_specs=[vmem] * 3,
        out_shape=[wide, wide, narrow],
        scratch_shapes=[
            pltpu.VMEM((n_seq, 2 * shares, piece_rows, units), LOW),
            pltpu.VMEM((width, units), LOW),
            pltpu.VMEM((width, units), LOW),
            pltpu.SemaphoreType.DMA((2 * shares * n_seq + 2,)),
        ],
        compiler_params=pltpu.CompilerParams(vmem_limit_bytes=VMEM_LIMIT),
    )(where, normed, cotangent, *gate_groups, gathered)


def ffn_grad_kernel(n_heads, runs, *refs):
    left_refs, unit_refs, out_ref = (refs[:2], refs[2 : 2 + runs]), refs[2 + runs : -1], refs[-1]
    size = out_ref.shape[3]
    turned = [jnp.concatenate([left[...].T for left in lefts], axis=1) for lefts in left_refs]
    for kind in range(3):
        left = turned[min(kind, 1)]
        for cols in ffn_chunks(out_ref.shape[4]):
            both, begin = None, 0
            for units in unit_refs:
                rows = units.shape[1]
                term = dot(left[:, begin : begin + rows], units[kind, :, cols], NN)
                both, begin = term if both is None else both + term, begin + rows
            both = both.astype(LOW)
            for at in range(n_heads):
                out_ref[0, at, kind, :, cols] = both[at * size : (at + 1) * size]


def ffn_gradients(n_heads, n_seq, back_rows, normed_rows, units, deps=()):
    width, n_units = normed_rows[0].shape[1], units[0].shape[2]
    tile = width // n_seq
    lefts = [
        pl.BlockSpec((rows.shape[0], tile), lambda at: (0, at)) for rows in (*back_rows, *normed_rows)
    ]
    rights = [pl.BlockSpec(run.shape, lambda at: (0, 0, 0)) for run in units]
    shape = (n_heads, 3, tile // n_heads, n_units)
    return ordered_call(
        deps,
        functools.partial(ffn_grad_kernel, n_heads, len(normed_rows)),
        grid=(n_seq,),
        in_specs=lefts + rights,
        out_specs=pl.BlockSpec((1,) + shape, lambda at: (at, 0, 0, 0, 0)),
        out_shape=jax.ShapeDtypeStruct((n_seq,) + shape, LOW),
        compiler_params=pltpu.CompilerParams(vmem_limit_bytes=VMEM_LIMIT),
    )(*back_rows, *normed_rows, *units)


def by_side(side, first, second):
    return (jnp.where(side == 0, first, second), jnp.where(side == 0, second, first))


def add_halves_kernel(side_at, where_ref, mine_ref, arrived_ref, keep_ref, send_ref):
    side = where_ref[side_at]
    for lead in range(mine_ref.shape[0]):
        for pair in range(mine_ref.shape[1]):
            first, second = (
                (
                    mine_ref[lead, pair, half].astype(F32) + arrived_ref[lead, pair, half].astype(F32)
                ).astype(LOW)
                for half in range(2)
            )
            keep_ref[lead, pair], send_ref[lead, pair] = by_side(side, first, second)


def add_halves(where, side_at, mine, arrived, deps=()):
    lead, pairs, _, rows, cols = mine.shape
    vmem = pl.BlockSpec(memory_space=pltpu.VMEM)
    return ordered_call(
        deps,
        functools.partial(add_halves_kernel, side_at),
        in_specs=[pl.BlockSpec(memory_space=pltpu.SMEM), vmem, vmem],
        out_specs=[vmem, vmem],
        out_shape=[jax.ShapeDtypeStruct((lead, pairs, rows, cols), LOW)] * 2,
        compiler_params=pltpu.CompilerParams(vmem_limit_bytes=VMEM_LIMIT),
    )(where, mine, arrived)


def add_split_kernel(count, first_slot, where_ref, *refs):
    pairs, out_refs = refs[: 2 * count], refs[2 * count :]
    for step, out_ref in enumerate(out_refs):
        at = where_ref[first_slot + step]
        begin = 0
        for mine_ref, arrived_ref in zip(pairs[::2], pairs[1::2]):
            for part in range(mine_ref.shape[1]):
                cols = mine_ref.shape[3]
                both = mine_ref[at, part].astype(F32) + arrived_ref[at, part].astype(F32)
                out_ref[:, begin : begin + cols] = both.astype(LOW)
                begin += cols


def add_split(where, first_slot, *pairs, deps=()):
    vmem = pl.BlockSpec(memory_space=pltpu.VMEM)
    steps, _, rows, _ = pairs[0][0].shape
    width = sum(mine.shape[1] * mine.shape[3] for mine, _ in pairs)
    return ordered_call(
        deps,
        functools.partial(add_split_kernel, len(pairs), first_slot),
        in_specs=[pl.BlockSpec(memory_space=pltpu.SMEM)] + [vmem] * (2 * len(pairs)),
        out_specs=[vmem] * steps,
        out_shape=[jax.ShapeDtypeStruct((rows, width), LOW)] * steps,
        compiler_params=pltpu.CompilerParams(vmem_limit_bytes=VMEM_LIMIT),
    )(where, *[half for pair in pairs for half in pair])


def one_grad_kernel(n_heads, groups, where_ref, *refs):
    grad_refs, w_ref, mine_ref, send_refs = refs[:groups], refs[groups], refs[groups + 1], refs[groups + 2 :]
    size = grad_refs[0].shape[2] // n_heads
    half = size // 2
    for mask in range(n_heads - 1, -1, -1):
        cols = pl.ds(pl.multiple_of(where_ref[mask] * size, size), size)
        grads = jnp.concatenate(
            [grad_refs[at][kind, :, cols] for kind in range(3) for at in range(groups)], axis=0
        )
        product = dot(grads, w_ref[...], TN).astype(LOW)
        if mask % 2:
            send_refs[mask - 1][...], send_refs[mask][...] = product[:half], product[half:]
        else:
            mine_ref[mask // 2] = product


def one_gradient(where, n_heads, grads, in_w, deps=()):
    groups = len(grads)
    length, width = grads[0].shape[2], in_w.shape[1]
    vmem = pl.BlockSpec(memory_space=pltpu.VMEM)
    size = length // n_heads
    result = ordered_call(
        deps,
        functools.partial(one_grad_kernel, n_heads, groups),
        in_specs=[pl.BlockSpec(memory_space=pltpu.SMEM)] + [vmem] * (groups + 1),
        out_specs=[vmem] * (1 + n_heads),
        out_shape=[jax.ShapeDtypeStruct((n_heads // 2, size, width), LOW)]
        + [jax.ShapeDtypeStruct((size // 2, width), LOW)] * n_heads,
        compiler_params=pltpu.CompilerParams(vmem_limit_bytes=VMEM_LIMIT),
    )(where, *grads, in_w)
    return (result[0], list(result[1:]))


def near_sum_kernel(shares, mine_ref, *refs):
    moved_refs, out_refs = refs[: 2 * shares], refs[2 * shares :]
    half = moved_refs[0].shape[0]
    for at in range(shares):
        for part in range(2):
            here = slice(part * half, (part + 1) * half)
            both = mine_ref[at, here].astype(F32) + moved_refs[2 * at + part][...].astype(F32)
            out_refs[at][here] = both.astype(LOW)


def near_sum(mine, moved, deps=()):
    shares, rows, width = mine.shape
    vmem = pl.BlockSpec(memory_space=pltpu.VMEM)
    return ordered_call(
        deps,
        functools.partial(near_sum_kernel, shares),
        in_specs=[vmem] * (1 + len(moved)),
        out_specs=[vmem] * shares,
        out_shape=[jax.ShapeDtypeStruct((rows, width), LOW)] * shares,
        compiler_params=pltpu.CompilerParams(vmem_limit_bytes=VMEM_LIMIT),
    )(mine, *moved)


def in_grad_kernel(side_at, where_ref, rows_ref, *refs):
    grad_refs, (mine_ref, send_ref) = refs[:-2], refs[-2:]
    n_seq, rows, _ = mine_ref.shape
    side = where_ref[side_at]
    for at, grad_ref in enumerate(grad_refs):
        kinds, cols, length = grad_ref.shape
        grads = grad_ref[...].reshape(kinds * cols, length)
        product = dot(grads, rows_ref[...], NN).astype(LOW).T.reshape(n_seq, 2, rows, kinds * cols)
        here = slice(at * kinds * cols, (at + 1) * kinds * cols)
        mine_ref[:, :, here], send_ref[:, :, here] = by_side(side, product[:, 0], product[:, 1])


def in_gradient(where, side_at, n_seq, group_rows, grads, deps=()):
    groups = len(grads)
    length, width = group_rows.shape
    cols = grads[0].shape[1]
    vmem = pl.BlockSpec(memory_space=pltpu.VMEM)
    shape = (n_seq, width // (2 * n_seq), 3 * cols * groups)
    return ordered_call(
        deps,
        functools.partial(in_grad_kernel, side_at),
        in_specs=[pl.BlockSpec(memory_space=pltpu.SMEM)] + [vmem] * (1 + groups),
        out_specs=[vmem, vmem],
        out_shape=[jax.ShapeDtypeStruct(shape, LOW)] * 2,
        compiler_params=pltpu.CompilerParams(vmem_limit_bytes=VMEM_LIMIT),
    )(where, group_rows, *grads)


def swap(value, axis, mask):
    return lax.ppermute(value, axis, [(i, i ^ mask) for i in range(lax.axis_size(axis))])


def shift(value, axis, step):
    size = lax.axis_size(axis)
    return lax.ppermute(value, axis, [(i, (i + step) % size) for i in range(size)])


def bits_from_high(size):
    bit = size // 2
    while bit:
        yield bit
        bit //= 2


def gather_masks(value, axis, bits):
    held = {0: value}
    for bit in bits:
        held.update({mask ^ bit: swap(block, axis, bit) for mask, block in list(held.items())})
    return held


def from_all(value, axis):
    return [value] + [shift(value, axis, step) for step in range(1, lax.axis_size(axis))]


def total(value, axis):
    size = lax.axis_size(axis)
    bit = 1
    while bit < size:
        if bit * 4 <= size:
            one, two, three = (swap(value, axis, mask * bit) for mask in (1, 2, 3))
            value = (value + one) + (two + three)
            bit *= 4
        else:
            value = value + swap(value, axis, bit)
            bit *= 2
    return value


def tie(*values):
    return lax.optimization_barrier(values)


def send_blocks(blocks, name):
    return [blocks[0]] + [shift(block, name, step) for step, block in enumerate(blocks) if step]


def add_up(blocks):
    result = blocks[0].astype(F32)
    for block in blocks[1:]:
        result = result + block.astype(F32)
    return result


def fold_masks(blocks, bits):
    sums = dict(blocks)
    for bit in bits:
        for mask in sorted(sums, reverse=True):
            if mask & bit:
                moved = swap(sums.pop(mask), "heads", bit)
                if bit == bits[-1]:
                    return (sums[0], moved)
                sums[mask ^ bit] = (sums[mask ^ bit].astype(F32) + moved.astype(F32)).astype(LOW)


def rows_by_default(value):
    return with_layout_constraint(value, Layout(tuple(range(value.ndim))))


def adam_moments(mean_old, var_old, grad):
    mean_new = BETA_ONE * mean_old + (1.0 - BETA_ONE) * grad
    var_new = BETA_TWO * var_old + (1.0 - BETA_TWO) * grad * grad
    direction = (
        mean_new / (1.0 - BETA_ONE**STEP) / (jnp.sqrt(var_new / (1.0 - BETA_TWO**STEP)) + ADAM_EPS)
    )
    return (mean_new, var_new, direction)


def lane_row(values):
    lanes = lax.broadcasted_iota(jnp.int32, (1, ROW), 1)
    row = jnp.zeros((1, ROW), F32)
    for lane, value in values.items():
        row = jnp.where(lanes == lane, value, row)
    return row


def total_of(value):
    return jnp.sum(jnp.sum(value, axis=1, keepdims=True), axis=0, keepdims=True)


def step_part(weight, mean_old, var_old, grad):
    mean_new, var_new, direction = adam_moments(mean_old, var_old, grad)
    update = direction + DECAY * weight
    return (mean_new, var_new, update, total_of(weight * weight), total_of(update * update))


def sum_blocks(refs, rows, cols):
    result = refs[0][rows, cols].astype(F32)
    for ref in refs[1:]:
        result = result + ref[rows, cols].astype(F32)
    return result


def in_step_kernel(n_blocks, groups, *refs):
    block_refs, (w_ref, m_ref, v_ref) = refs[:n_blocks], refs[n_blocks : n_blocks + 3]
    mean_ref, var_ref, update_ref, row_ref = refs[n_blocks + 3 :]
    size = w_ref.shape[2] // groups
    values = {}
    for kind in range(w_ref.shape[0]):
        for at in range(groups):
            here = (kind, slice(None), slice(at * size, (at + 1) * size))
            begin = (at * w_ref.shape[0] + kind) * size
            grad = sum_blocks(block_refs, slice(None), slice(begin, begin + size))
            mean, var, update, weight_sq, update_sq = step_part(
                w_ref[here], m_ref[here], v_ref[here], grad
            )
            mean_ref[here], var_ref[here], update_ref[here] = mean, var, update
            values[kind] = weight_sq + values[kind] if at else weight_sq
            values[MATRICES + kind] = update_sq + values[MATRICES + kind] if at else update_sq
    row_ref[...] = lane_row(values)


def ffn_step_kernel(*refs):
    grad_ref, gu_refs, down_refs, out_refs = refs[0], refs[1:4], refs[4:7], refs[7:]
    row_ref = out_refs[6]
    rows = down_refs[0].shape[0]
    values = {}
    for kind in range(3):
        begin = (kind + 1) % 3 * rows
        grad = grad_ref[begin : begin + rows, :].astype(F32)
        here = (kind,) if kind < 2 else (slice(None),)
        ins, outs = (gu_refs, out_refs[:3]) if kind < 2 else (down_refs, out_refs[3:6])
        results = step_part(*[ref[here] for ref in ins], grad)
        for ref, result in zip(outs, results[:3]):
            ref[here] = result
        values[4 + kind], values[MATRICES + 4 + kind] = results[3:]
    row_ref[...] = lane_row(values)


def out_step_kernel(own_ref, arrived_ref, w_ref, m_ref, v_ref, mean_ref, var_ref, update_ref, row_ref):
    grad = (own_ref[...].astype(F32) + arrived_ref[...].astype(F32)).T
    mean, var, update, weight_sq, update_sq = step_part(w_ref[...], m_ref[...], v_ref[...], grad)
    mean_ref[...], var_ref[...], update_ref[...] = mean, var, update
    row_ref[...] = lane_row({3: weight_sq, MATRICES + 3: update_sq})


def step_call(kernel, arrays, like, deps=()):
    vmem = pl.BlockSpec(memory_space=pltpu.VMEM)
    shapes = [jax.ShapeDtypeStruct(array.shape, F32) for array in like for _ in range(3)]
    return ordered_call(
        deps,
        kernel,
        in_specs=[vmem] * len(arrays),
        out_specs=[vmem] * (len(shapes) + 1),
        out_shape=shapes + [jax.ShapeDtypeStruct((1, ROW), F32)],
        compiler_params=pltpu.CompilerParams(vmem_limit_bytes=VMEM_LIMIT),
    )(*arrays)


def last_step_kernel(*refs):
    sums_ref, gain_refs, refs = refs[0], refs[1:4], refs[4:]
    weight_refs, update_refs, gain_outs, new_refs = refs[:4], refs[4:8], refs[8:11], refs[11:]
    sums = sums_ref[2:3, :]
    lanes = lax.broadcasted_iota(jnp.int32, sums.shape, 1)

    def lane(at):
        return total_of(jnp.where(lanes == at, sums, 0.0))

    mean_new, var_new, direction = adam_moments(gain_refs[1][...], gain_refs[2][...], sums_ref[0:2, :])
    gain_outs[0][...] = gain_refs[0][...] - GAIN_RATE * direction
    gain_outs[1][...], gain_outs[2][...] = mean_new, var_new
    at = 0
    for weight_ref, update_ref, new_ref in zip(weight_refs, update_refs, new_refs):
        parts = [(kind,) for kind in range(weight_ref.shape[0])]
        for here in parts if len(weight_ref.shape) == 3 else [(slice(None),)]:
            ratio = jnp.sqrt(lane(at)) / jnp.sqrt(lane(MATRICES + at) + 1e-12)
            new_ref[here] = weight_ref[here] - MATRIX_RATE * ratio * update_ref[here]
            at += 1


def last_step(sums, gains, weights, updates):
    vmem = pl.BlockSpec(memory_space=pltpu.VMEM)
    arrays = [sums, *gains, *weights, *updates]
    outs = [jax.ShapeDtypeStruct(array.shape, F32) for array in (*gains, *weights)]
    return ordered_call(
        (),
        last_step_kernel,
        in_specs=[vmem] * len(arrays),
        out_specs=[vmem] * len(outs),
        out_shape=outs,
        compiler_params=pltpu.CompilerParams(vmem_limit_bytes=VMEM_LIMIT),
    )(*arrays)


def input_grad_kernel(own_ref, arrived_ref, tokens_ref, gain_ref, grad_ref, out_ref, gain_grad_ref):
    rows = tokens_ref[...].astype(F32)
    inverse = inverse_root(rows)
    grad_one = own_ref[...].astype(F32) + arrived_ref[...].astype(F32)
    scaled = gain_ref[0:1, :] * grad_one
    inner = jnp.mean(scaled * rows, axis=-1, keepdims=True)
    out_ref[...] = grad_ref[...] + inverse * scaled - rows * (inverse**3 * inner)
    gain_grad_ref[...] = jnp.sum(grad_one * rows * inverse, axis=0, keepdims=True)


def input_gradient(own, arrived, tokens, gains, grad_hidden):
    rows, width = tokens.shape
    vmem = pl.BlockSpec(memory_space=pltpu.VMEM)
    return ordered_call(
        (),
        input_grad_kernel,
        in_specs=[vmem] * 5,
        out_specs=[vmem] * 2,
        out_shape=[
            jax.ShapeDtypeStruct((rows, width), F32),
            jax.ShapeDtypeStruct((1, width), F32),
        ],
        compiler_params=pltpu.CompilerParams(vmem_limit_bytes=VMEM_LIMIT),
    )(own, arrived, tokens, gains, grad_hidden)


def rope_tables(position_ids):
    half_dim = HDIM // 2
    freqs = ROPE_BASE ** (-(jnp.arange(half_dim, dtype=jnp.float32) * 2.0 / HDIM))
    angles = freqs[:, None] * position_ids.astype(jnp.float32)[None, :]
    return (jnp.cos(angles), jnp.sin(angles))


def per_device(
    tokens_in,
    first_value,
    cotangent,
    counts,
    segments,
    positions,
    norm_gains,
    gain_mean,
    gain_var,
    heads_in,
    heads_in_mean,
    heads_in_var,
    heads_out,
    heads_out_mean,
    heads_out_var,
    gate_up,
    gate_up_mean,
    gate_up_var,
    down_proj,
    down_mean,
    down_var,
):
    n_seq, n_heads, n_hid = (lax.axis_size(name) for name in ("seq", "heads", "hid"))
    at_seq, at_heads, at_hid = (lax.axis_index(name) for name in ("seq", "heads", "hid"))
    own_rows = tokens_in[0].astype(F32)
    tok_rows, model_width = own_rows.shape
    length = tok_rows * n_heads
    head_cols = heads_in.shape[2]
    hidden_cols = gate_up.shape[2]
    near = 1
    far_bits = [bit for bit in bits_from_high(n_heads) if bit > near]
    masks = list(range(n_heads))
    groups = 1
    seq_slots = [lax.rem(at_seq + n_seq - step, n_seq) for step in range(n_seq)]
    where = jnp.stack(
        [at_heads ^ mask for mask in masks]
        + seq_slots
        + [at_hid, at_hid ^ 1]
        + [lax.rem(at_seq + step, n_seq) for step in range(n_seq)]
        + [lax.rem(at_heads // bit, 2) for bit in [near] + far_bits[::-1]]
    ).astype(jnp.int32)
    hid_side = n_heads + n_seq
    seq_steps = hid_side + 2
    heads_sides = seq_steps + n_seq

    head_low, own_rows = tie(
        jnp.concatenate(
            [jnp.swapaxes(heads_in, 0, 1).reshape(-1, 3 * head_cols), heads_out.T], axis=1
        ).astype(LOW),
        own_rows,
    )
    in_low, out_low = head_low[:, : 3 * head_cols], head_low[:, 3 * head_cols :]
    half = in_low.shape[0] // 2
    upper_pieces = from_all(in_low[:half], "seq")
    piece_rows = gate_up.shape[1]
    flats = out_low.shape[0] // piece_rows

    def flat(rows):
        return jnp.moveaxis(rows.reshape(flats, piece_rows, head_cols), 0, 1).reshape(piece_rows, -1)

    lower_sent = jnp.concatenate([in_low[half:], out_low[:half], out_low[half:]], axis=1)
    lower_moved = swap(lower_sent, "hid", 1)

    inv_one = inverse_root(own_rows)
    normed_one = (own_rows * inv_one * norm_gains[0]).astype(LOW)
    far_blocks = gather_masks(normed_one, "heads", far_bits)
    lower_moved, far_blocks[0] = tie(lower_moved, far_blocks[0])
    out_moved = jnp.concatenate(
        [lower_moved[:, 3 * head_cols : 4 * head_cols], lower_moved[:, 4 * head_cols :]], axis=0
    )

    gathered = lax.all_gather(
        jnp.concatenate(
            [gate_up[1].astype(LOW), down_proj.T.astype(LOW), flat(out_low), flat(out_moved)],
            axis=1,
        ),
        ("seq", "heads"),
        axis=0,
        tiled=True,
    )

    upper_pieces, lower_pair = tie(
        upper_pieces, jnp.stack([in_low[half:], lower_moved[:, : 3 * head_cols]])
    )
    upper, lower_pair = tie(jnp.stack(upper_pieces), lower_pair)
    upper_moved = swap(upper, "hid", 1)
    lower_pieces = from_all(lower_pair, "seq")
    cosine, sine_table = rope_tables(positions[0])
    row_ids = jnp.arange(length, dtype=jnp.int32)
    is_valid = row_ids % tok_rows < jnp.repeat(counts[0], tok_rows, total_repeat_length=length)
    segs = (segments, jnp.where(is_valid[None], segments, -1))
    far_blocks, lower_pieces, upper_moved, gate_low, cosine, sine_table, segs = tie(
        far_blocks,
        lower_pieces,
        upper_moved,
        gate_up[0].astype(LOW),
        cosine,
        sine_table,
        segs,
    )
    gate_pieces = from_all(gate_low, "seq")
    near_rows = jnp.stack([far_blocks[mask] for mask in masks[::2]])
    far_rows = swap(near_rows, "heads", near)
    lower = jnp.stack(lower_pieces)

    group_rows, in_w, queries, keys_rot, values = project(
        where,
        near_rows,
        far_rows,
        upper,
        upper_moved,
        lower,
        first_value[0],
        cosine,
        sine_table,
    )
    group_rows = group_rows.reshape(length, model_width)
    cot_low, queries = tie(cotangent[0], queries)
    back_other = swap(cot_low, "hid", 1)

    mixed, sends, lse = attention_forward(
        where, n_heads, queries, keys_rot, values, *segs
    )
    back_other, sends = tie(back_other, sends)
    arrived = [swap(sends[mask], "heads", mask) if mask else sends[mask] for mask in masks]
    gate_pieces, arrived = tie(gate_pieces, arrived)
    gate_stack = jnp.stack(gate_pieces)
    gate_blocks = gather_masks(gate_stack, "heads", far_bits)
    first_low, values_low, lse = tie(first_value[0], values, lse)
    first_wide, blended_wide = first_low.astype(F32), values_low.astype(F32)
    value_row = lane_row(
        {
            2 * MATRICES: jnp.sum(first_wide * first_wide),
            2 * MATRICES + 1: jnp.sum(blended_wide * blended_wide),
        }
    )
    out_w, hidden, normed_two, *normed_halves = join_heads(
        where, n_seq, arrived, tokens_in[0], norm_gains, gathered, deps=(gate_stack, value_row)
    )
    gate_blocks, normed_two = tie(gate_blocks, normed_two)
    gate_near = jnp.stack([gate_blocks[mask] for mask in masks[::2]])
    gate_far = swap(gate_near, "heads", near)
    normed_other = [swap(half, "hid", 1) for half in normed_halves]
    weights = ((gate_near, gate_far), gathered)

    ffn_own, back_own, units_own = feed_forward(
        where, normed_two, cotangent[0], 0, *weights
    )
    units, ffn_far, back_arrived = [units_own], [], []
    deps = back_own
    for part in range(2):
        ffn_part, back_part, units_part = feed_forward(
            where, normed_other[part], back_other, part, *weights, deps=deps
        )
        deps = back_part
        units.append(units_part)
        ffn_far.append(ffn_part)
        back_arrived.append(swap(back_part, "hid", 1))

    made = ffn_gradients(
        n_heads,
        n_seq,
        (cotangent[0], back_other),
        (normed_two, *normed_other),
        units,
        deps=(deps, back_arrived[0]),
    )
    made, back_arrived[1] = tie(made, back_arrived[1])
    ffn_grads = lax.psum_scatter(
        made.reshape(-1, hidden_cols), ("seq", "heads"), scatter_dimension=0, tiled=True
    )

    grad_hidden, gain_grad_two, grad_hidden_low, grad_pieces = part_heads(
        where,
        groups,
        back_own,
        back_arrived,
        hidden,
        cotangent[0],
        norm_gains,
        out_w,
    )
    ffn_far, grad_hidden_low = tie(ffn_far, grad_hidden_low)
    grad_arrived = [grad_pieces[0][0]] + [
        swap(grad_pieces[mask][0], "heads", mask) for mask in masks[1:]
    ]
    out_mine, out_sent = out_gradient(grad_hidden_low, arrived, n_seq, n_hid)
    grad_arrived, ffn_far, out_sent = tie(grad_arrived, jnp.concatenate(ffn_far, axis=0), out_sent)
    out_half = swap(out_sent, "heads", near)
    ffn_arrived = swap(ffn_far, "hid", 1)
    grads, first_grad = attention_backward(
        where,
        0,
        grad_arrived,
        queries,
        keys_rot,
        values,
        mixed,
        lse,
        segs,
        cosine,
        sine_table,
    )
    out_mine, out_sent = add_halves(
        where,
        hid_side,
        out_mine.reshape(n_seq, 1, 2, -1, head_cols),
        out_half.reshape(n_seq, 1, 2, -1, head_cols),
        deps=first_grad,
    )
    out_half = swap(out_sent, "hid", 1)
    grads = [grads]
    in_mine, in_sent = in_gradient(where, hid_side, n_seq, group_rows, grads, deps=out_sent)
    in_sent, ffn_arrived = tie(in_sent, ffn_arrived)
    in_half = swap(in_sent, "hid", 1)
    one_mine, one_sent = one_gradient(where, n_heads, grads, in_w, deps=in_sent)
    one_moved = [swap(part, "heads", near) for part in one_sent]
    shares_shape = (n_seq, n_heads // 2, -1, head_cols)
    out_blocks = add_split(
        where,
        seq_steps,
        (out_mine.reshape(shares_shape), out_half.reshape(shares_shape)),
        deps=one_sent[0],
    )
    one_moved, out_blocks = tie(one_moved, out_blocks)
    near_sums, out_blocks = tie(near_sum(one_mine, one_moved), out_blocks)
    out_blocks = send_blocks(out_blocks, "seq")
    one_own, one_arrived = fold_masks({mask: near_sums[mask // 2] for mask in masks[::2]}, far_bits)
    in_blocks = add_split(
        where, seq_steps, (in_mine[:, None], in_half[:, None]), deps=out_blocks[0]
    )
    out_blocks, in_blocks = tie(out_blocks, in_blocks)
    in_blocks = send_blocks(in_blocks, "seq")

    gu = (gate_up, gate_up_mean, gate_up_var)
    dn = [array.T for array in (down_proj, down_mean, down_var)]
    gu_mean, gu_var, gu_update, dn_mean, dn_var, dn_update, ffn_row = step_call(
        ffn_step_kernel,
        [ffn_grads, *gu, *dn],
        (gate_up, dn[0]),
        deps=in_blocks[0],
    )
    out_blocks, out_first = tie(out_blocks, in_blocks[0])
    out_part = add_up(out_blocks).astype(LOW).reshape(-1, n_heads // 2, head_cols)
    out_own, out_arrived = fold_masks({mask: out_part[:, mask // 2] for mask in masks[::2]}, far_bits)
    out_mean, out_var, out_update, out_row = step_call(
        out_step_kernel,
        [out_own, out_arrived, heads_out, heads_out_mean, heads_out_var],
        (heads_out,),
        deps=ffn_row,
    )
    first_grad = first_grad.T[None]
    block_out = (hidden + (ffn_own.astype(F32) + ffn_arrived.astype(F32))).astype(LOW)[None]
    in_blocks, out_row, first_grad, block_out = tie(
        [out_first, *in_blocks[1:]], out_row, first_grad, block_out
    )
    in_mean, in_var, in_update, in_row = step_call(
        functools.partial(in_step_kernel, n_seq, groups),
        [*in_blocks, heads_in, heads_in_mean, heads_in_var],
        (heads_in,),
    )
    input_grad, gain_grad_one = input_gradient(
        one_own, one_arrived, tokens_in[0], norm_gains, grad_hidden
    )
    packed = jnp.concatenate(
        [gain_grad_one, gain_grad_two, ffn_row + out_row + (in_row + value_row)], axis=0
    )
    for axis in ("heads", "seq", "hid"):
        packed = total(packed, axis)
    gains_new, gmean_new, gvar_new, in_new, out_new, gu_new, dn_new = last_step(
        packed,
        (norm_gains, gain_mean, gain_var),
        (heads_in, heads_out, gate_up, dn[0]),
        (in_update, out_update, gu_update, dn_update),
    )
    dn_new, dn_mean, dn_var = (array.T for array in (dn_new, dn_mean, dn_var))
    entries = float(
        length * head_cols * lax.axis_size("seq") * lax.axis_size("heads") * lax.axis_size("hid")
    )
    norms = jnp.sqrt(packed[2, : 2 * MATRICES])
    value_norms = jnp.sqrt(packed[2, 2 * MATRICES : 2 * MATRICES + 2] / entries)
    return (
        block_out,
        input_grad[None],
        first_grad,
        gains_new,
        gmean_new,
        gvar_new,
        in_new,
        in_mean,
        in_var,
        out_new,
        out_mean,
        out_var,
        gu_new,
        gu_mean,
        gu_var,
        dn_new,
        dn_mean,
        dn_var,
        norms,
        value_norms,
    )


def solution(mesh):
    placed = (
        P(("seq", "hid"), "heads", None),
        P(("seq", "hid"), None, "heads"),
        P(("seq", "hid"), "heads", None),
        P(("seq", "hid"), None),
        P(("seq", "hid"), None),
        P(("seq", "hid"), None),
        P(),
        P(),
        P(),
        P(None, ("seq", "hid"), "heads"),
        P(None, ("seq", "hid"), "heads"),
        P(None, ("seq", "hid"), "heads"),
        P("heads", ("seq", "hid")),
        P("heads", ("seq", "hid")),
        P("heads", ("seq", "hid")),
        P(None, ("seq", "heads"), "hid"),
        P(None, ("seq", "heads"), "hid"),
        P(None, ("seq", "heads"), "hid"),
        P("hid", ("seq", "heads")),
        P("hid", ("seq", "heads")),
        P("hid", ("seq", "heads")),
    )
    return jax.shard_map(
        per_device,
        mesh=mesh,
        in_specs=placed,
        out_specs=(
            P(("seq", "hid"), "heads", None),
            P(("seq", "hid"), "heads", None),
            P(("seq", "hid"), None, "heads"),
            P(),
            P(),
            P(),
            P(None, ("seq", "hid"), "heads"),
            P(None, ("seq", "hid"), "heads"),
            P(None, ("seq", "hid"), "heads"),
            P("heads", ("seq", "hid")),
            P("heads", ("seq", "hid")),
            P("heads", ("seq", "hid")),
            P(None, ("seq", "heads"), "hid"),
            P(None, ("seq", "heads"), "hid"),
            P(None, ("seq", "heads"), "hid"),
            P("hid", ("seq", "heads")),
            P("hid", ("seq", "heads")),
            P("hid", ("seq", "heads")),
            P(),
            P(),
        ),
        check_vma=False,
    )
```
